128 devices in a mesh: dp: 4 (over y_hi, core), sp: 32 (over z, x, y_lo).
Axes of the slice: x: 4, y: 4 (y_hi: 2, y_lo: 2; y = y_hi * 2 + y_lo), z: 4, core: 2. Of those that a mesh axis runs over, the one named last changes fastest.
Arguments:
- x_long: bfloat16 [16384, 1024], P(('dp', 'sp')), may hold values from -24 to 24
- x_short: bfloat16 [131072, 1024], P(('dp', 'sp')), may hold values from -24 to 24
- long_blocks: int32 [4], replicated, may hold values from 4 to 8, as said below
- short_user: int32 [128, 2], P(('dp', 'sp')), may hold values from 0 to 1, as said below
- proj_in: bfloat16 [1024, 1536], replicated, may hold values from -0.1875 to 0.1875
- proj_out: bfloat16 [512, 1024], replicated, may hold values from -0.25 to 0.25
- cot_long: bfloat16 [16384, 1024], P(('dp', 'sp')), may hold values from -24 to 24
- cot_short: bfloat16 [131072, 1024], P(('dp', 'sp')), may hold values from -24 to 24
Outputs:
- out_long: bfloat16 [16384, 1024], P(('dp', 'sp'))
- out_short: bfloat16 [131072, 1024], P(('dp', 'sp'))
- back_long: bfloat16 [16384, 1024], P(('dp', 'sp'))
- back_short: bfloat16 [131072, 1024], P(('dp', 'sp'))
- grad_in: float32 [1024, 1536], P(('dp', 'sp'))
- grad_out_t: float32 [1024, 512], P(('dp', 'sp'))
The draws below stay inside these ranges and needn't reach their ends.
Inputs may be any that keep to these rules, and one draw needn't show every extreme that they name: Rows past long_blocks[g] * 512 of a long history are padding; some group's history fills all its blocks. `short_user`: along a device's blocks the user numbers start at 0 and never fall; each user covers one or two whole blocks, and the blocks of one user lie in one aligned pair (blocks 2p and 2p + 1); on some device every user covers one block, and on some device a user covers two.
All inputs are finite; a program needn't handle non-finite values.
Results may differ from the reference program's by a relative error of at most 0.013.
Values may be sent and summed in bfloat16 or wider, within the bound.
No kernel may reach another device: no remote copies, remote signals or barrier semaphores. Data moves between devices by JAX's collectives and lax.ppermute only.
A program may use at most 192 MiB of HBM per device.

```python
import jax
import jax.numpy as jnp
from jax import lax

D = 1024
H = 4
BLOCK = 512
SHORT_DEV = 1024
HV = 512
PROJ = 1536
LONG_LEN = 4096
LONG_BLOCKS = 8
SBLK = 2
ROWS_ALL = 147456
N_DP = 4
N_SP = 32
DEVICES = 128


def draw_long_blocks(key, part):
    key = jax.random.fold_in(key, 11)
    first_key, second_key = jax.random.split(key)
    counts = jax.random.randint(first_key, (N_DP,), LONG_BLOCKS // 2, LONG_BLOCKS + 1)
    full_group = jax.random.randint(second_key, (), 0, N_DP)
    return counts.at[full_group].set(LONG_BLOCKS).astype(jnp.int32)


def draw_short_user(key, part):
    key = jax.random.fold_in(key, 23)
    split_key, single_key, joined_key = jax.random.split(key, 3)
    pair_count = SBLK // 2
    splits = jax.random.randint(split_key, (DEVICES, pair_count), 0, 2).astype(jnp.int32)
    single_dev = jax.random.randint(single_key, (), 0, DEVICES).astype(jnp.int32)
    joined_dev = ((single_dev + 1 + jax.random.randint(joined_key, (), 0, DEVICES - 1)) % DEVICES).astype(jnp.int32)
    dev_rows = jnp.arange(DEVICES, dtype=jnp.int32)[:, None]
    pair_cols = jnp.arange(pair_count, dtype=jnp.int32)[None, :]
    splits = jnp.where(dev_rows == single_dev, 1, splits)
    splits = jnp.where((dev_rows == joined_dev) & (pair_cols == 0), 0, splits)
    base_ids = jnp.cumsum(splits, axis=1) - splits + pair_cols
    user_ids = jnp.stack([base_ids, base_ids + splits], axis=2)
    return user_ids.reshape(DEVICES, SBLK).astype(jnp.int32)


def raised(entries, stream_key, source, target, shards_of, factor):
    owner, partner = [(jnp.arange(entries.shape[dim]) // (entries.shape[dim] // shards_of)).reshape([-1 if axis == dim else 1 for axis in range(entries.ndim)]) for dim in (source, target)]
    chosen = jax.random.permutation(stream_key, shards_of)[partner]
    strong = (owner == chosen) | (owner == (partner + shards_of // 2) % shards_of)
    return jnp.where(strong, factor * entries, entries)


def level_of(stream_key, shape, cuts, least, high):
    gain, own = 1.0, jax.random.fold_in(stream_key, 6)
    for position, parts in cuts:
        steps = jnp.exp(jax.random.uniform(jax.random.fold_in(own, position), (parts,), jnp.float32, least / len(cuts), high / len(cuts)))
        gain = gain * jnp.repeat(steps, shape[position] // parts).reshape([-1 if axis == position else 1 for axis in range(len(shape))])
    return gain


def centred(stream_key, dims, spread, reach, cuts=(), held_as=jnp.bfloat16):
    gain = level_of(stream_key, dims, cuts, -0.22, 0.18) if cuts else 1.0
    entries = jax.random.normal(stream_key, dims, jnp.float32) * spread * gain
    return jnp.minimum(jnp.maximum(entries, -reach), reach).astype(held_as)


def heavy_noise(own_key, shape, deviation, bound, cuts, heavy, kind=jnp.bfloat16):
    result = deviation * jax.random.normal(own_key, shape, jnp.float32)
    if cuts:
        result = result * level_of(own_key, shape, cuts, -0.22, 0.18)
    return jnp.clip(raised(result, jax.random.fold_in(own_key, 3), *heavy), -bound, bound).astype(kind)


def setup_inputs(seed: int = 0) -> dict:
    streams_of = jax.random.split(jax.random.key(seed), 9)
    return {
        "x_long": heavy_noise(streams_of[0], (N_DP * LONG_LEN, D), 1.0, 24.0, ((0, 128),), (0, 1, 128, 5.5)),
        "x_short": heavy_noise(streams_of[1], (DEVICES * SHORT_DEV, D), 1.0, 24.0, ((0, 128),), (0, 1, 128, 5.5)),
        "long_blocks": draw_long_blocks(jax.random.fold_in(streams_of[8], 71), 0),
        "short_user": draw_short_user(jax.random.fold_in(streams_of[8], 71), 0),
        "proj_in": centred(streams_of[4], (D, PROJ), D ** -0.5, 0.1875),
        "proj_out": centred(streams_of[5], (HV, D), HV ** -0.5, 0.25),
        "cot_long": heavy_noise(streams_of[6], (N_DP * LONG_LEN, D), 1.0, 24.0, ((0, 128),), (0, 1, 128, 5.5)),
        "cot_short": heavy_noise(streams_of[7], (DEVICES * SHORT_DEV, D), 1.0, 24.0, ((0, 128),), (0, 1, 128, 5.5)),
    }


EPS = 1e-05

def silu_slope(inputs):
    sigma = jax.nn.sigmoid(inputs)
    return sigma * (1.0 + inputs * (1.0 - sigma))

def norm_rows(inputs):
    center = inputs - lax.optimization_barrier(jnp.mean(inputs, axis=-1, keepdims=True))
    inv_root = lax.rsqrt(lax.optimization_barrier(jnp.mean(center * center, axis=-1, keepdims=True)) + EPS)
    return (center * inv_root, inv_root)

def norm_back(upstream, normed, inv_root):
    return inv_root * (upstream - lax.optimization_barrier(jnp.mean(upstream, axis=-1, keepdims=True)) - normed * lax.optimization_barrier(jnp.mean(upstream * normed, axis=-1, keepdims=True)))

def contract(first_op, second_op, contract_dims):
    return lax.dot_general(first_op, second_op, (contract_dims, ((), ())), preferred_element_type=jnp.float32)

def attend(queries, keys_vals, coeffs):
    key_width = queries.shape[1] // H
    val_width = (keys_vals.shape[1] - queries.shape[1]) // H
    keys_end = queries.shape[1]
    pieces = []
    for which_head in range(H):
        head_q = queries[:, which_head * key_width:(which_head + 1) * key_width]
        head_k = keys_vals[:, which_head * key_width:(which_head + 1) * key_width]
        head_v = keys_vals[:, keys_end + which_head * val_width:keys_end + (which_head + 1) * val_width]
        scores = contract(head_q, head_k, ((1,), (1,))) * key_width ** (-0.5)
        weights = (jax.nn.silu(scores) * coeffs).astype(jnp.bfloat16)
        pieces.append(contract(weights, head_v, ((1,), (0,))))
    return jnp.concatenate(pieces, axis=1)

def attend_back(queries, keys_vals, grad_mixed, coeffs, want_query, want_keys):
    key_width = queries.shape[1] // H
    val_width = (keys_vals.shape[1] - queries.shape[1]) // H
    keys_end = queries.shape[1]
    root_scale = key_width ** (-0.5)
    query_parts = []
    key_parts = []
    value_parts = []
    for which_head in range(H):
        head_q = queries[:, which_head * key_width:(which_head + 1) * key_width]
        head_k = keys_vals[:, which_head * key_width:(which_head + 1) * key_width]
        head_v = keys_vals[:, keys_end + which_head * val_width:keys_end + (which_head + 1) * val_width]
        head_g = grad_mixed[:, which_head * val_width:(which_head + 1) * val_width]
        scores = contract(head_q, head_k, ((1,), (1,))) * root_scale
        grad_w = contract(head_g, head_v, ((1,), (1,)))
        slopes = (grad_w * coeffs * silu_slope(scores)).astype(jnp.bfloat16)
        if want_query:
            query_parts.append(contract(slopes, head_k, ((1,), (0,))) * root_scale)
        if want_keys:
            weights = (jax.nn.silu(scores) * coeffs).astype(jnp.bfloat16)
            key_parts.append(contract(slopes, head_q, ((0,), (0,))) * root_scale)
            value_parts.append(contract(weights, head_g, ((0,), (0,))))
    grad_q = jnp.concatenate(query_parts, axis=1) if want_query else None
    grad_kv = jnp.concatenate(key_parts + value_parts, axis=1) if want_keys else None
    return (grad_q, grad_kv)

def head_out(x_rows, cotangent, proj_out, gate_u, mixed_out):
    mixed_n, inv_mix = norm_rows(mixed_out)
    gate_f = gate_u.astype(jnp.float32)
    gated_bf = (mixed_n * gate_f).astype(jnp.bfloat16)
    output = (x_rows.astype(jnp.float32) + contract(gated_bf, proj_out, ((1,), (0,)))).astype(jnp.bfloat16)
    grad_g = contract(cotangent, proj_out, ((1,), (1,)))
    grad_mixed = norm_back(grad_g * gate_f, mixed_n, inv_mix).astype(jnp.bfloat16)
    return (output, gated_bf, grad_g * mixed_n, grad_mixed)

def input_back(cotangent, proj_in, normed, inv_std, pre_act, grad_act):
    grad_pre = (grad_act * silu_slope(pre_act)).astype(jnp.bfloat16)
    grad_norm = contract(grad_pre, proj_in, ((1,), (1,)))
    back_rows = (cotangent.astype(jnp.float32) + norm_back(grad_norm, normed, inv_std)).astype(jnp.bfloat16)
    return (grad_pre, back_rows)

def long_coeffs(query_pos, key_pos, valid_rows):
    inside = (key_pos[None, :] <= query_pos[:, None]) & (query_pos[:, None] < valid_rows)
    return inside.astype(jnp.float32) / valid_rows.astype(jnp.float32)

def short_coeffs(user_ids):
    block_count = lax.optimization_barrier(jnp.sum((user_ids[:, None] == user_ids[None, :]).astype(jnp.int32), axis=1))
    row_user = jnp.repeat(user_ids, BLOCK)
    row_len = jnp.repeat(block_count * BLOCK, BLOCK)
    row_ids = jnp.arange(row_user.shape[0], dtype=jnp.int32)
    inside = (row_user[:, None] == row_user[None, :]) & (row_ids[None, :] <= row_ids[:, None])
    return inside.astype(jnp.float32) / row_len[:, None].astype(jnp.float32)

def full_layer(x_rows, cotangent, proj_in, proj_out, coeffs):
    value_cols = proj_out.shape[0]
    query_cols = (proj_in.shape[1] - 2 * value_cols) // 2
    normed, inv_std = norm_rows(x_rows.astype(jnp.float32))
    x_bf = normed.astype(jnp.bfloat16)
    pre_act = contract(x_bf, proj_in, ((1,), (0,)))
    activated = jax.nn.silu(pre_act).astype(jnp.bfloat16)
    gate_u = activated[:, :value_cols]
    queries = activated[:, value_cols:value_cols + query_cols]
    keys_vals = activated[:, value_cols + query_cols:]
    mixed_out = attend(queries, keys_vals, coeffs)
    output, gated_bf, grad_gate, grad_mixed = head_out(x_rows, cotangent, proj_out, gate_u, mixed_out)
    grad_q, grad_kv = attend_back(queries, keys_vals, grad_mixed, coeffs, True, True)
    grad_pre, back_rows = input_back(cotangent, proj_in, normed, inv_std, pre_act, jnp.concatenate([grad_gate, grad_q, grad_kv], axis=1))
    return (output, back_rows, x_bf, grad_pre, gated_bf)

def reference(x_long, x_short, long_blocks, short_user, proj_in, proj_out, cot_long, cot_short):

    def long_step(totals, scan_items):
        x_rows, cotangent, blocks = scan_items
        positions = jnp.arange(LONG_LEN, dtype=jnp.int32)
        coeffs = long_coeffs(positions, positions, blocks * BLOCK)
        output, back_rows, x_bf, grad_pre, gated_bf = full_layer(x_rows, cotangent, proj_in, proj_out, coeffs)
        new_totals = (totals[0] + contract(x_bf, grad_pre, ((0,), (0,))), totals[1] + contract(cotangent, gated_bf, ((0,), (0,))))
        return (new_totals, (output, back_rows))

    def short_step(totals, scan_items):
        x_rows, cotangent, user_ids = scan_items
        output, back_rows, x_bf, grad_pre, gated_bf = full_layer(x_rows, cotangent, proj_in, proj_out, short_coeffs(user_ids))
        new_totals = (totals[0] + contract(x_bf, grad_pre, ((0,), (0,))), totals[1] + contract(cotangent, gated_bf, ((0,), (0,))))
        return (new_totals, (output, back_rows))
    start_sums = (jnp.zeros((D, PROJ), jnp.float32), jnp.zeros((D, HV), jnp.float32))
    totals, (out_l, back_l) = lax.scan(long_step, start_sums, (x_long.reshape(N_DP, LONG_LEN, D), cot_long.reshape(N_DP, LONG_LEN, D), long_blocks))
    totals, (out_s, back_s) = lax.scan(short_step, totals, (x_short.reshape(N_DP * N_SP, SHORT_DEV, D), cot_short.reshape(N_DP * N_SP, SHORT_DEV, D), short_user))
    factor = float(ROWS_ALL) ** (-0.5)
    return (out_l.reshape(N_DP * LONG_LEN, D), out_s.reshape(N_DP * N_SP * SHORT_DEV, D), back_l.reshape(N_DP * LONG_LEN, D), back_s.reshape(N_DP * N_SP * SHORT_DEV, D), totals[0] * factor, totals[1] * factor)
```

```python
import functools

import jax
import jax.numpy as jnp
from jax import lax
from jax.experimental import pallas as pl
from jax.experimental.pallas import tpu as pltpu
from jax.sharding import PartitionSpec as P

H = 4
BLOCK = 512
KW = 64
VW = 128
HW = 2 * KW + VW
EPS = 1e-05
HALF_SCALE = 0.5 * KW**-0.5
F32 = jnp.float32
BF16 = jnp.bfloat16
MIB = 1024 * 1024


def dot(first, second, first_dim, second_dim):
    return lax.dot_general(
        first, second, (((first_dim,), (second_dim,)), ((), ())), preferred_element_type=F32
    )


def norm_rows(rows):
    center = rows - jnp.mean(rows, axis=-1, keepdims=True)
    inv_root = lax.rsqrt(jnp.mean(center * center, axis=-1, keepdims=True) + EPS)
    return center * inv_root, inv_root


def norm_back(upstream, normed, inv_root):
    return inv_root * (
        upstream
        - jnp.mean(upstream, axis=-1, keepdims=True)
        - normed * jnp.mean(upstream * normed, axis=-1, keepdims=True)
    )


def silu_half(half):
    return half * (1.0 + jnp.tanh(half))


def silu_both(half):
    curve = jnp.tanh(half)
    above = 1.0 + curve
    act = half * above
    return act, above + act * (1.0 - curve)


def low_lanes(shape):
    return lax.broadcasted_iota(jnp.int32, shape, 1) < KW


def turned(pair):
    return pltpu.roll(pair.astype(F32), KW, 1)


def score_side(qk):
    return jnp.where(low_lanes(qk.shape), 0.0, turned(qk) * HALF_SCALE).astype(BF16)


def causal(keys_first, keys, queries, key_start=0, query_start=0):
    shape = (keys, queries) if keys_first else (queries, keys)
    key_pos = key_start + lax.broadcasted_iota(jnp.int32, shape, 0 if keys_first else 1)
    query_pos = query_start + lax.broadcasted_iota(jnp.int32, shape, 1 if keys_first else 0)
    return key_pos <= query_pos


def project(x_bf, proj):
    act, slope = silu_both(0.5 * dot(x_bf, proj, 1, 0))
    return act.astype(BF16), 0.5 * slope


def head_out(x_rows, cot, proj_out, gate_u, slope_gate, mixed):
    mixed_n, inv_mix = norm_rows(mixed)
    gate_f = gate_u.astype(F32)
    gated = (mixed_n * gate_f).astype(BF16)
    out = (x_rows.astype(F32) + dot(gated, proj_out, 1, 0)).astype(BF16)
    grad_g = dot(cot, proj_out, 1, 1)
    grad_mixed = norm_back(grad_g * gate_f, mixed_n, inv_mix)
    grad_gate = (grad_g * mixed_n * slope_gate).astype(BF16)
    return out, gated, grad_gate, grad_mixed


def run_place():
    index = lax.axis_index("sp")
    return lax.rem(index, H), lax.div(index, H), lax.axis_index("dp")


def split_rows(part, start):
    for block in range(2):
        yield block, pl.ds(pl.multiple_of(start + 2 * part * block, part), part)


def long_project_kernel(
    x_ref,
    cot_ref,
    pin_gate_ref,
    pin_q_ref,
    pin_k_ref,
    pin_v_ref,
    proj_ref,
    send_ref,
    inv_ref,
    gate_ref,
    slope_ref,
    half_ref,
    *refs,
):
    pack_refs, (xbf_ref, rest_ref) = refs[:H], refs[H:]
    step = pl.program_id(0)
    width = x_ref.shape[1]

    @pl.when(step == 0)
    def _():
        normed, inv_std = norm_rows(x_ref[...].astype(F32))
        xbf_ref[...] = normed.astype(BF16)
        inv_ref[...] = inv_std

    x_bf = xbf_ref[...]
    act, slope = project(x_bf, pin_gate_ref[...])
    gate_ref[...] = act
    slope_ref[...] = slope.astype(BF16)
    q_pair, k_pair = pin_q_ref[...], pin_k_ref[...]
    low = low_lanes(q_pair.shape)
    even = jnp.where(low, q_pair.astype(F32), turned(k_pair)).astype(BF16)
    odd = jnp.where(low, turned(q_pair), k_pair.astype(F32)).astype(BF16)
    proj = jnp.concatenate([even, pin_v_ref[:, :VW], odd, pin_v_ref[:, VW:]], axis=1)
    proj_ref[...] = proj
    act, slope = project(x_bf, proj)
    rest_ref[step] = slope.astype(BF16)
    for copy in range(send_ref.shape[0]):
        for which in range(2):
            send_ref[copy, which] = act[:, HW * which : HW * (which + 1)]

    @pl.when(step == 1)
    def _():
        mine, _, group = run_place()
        part = width // 4
        for block, features in split_rows(part, (1 - lax.rem(group, 2)) * part):
            half_ref[:, block * part : (block + 1) * part] = cot_ref[:, features]
            half_ref[:, (block + 2) * part : (block + 3) * part] = xbf_ref[:, features]
        for bits in range(H):
            head = mine ^ bits
            start = pl.multiple_of(lax.rem(head, 2) * HW, HW)
            pack_refs[bits][:, :width] = xbf_ref[...]
            pack_refs[bits][:, width:] = rest_ref[lax.div(head, 2), :, pl.ds(start, HW)]


def short_forward_kernel(
    user_ref,
    x_ref,
    cot_ref,
    pin_ref,
    proj_ref,
    pout_ref,
    out_ref,
    qkv_ref,
    g_ref,
    grad_gate_ref,
    slope_ref,
    xbf_ref,
    inv_ref,
    mine_ref,
    other_ref,
    sum_ref,
    seen_ref,
    mixed_ref,
    side_ref,
):
    step = pl.program_id(0)
    joined = user_ref[0, 0] == user_ref[0, 1]
    share = jnp.where(joined, 0.5 / BLOCK, 1.0 / BLOCK)
    normed, inv_std = norm_rows(x_ref[...].astype(F32))
    x_bf = normed.astype(BF16)
    xbf_ref[...] = x_bf
    inv_ref[...] = inv_std
    act, slope = project(x_bf, proj_ref[...])
    slope_ref[...] = slope.astype(BF16)
    qkv_ref[...] = act
    gate_u, slope_gate = project(x_bf, pin_ref[...])
    half = BLOCK // 2
    for which in range(H):
        qk = act[:, HW * which : HW * which + 2 * KW]
        values = act[:, HW * which + 2 * KW : HW * (which + 1)]
        side = score_side(qk)
        scores = dot(side, qk[:half], 1, 1)
        weights = jnp.where(causal(False, half, BLOCK), silu_half(scores), 0.0).astype(BF16)
        mixed = dot(weights, values[:half], 1, 0)
        scores = dot(side[half:], qk[half:], 1, 1)
        weights = jnp.where(causal(False, half, half), silu_half(scores), 0.0).astype(BF16)
        lower = mixed[half:] + dot(weights, values[half:], 1, 0)
        mixed_ref[:half, VW * which : VW * (which + 1)] = mixed[:half]
        mixed_ref[half:, VW * which : VW * (which + 1)] = lower

        side_ref[:, 2 * KW * which : 2 * KW * (which + 1)] = side

    @pl.when(jnp.logical_and(step == 1, joined))
    def _():
        for which in range(H):
            first = HW * which
            side = side_ref[:, 2 * KW * which : 2 * KW * (which + 1)]
            scores = dot(side, seen_ref[:, first : first + 2 * KW], 1, 1)
            mixed_ref[:, VW * which : VW * (which + 1)] += dot(
                silu_half(scores).astype(BF16), seen_ref[:, first + 2 * KW : first + HW], 1, 0
            )

    @pl.when(step == 0)
    def _():
        seen_ref[...] = act

    out, gated, grad_gate, grad_mixed = head_out(
        x_ref[...],
        cot_ref[...],
        pout_ref[...],
        gate_u,
        slope_gate,
        mixed_ref[...] * share,
    )
    out_ref[...] = out
    grad_gate_ref[...] = grad_gate
    g_ref[...] = (grad_mixed.astype(BF16).astype(F32) * share).astype(BF16)
    gates = gated.shape[1]

    @pl.when(step == 0)
    def _():
        sum_ref[:, :gates] = dot(cot_ref[...], gated, 0, 0)
        sum_ref[:, gates:] = dot(xbf_ref[...], grad_gate_ref[...], 0, 0)

    @pl.when(step == 1)
    def _():
        part = mine_ref.shape[0] // 2
        core = lax.rem(lax.axis_index("dp"), 2)
        for target, side in ((mine_ref, core), (other_ref, 1 - core)):
            for block, features in split_rows(part, side * part):
                here = slice(block * part, (block + 1) * part)
                total = sum_ref[features, :gates] + dot(cot_ref[:, features], gated, 0, 0)
                target[here, :gates] = total.astype(BF16)
                total = dot(xbf_ref[:, features], grad_gate_ref[...], 0, 0)
                target[here, gates:] = (sum_ref[features, gates:] + total).astype(BF16)


def back_block(query_side, query_qk, key_qk, values, g_rows, mask):
    act, slope = silu_both(dot(key_qk, query_side, 1, 1))
    slopes = dot(values, g_rows, 1, 1) * slope
    if mask is not None:
        act = jnp.where(mask, act, 0.0)
        slopes = jnp.where(mask, slopes, 0.0)
    slopes = slopes.astype(BF16)
    grad_q = dot(slopes, key_qk, 0, 0)
    grad_k = dot(slopes, query_qk, 1, 0)
    grad_v = dot(act.astype(BF16), g_rows, 1, 0)
    return grad_q, grad_k, grad_v


def short_back_kernel(
    user_ref, qkv_ref, g_ref, slope_ref, xbf_ref, grad_ref, mine_ref, other_ref, acc_ref, side_ref
):
    joined = user_ref[0, 0] == user_ref[0, 1]
    half = BLOCK // 2
    heads = range(qkv_ref.shape[1] // HW)
    for which in heads:
        first = HW * which
        qk = qkv_ref[:, first : first + 2 * KW]
        side = score_side(qk)
        values = qkv_ref[:, first + 2 * KW : first + HW]
        g_rows = g_ref[:, VW * which : VW * (which + 1)]
        lanes = low_lanes((half, 2 * KW))
        for block in range(qkv_ref.shape[0] // BLOCK):
            top = slice(block * BLOCK, block * BLOCK + half)
            end = slice(block * BLOCK + half, (block + 1) * BLOCK)
            both = slice(block * BLOCK, (block + 1) * BLOCK)
            dq_one, dk_one, dv_one = back_block(
                side[both], qk[both], qk[top], values[top], g_rows[both], causal(True, half, BLOCK)
            )
            dq_two, dk_two, dv_two = back_block(
                side[end], qk[end], qk[end], values[end], g_rows[end], causal(True, half, half)
            )
            acc_ref[top, first : first + 2 * KW] = jnp.where(lanes, dk_one, dq_one[:half])
            acc_ref[end, first : first + 2 * KW] = jnp.where(lanes, dk_two, dq_one[half:] + dq_two)
            acc_ref[top, first + 2 * KW : first + HW] = dv_one
            acc_ref[end, first + 2 * KW : first + HW] = dv_two
        side_ref[:, 2 * KW * which : 2 * KW * (which + 1)] = side[BLOCK:]

    @pl.when(joined)
    def _():
        one, two = slice(0, BLOCK), slice(BLOCK, 2 * BLOCK)
        for which in heads:
            first = HW * which
            pair = slice(first, first + 2 * KW)
            grad_q, grad_k, grad_v = back_block(
                side_ref[:, 2 * KW * which : 2 * KW * (which + 1)],
                qkv_ref[two, pair],
                qkv_ref[one, pair],
                qkv_ref[one, first + 2 * KW : first + HW],
                g_ref[two, VW * which : VW * (which + 1)],
                None,
            )
            lanes = low_lanes((BLOCK, 2 * KW))
            acc_ref[one, pair] += jnp.where(lanes, grad_k, 0.0)
            acc_ref[two, pair] += jnp.where(lanes, 0.0, grad_q)
            acc_ref[one, first + 2 * KW : first + HW] += grad_v

    for which in heads:
        first = HW * which
        pair, rest = slice(first, first + 2 * KW), slice(first + 2 * KW, first + HW)
        grads = turned(acc_ref[:, pair]) * HALF_SCALE
        grad_ref[:, pair] = (grads * slope_ref[:, pair].astype(F32)).astype(BF16)
        grad_ref[:, rest] = (acc_ref[:, rest] * slope_ref[:, rest].astype(F32)).astype(BF16)
    grad_pre = grad_ref[...]
    part = mine_ref.shape[0] // 2
    core = lax.rem(lax.axis_index("dp"), 2)
    for target, side in ((mine_ref, core), (other_ref, 1 - core)):
        for block, features in split_rows(part, side * part):
            total = dot(xbf_ref[:, features], grad_pre, 0, 0)
            target[block * part : (block + 1) * part] = total.astype(BF16)


def rows_at(index):
    return pl.ds(pl.multiple_of(index * BLOCK, BLOCK), BLOCK)


def long_attend_kernel(blocks_smem, all_ref, *refs):
    mixed_refs, acc_ref = refs[:H], refs[H]
    mine, chunk, group = run_place()
    valid = blocks_smem[group]
    acc_ref[...] = jnp.zeros_like(acc_ref)

    @pl.when(chunk < valid)
    def _():
        side = score_side(all_ref[rows_at(chunk), : 2 * KW])

        @pl.loop(0, chunk)
        def _(index):
            scores = dot(side, all_ref[rows_at(index), : 2 * KW], 1, 1)
            acc_ref[...] += dot(
                silu_half(scores).astype(BF16), all_ref[rows_at(index), 2 * KW :], 1, 0
            )

        weights = silu_half(dot(side, all_ref[rows_at(chunk), : 2 * KW], 1, 1))
        weights = jnp.where(causal(False, BLOCK, BLOCK), weights, 0.0).astype(BF16)
        acc_ref[...] += dot(weights, all_ref[rows_at(chunk), 2 * KW :], 1, 0)

    coeff = 1.0 / (valid * BLOCK).astype(F32)
    rows = mixed_refs[0].shape[0]
    for bits in range(H):
        start = pl.multiple_of((mine ^ bits) * rows, rows)
        mixed_refs[bits][...] = (acc_ref[pl.ds(start, rows), :] * coeff).astype(BF16)


def long_back_kernel(blocks_smem, all_ref, g_ref, *refs):
    pack_refs, sum_refs, grad_refs = refs[:H], refs[H : H + 2], refs[H + 2 : 2 * H + 2]
    dq_ref, dk_ref, dv_ref, x_ref, pre_ref = refs[2 * H + 2 :]
    mine, chunk, group = run_place()
    valid = blocks_smem[group]
    dq_ref[...] = jnp.zeros_like(dq_ref)
    dk_ref[...] = jnp.zeros_like(dk_ref)
    dv_ref[...] = jnp.zeros_like(dv_ref)

    @pl.when(chunk < valid)
    def _():
        own = rows_at(chunk)
        qk = all_ref[own, : 2 * KW]
        side = score_side(qk)
        values = all_ref[own, 2 * KW :]
        g_own = g_ref[own, :]
        grad_q, grad_k, grad_v = back_block(
            side, qk, qk, values, g_own, causal(True, BLOCK, BLOCK)
        )
        dq_ref[...] = grad_q
        dk_ref[...] = grad_k
        dv_ref[...] = grad_v

        @pl.loop(0, chunk)
        def _(index):
            keys = all_ref[rows_at(index), : 2 * KW]
            act, slope = silu_both(dot(side, keys, 1, 1))
            slopes = dot(g_own, all_ref[rows_at(index), 2 * KW :], 1, 1) * slope
            dq_ref[...] += dot(slopes.astype(BF16), keys, 1, 0)

        @pl.loop(chunk + 1, valid)
        def _(index):
            g_rows = g_ref[rows_at(index), :]
            queries = all_ref[rows_at(index), : 2 * KW]
            act, slope = silu_both(dot(qk, score_side(queries), 1, 1))
            slopes = (dot(values, g_rows, 1, 1) * slope).astype(BF16)
            dk_ref[...] += dot(slopes, queries, 1, 0)
            dv_ref[...] += dot(act.astype(BF16), g_rows, 1, 0)

    coeff = 1.0 / (valid * BLOCK).astype(F32)
    rows = grad_refs[0].shape[0]
    width = x_ref.shape[1]
    lanes = low_lanes((rows, 2 * KW))
    for bits in range(H):
        part = pl.ds(pl.multiple_of((mine ^ bits) * rows, rows), rows)
        pair = turned(jnp.where(lanes, dk_ref[part, :], dq_ref[part, :])) * HALF_SCALE
        slope = pack_refs[bits][:, width:].astype(F32)
        here = slice(bits * rows, (bits + 1) * rows)
        pre_ref[here, : 2 * KW] = (pair * coeff * slope[:, : 2 * KW]).astype(BF16)
        pre_ref[here, 2 * KW :] = (dv_ref[part, :] * coeff * slope[:, 2 * KW :]).astype(BF16)
        grad_refs[bits][...] = pre_ref[here, :]
        x_ref[here, :] = pack_refs[bits][:, :width]
    part = sum_refs[0].shape[0] // 2
    core = lax.rem(group, 2)
    for target, side in zip(sum_refs, (core, 1 - core)):
        for block, features in split_rows(part, side * part):
            total = dot(x_ref[:, features], pre_ref[...], 0, 0)
            target[block * part : (block + 1) * part] = total.astype(BF16)


def long_head_kernel(
    got_0,
    got_1,
    got_2,
    got_3,
    x_ref,
    cot_ref,
    pout_ref,
    gate_ref,
    slope_ref,
    out_ref,
    send_ref,
    mid_ref,
    mixed_ref,
):
    mine, _, _ = run_place()
    for bits, got in enumerate((got_0, got_1, got_2, got_3)):
        start = pl.multiple_of((mine ^ bits) * VW, VW)
        mixed_ref[:, pl.ds(start, VW)] = got[...].astype(F32)
    out, gated, grad_gate, grad_mixed = head_out(
        x_ref[...],
        cot_ref[...],
        pout_ref[...],
        gate_ref[...],
        slope_ref[...].astype(F32),
        mixed_ref[...],
    )
    out_ref[...] = out
    cols = gated.shape[1]
    mid_ref[:, :cols] = gated
    mid_ref[:, cols:] = grad_gate
    grad_mixed = grad_mixed.astype(BF16)
    for copy in range(send_ref.shape[0]):
        for which in range(H):
            send_ref[copy, which] = grad_mixed[:, VW * which : VW * (which + 1)]


def early_sums_kernel(
    pack_ref, cot_ref, mid_ref, half_ref, mid_got, mine_ref, got_ref, sum_ref
):
    cols = mid_ref.shape[1] // 2
    part = sum_ref.shape[0] // 2
    core = lax.rem(lax.axis_index("dp"), 2)
    mid = jnp.concatenate([mid_ref[...], mid_got[...]], axis=0)
    for block, features in split_rows(part, core * part):
        here = slice(block * part, (block + 1) * part)
        for place, own in ((0, cot_ref), (1, pack_ref)):
            start = (2 * place + block) * part
            rows = jnp.concatenate([own[:, features], half_ref[:, start : start + part]], axis=0)
            there = slice(place * cols, (place + 1) * cols)
            total = mine_ref[here, there].astype(F32) + got_ref[here, there].astype(F32)
            sum_ref[here, there] = (total + dot(rows, mid[:, there], 0, 0)).astype(BF16)


def late_pair_sum_kernel(short_mine, short_got, long_mine, long_got, sum_ref):
    mine, _, _ = run_place()
    total = short_mine[...].astype(F32) + short_got[...].astype(F32)
    sum_ref[...] = total.astype(BF16)
    head = pl.ds(pl.multiple_of(mine * HW, HW), HW)
    total = short_mine[:, head].astype(F32) + short_got[:, head].astype(F32)
    total += long_mine[...].astype(F32) + long_got[...].astype(F32)
    sum_ref[:, head] = total.astype(BF16)


def final_sums_kernel(factor, early_ref, late_ref, in_ref, out_ref):
    gates = out_ref.shape[1]
    out_ref[...] = early_ref[:, :gates] * factor
    in_ref[:, :gates] = early_ref[:, gates:] * factor
    late = late_ref[0].astype(F32)
    for step in range(1, late_ref.shape[0]):
        late += late_ref[step].astype(F32)
    late = late * factor
    low = low_lanes((late.shape[0], 2 * KW))
    for pair in range(H // 2):
        first = 2 * HW * pair
        even, odd = late[:, first : first + 2 * KW], late[:, first + HW : first + HW + 2 * KW]
        first_q = gates + 2 * KW * pair
        first_k = first_q + H * KW
        first_v = gates + 2 * H * KW + 2 * VW * pair
        in_ref[:, first_q : first_q + 2 * KW] = jnp.where(low, even, turned(odd))
        in_ref[:, first_k : first_k + 2 * KW] = jnp.where(low, turned(even), odd)
        in_ref[:, first_v : first_v + VW] = late[:, first + 2 * KW : first + HW]
        in_ref[:, first_v + VW : first_v + 2 * VW] = late[:, first + HW + 2 * KW : first + 2 * HW]


def input_back_kernel(
    grad_gate_ref,
    grad_ref,
    cot_ref,
    xbf_ref,
    inv_ref,
    pin_ref,
    proj_ref,
    got_0,
    got_1,
    got_2,
    got_3,
    long_gate_ref,
    long_cot_ref,
    pack_ref,
    long_inv_ref,
    back_ref,
    long_back_ref,
    long_grad_ref,
):
    step = pl.program_id(0)
    width = cot_ref.shape[1]

    def finish(gate, grad, cot, normed, inv, target):
        grad_norm = dot(gate[...], pin_ref[...], 1, 1) + dot(grad[...], proj_ref[...], 1, 1)
        back = norm_back(grad_norm, normed.astype(F32), inv[...])
        target[...] = (cot[...].astype(F32) + back).astype(BF16)

    @pl.when(step < 2)
    def _():
        finish(grad_gate_ref, grad_ref, cot_ref, xbf_ref[...], inv_ref, back_ref)

    @pl.when(step == 2)
    def _():
        mine, _, _ = run_place()
        for bits, got in enumerate((got_0, got_1, got_2, got_3)):
            start = pl.multiple_of((mine ^ bits) * HW, HW)
            long_grad_ref[:, pl.ds(start, HW)] = got[...]
        finish(
            long_gate_ref,
            long_grad_ref,
            long_cot_ref,
            pack_ref[:, :width],
            long_inv_ref,
            long_back_ref,
        )


def shaped(shape, dtype=BF16):
    return jax.ShapeDtypeStruct(shape, dtype)


def in_hbm(shape, dtype=BF16):
    return pltpu.HBM(shape, dtype)


def call(kernel, out_shape, flops, moved, name, vmem=24, **kwargs):
    return pl.pallas_call(
        kernel,
        out_shape=out_shape,
        cost_estimate=pl.CostEstimate(flops=flops, bytes_accessed=moved, transcendentals=0),
        compiler_params=pltpu.CompilerParams(vmem_limit_bytes=vmem * MIB),
        name=name,
        **kwargs,
    )


SMEM = pl.BlockSpec(memory_space=pltpu.SMEM)
WHOLE = pl.BlockSpec(memory_space=pltpu.VMEM)


def rows_spec(rows, cols):
    return pl.BlockSpec((rows, cols), lambda step: (step, 0))


def cols_spec(rows, cols):
    return pl.BlockSpec((rows, cols), lambda step: (0, step))


def fixed_spec(rows, cols):
    return pl.BlockSpec((rows, cols), lambda step: (0, 0))


def swap_heads(pieces):
    size = lax.axis_size("sp")
    return [pieces[0]] + [
        lax.ppermute(pieces[bits], "sp", [(src, src ^ bits) for src in range(size)])
        for bits in range(1, H)
    ]


def spread_heads(sent):
    chunks, heads, rows, cols = sent.shape
    got = lax.all_to_all(sent.reshape(chunks * heads, rows, cols), "sp", 0, 0, tiled=True)
    return got.reshape(chunks * heads * rows, cols)


def swap_cores(half):
    size = lax.axis_size("dp")
    return lax.ppermute(half, "dp", [(src, src ^ 1) for src in range(size)])


def scatter_pairs(partial):
    runs, size = lax.axis_size("dp"), lax.axis_size("sp")
    groups = [
        [run * size + place for run in range(core, runs, 2) for place in range(size)]
        for core in range(2)
    ]
    count = len(groups[0])
    sent = partial.reshape(count, partial.shape[0] // count, partial.shape[1])
    return lax.all_to_all(sent, ("dp", "sp"), 0, 0, tiled=True, axis_index_groups=groups)


def body(x_long, x_short, long_blocks, short_user, proj_in, proj_out, cot_long, cot_short):
    sp_size = lax.axis_size("sp")
    long_rows, width = x_long.shape
    short_rows = x_short.shape[0]
    gates = proj_out.shape[0]
    cols = proj_in.shape[1]
    rest = cols - gates
    half = width // 2
    chunks = sp_size // H

    proj, sent, inv_long, gate_long, slope_long, half_other, *packs = call(
        long_project_kernel,
        (
            in_hbm((width, rest)),
            in_hbm((chunks, H, long_rows, HW)),
            in_hbm((long_rows, 1), F32),
            in_hbm((long_rows, gates)),
            in_hbm((long_rows, gates)),
            in_hbm((long_rows, width)),
        )
        + (in_hbm((long_rows, width + HW)),) * H,
        2 * long_rows * width * cols,
        10 * 2**20,
        "long_project",
        vmem=60,
        grid=(2,),
        in_specs=[
            fixed_spec(long_rows, width),
            fixed_spec(long_rows, width),
            cols_spec(width, gates // 2),
            pl.BlockSpec((width, 2 * KW), lambda step: (0, step + gates // (2 * KW))),
            pl.BlockSpec((width, 2 * KW), lambda step: (0, step + (gates + H * KW) // (2 * KW))),
            pl.BlockSpec((width, 2 * VW), lambda step: (0, step + (gates + 2 * H * KW) // (2 * VW))),
        ],
        out_specs=[
            cols_spec(width, rest // 2),
            pl.BlockSpec((chunks, 2, long_rows, HW), lambda step: (0, step, 0, 0)),
            fixed_spec(long_rows, 1),
            cols_spec(long_rows, gates // 2),
            cols_spec(long_rows, gates // 2),
            fixed_spec(long_rows, width),
        ]
        + [fixed_spec(long_rows, width + HW)] * H,
        scratch_shapes=[
            pltpu.VMEM((long_rows, width), BF16),
            pltpu.VMEM((2, long_rows, rest // 2), BF16),
        ],
    )(x_long, cot_long, proj_in, proj_in, proj_in, proj_in)
    whole = spread_heads(sent)

    short_out = call(
        short_forward_kernel,
        (
            in_hbm((short_rows, width)),
            in_hbm((short_rows, rest)),
            in_hbm((short_rows, gates)),
            in_hbm((short_rows, gates)),
            in_hbm((short_rows, rest)),
            in_hbm((short_rows, width)),
            in_hbm((short_rows, 1), F32),
            in_hbm((half, 2 * gates)),
            in_hbm((half, 2 * gates)),
        ),
        20 * 10**9,
        24 * 2**20,
        "short_forward",
        vmem=56,
        grid=(short_rows // BLOCK,),
        in_specs=[
            SMEM,
            rows_spec(BLOCK, width),
            rows_spec(BLOCK, width),
            fixed_spec(width, gates),
            fixed_spec(width, rest),
            fixed_spec(gates, width),
        ],
        out_specs=[
            rows_spec(BLOCK, width),
            rows_spec(BLOCK, rest),
            rows_spec(BLOCK, gates),
            rows_spec(BLOCK, gates),
            rows_spec(BLOCK, rest),
            rows_spec(BLOCK, width),
            rows_spec(BLOCK, 1),
            fixed_spec(half, 2 * gates),
            fixed_spec(half, 2 * gates),
        ],
        scratch_shapes=[
            pltpu.VMEM((width, 2 * gates), F32),
            pltpu.VMEM((BLOCK, rest), BF16),
            pltpu.VMEM((BLOCK, gates), F32),
            pltpu.VMEM((BLOCK, 2 * KW * H), BF16),
        ],
    )(short_user, x_short, cot_short, proj_in, proj, proj_out)
    out_short, qkv_short, g_short, gate_short, slope_short, xbf_short, inv_short = short_out[:7]
    early_mine, early_other = short_out[7:]
    early_got = swap_cores(early_other)

    whole, early_got, out_short = lax.optimization_barrier((whole, early_got, out_short))
    mixed = call(
        long_attend_kernel,
        (shaped((long_rows, VW)),) * H,
        2 * 10**9,
        2 * 2**20,
        "long_attend",
        in_specs=[SMEM, WHOLE],
        scratch_shapes=[
            pltpu.VMEM((BLOCK, VW), F32),
        ],
    )(long_blocks, whole)
    out_long, sent, mid = call(
        long_head_kernel,
        (
            shaped((long_rows, width)),
            in_hbm((chunks, H, long_rows, VW)),
            in_hbm((long_rows, 2 * gates)),
        ),
        4 * long_rows * width * gates,
        3 * 2**20,
        "long_head",
        in_specs=[WHOLE] * 9,
        scratch_shapes=[pltpu.VMEM((long_rows, gates), F32)],
    )(*swap_heads(mixed), x_long, cot_long, proj_out, gate_long, slope_long)
    sent, qkv_short, mid, packs, half_other = lax.optimization_barrier(
        (sent, qkv_short, mid, packs, half_other)
    )
    all_g = spread_heads(sent)
    packs = swap_heads(packs)
    half_got = swap_cores(half_other)
    mid_got = swap_cores(mid)
    grad_short, short_mine, short_other = call(
        short_back_kernel,
        (in_hbm((short_rows, rest)), in_hbm((half, rest)), in_hbm((half, rest))),
        16 * 10**9,
        13 * 2**20,
        "short_back",
        vmem=56,
        grid=(2,),
        in_specs=[
            SMEM,
            cols_spec(short_rows, rest // 2),
            cols_spec(short_rows, gates // 2),
            cols_spec(short_rows, rest // 2),
            fixed_spec(short_rows, width),
        ],
        out_specs=[
            cols_spec(short_rows, rest // 2),
            cols_spec(half, rest // 2),
            cols_spec(half, rest // 2),
        ],
        scratch_shapes=[
            pltpu.VMEM((short_rows, rest // 2), F32),
            pltpu.VMEM((BLOCK, rest // 4), BF16),
        ],
    )(short_user, qkv_short, g_short, slope_short, xbf_short)
    mid_got, half_got, packs, grad_short = lax.optimization_barrier(
        (mid_got, half_got, packs, grad_short)
    )
    short_got = swap_cores(short_other)
    early = call(
        early_sums_kernel,
        in_hbm((half, 2 * gates)),
        8 * long_rows * half * gates,
        5 * 2**20,
        "early_sums",
    )(packs[0], cot_long, mid, half_got, mid_got, early_mine, early_got)
    all_g, early = lax.optimization_barrier((all_g, early))
    early = scatter_pairs(early)

    long_mine, long_other, *grads = call(
        long_back_kernel,
        (in_hbm((half, HW)),) * 2 + (shaped((long_rows, HW)),) * H,
        7 * 10**9,
        6 * 2**20,
        "long_back",
        in_specs=[SMEM] + [WHOLE] * (2 + H),
        scratch_shapes=[
            pltpu.VMEM((BLOCK, 2 * KW), F32),
            pltpu.VMEM((BLOCK, 2 * KW), F32),
            pltpu.VMEM((BLOCK, VW), F32),
            pltpu.VMEM((BLOCK, width), BF16),
            pltpu.VMEM((BLOCK, HW), BF16),
        ],
    )(long_blocks, whole, all_g, *packs)
    grads = swap_heads(grads)
    late = call(
        late_pair_sum_kernel,
        in_hbm((half, rest)),
        half * rest,
        4 * 2**20,
        "late_pair_sum",
        vmem=60,
        grid=(2,),
        in_specs=[rows_spec(half // 2, rest)] * 2 + [rows_spec(half // 2, HW)] * 2,
        out_specs=rows_spec(half // 2, rest),
    )(short_mine, short_got, long_mine, swap_cores(long_other))
    late, grads, gate_short = lax.optimization_barrier((late, grads, gate_short))
    late = scatter_pairs(late)

    def short_rows_spec(cols):
        return pl.BlockSpec((BLOCK, cols), lambda step: (jnp.minimum(step, 1), 0))

    back_short, back_long = call(
        input_back_kernel,
        (in_hbm((short_rows, width)), in_hbm((long_rows, width))),
        2 * (short_rows + long_rows) * width * cols,
        14 * 2**20,
        "input_back",
        vmem=60,
        grid=(short_rows // BLOCK + 1,),
        in_specs=[
            short_rows_spec(gates),
            short_rows_spec(rest),
            short_rows_spec(width),
            short_rows_spec(width),
            short_rows_spec(1),
            fixed_spec(width, gates),
            fixed_spec(width, rest),
        ]
        + [fixed_spec(long_rows, HW)] * H
        + [
            pl.BlockSpec((long_rows, gates), lambda step: (0, 1)),
            fixed_spec(long_rows, width),
            fixed_spec(long_rows, width + HW),
            fixed_spec(long_rows, 1),
        ],
        out_specs=[short_rows_spec(width), fixed_spec(long_rows, width)],
        scratch_shapes=[pltpu.VMEM((long_rows, rest), BF16)],
    )(
        gate_short,
        grad_short,
        cot_short,
        xbf_short,
        inv_short,
        proj_in,
        proj,
        *grads,
        mid,
        cot_long,
        packs[0],
        inv_long,
    )
    total_rows = lax.axis_size("dp") * sp_size * (long_rows + short_rows)
    early = jnp.sum(early.astype(F32), axis=0)
    sum_in, sum_out = call(
        functools.partial(final_sums_kernel, float(total_rows) ** (-0.5)),
        (shaped((early.shape[0], cols), F32), shaped((early.shape[0], gates), F32)),
        128 * 2**10,
        2**20,
        "final_sums",
    )(early, late)
    return (out_long, out_short, back_long, back_short, sum_in, sum_out)


def solution(mesh):
    rows = P(("dp", "sp"), None)
    return jax.shard_map(
        body,
        mesh=mesh,
        in_specs=(rows, rows, P(), rows, P(), P(), rows, rows),
        out_specs=(rows,) * 6,
        check_vma=False,
    )
```

```python
import functools

import jax
import jax.numpy as jnp
from jax import lax
from jax.experimental import pallas as pl
from jax.experimental.pallas import tpu as pltpu
from jax.sharding import PartitionSpec as P

H = 4
BLOCK = 512
KW = 64
VW = 128
HW = 2 * KW + VW
EPS = 1e-05
HALF_SCALE = 0.5 * KW**-0.5
F32 = jnp.float32
BF16 = jnp.bfloat16
MIB = 1024 * 1024


def dot(first, second, first_dim, second_dim):
    return lax.dot_general(
        first, second, (((first_dim,), (second_dim,)), ((), ())), preferred_element_type=F32
    )


def norm_rows(rows):
    center = rows - jnp.mean(rows, axis=-1, keepdims=True)
    inv_root = lax.rsqrt(jnp.mean(center * center, axis=-1, keepdims=True) + EPS)
    return center * inv_root, inv_root


def norm_back(upstream, normed, inv_root):
    return inv_root * (
        upstream
        - jnp.mean(upstream, axis=-1, keepdims=True)
        - normed * jnp.mean(upstream * normed, axis=-1, keepdims=True)
    )


def silu_half(half):
    return half * (1.0 + jnp.tanh(half))


def silu_both(half):
    curve = jnp.tanh(half)
    above = 1.0 + curve
    act = half * above
    return act, above + act * (1.0 - curve)


def low_lanes(shape):
    return lax.broadcasted_iota(jnp.int32, shape, 1) < KW


def turned(pair):
    return pltpu.roll(pair.astype(F32), KW, 1)


def score_side(qk):
    return jnp.where(low_lanes(qk.shape), 0.0, turned(qk) * HALF_SCALE).astype(BF16)


def causal(keys_first, keys, queries, key_start=0, query_start=0):
    shape = (keys, queries) if keys_first else (queries, keys)
    key_pos = key_start + lax.broadcasted_iota(jnp.int32, shape, 0 if keys_first else 1)
    query_pos = query_start + lax.broadcasted_iota(jnp.int32, shape, 1 if keys_first else 0)
    return key_pos <= query_pos


def project(x_bf, proj):
    act, slope = silu_both(0.5 * dot(x_bf, proj, 1, 0))
    return act.astype(BF16), 0.5 * slope


def head_out(x_rows, cot, proj_out, gate_u, slope_gate, mixed):
    mixed_n, inv_mix = norm_rows(mixed)
    gate_f = gate_u.astype(F32)
    gated = (mixed_n * gate_f).astype(BF16)
    out = (x_rows.astype(F32) + dot(gated, proj_out, 1, 0)).astype(BF16)
    grad_g = dot(cot, proj_out, 1, 1)
    grad_mixed = norm_back(grad_g * gate_f, mixed_n, inv_mix)
    grad_gate = (grad_g * mixed_n * slope_gate).astype(BF16)
    return out, gated, grad_gate, grad_mixed


def run_place():
    index = lax.axis_index("sp")
    return lax.rem(index, H), lax.div(index, H), lax.axis_index("dp")


def split_rows(part, start):
    for block in range(2):
        yield block, pl.ds(pl.multiple_of(start + 2 * part * block, part), part)


def long_project_kernel(
    x_ref, pin_q_ref, pin_k_ref, pin_v_ref, proj_ref, send_ref, inv_ref, xbf_ref, slope_ref
):
    @pl.when(pl.program_id(0) == 0)
    def _():
        normed, inv_std = norm_rows(x_ref[...].astype(F32))
        xbf_ref[...] = normed.astype(BF16)
        inv_ref[...] = inv_std

    q_pair, k_pair = pin_q_ref[...], pin_k_ref[...]
    low = low_lanes(q_pair.shape)
    even = jnp.where(low, q_pair.astype(F32), turned(k_pair)).astype(BF16)
    odd = jnp.where(low, turned(q_pair), k_pair.astype(F32)).astype(BF16)
    proj = jnp.concatenate([even, pin_v_ref[:, :VW], odd, pin_v_ref[:, VW:]], axis=1)
    proj_ref[...] = proj
    act, slope = project(xbf_ref[...], proj)
    slope_ref[...] = slope.astype(BF16)
    for copy in range(send_ref.shape[0]):
        for which in range(2):
            send_ref[copy, which] = act[:, HW * which : HW * (which + 1)]


def long_gate_kernel(xbf_ref, pin_ref, cot_ref, gate_ref, slope_gate_ref, half_ref):
    _, _, group = run_place()
    part = xbf_ref.shape[1] // 4
    act, slope = project(xbf_ref[...], pin_ref[...])
    gate_ref[...] = act
    slope_gate_ref[...] = slope.astype(BF16)
    for block, features in split_rows(part, (1 - lax.rem(group, 2)) * part):
        half_ref[:, block * part : (block + 1) * part] = cot_ref[:, features]
        half_ref[:, (block + 2) * part : (block + 3) * part] = xbf_ref[:, features]


def short_forward_kernel(
    user_ref,
    x_ref,
    cot_ref,
    pin_ref,
    proj_ref,
    pout_ref,
    out_ref,
    qkv_ref,
    g_ref,
    grad_gate_ref,
    slope_ref,
    xbf_ref,
    turned_ref,
    inv_ref,
    mine_ref,
    other_ref,
    sum_ref,
    seen_ref,
    mixed_ref,
    side_ref,
):
    step = pl.program_id(0)
    joined = user_ref[0, 0] == user_ref[0, 1]
    share = jnp.where(joined, 0.5 / BLOCK, 1.0 / BLOCK)
    normed, inv_std = norm_rows(x_ref[...].astype(F32))
    x_bf = normed.astype(BF16)
    xbf_ref[...] = x_bf
    turned_ref[...] = x_bf.T
    inv_ref[...] = inv_std
    act, slope = project(x_bf, proj_ref[...])
    slope_ref[...] = slope.astype(BF16)
    qkv_ref[...] = act
    gate_u, slope_gate = project(x_bf, pin_ref[...])
    half = BLOCK // 2
    for which in range(H):
        qk = act[:, HW * which : HW * which + 2 * KW]
        values = act[:, HW * which + 2 * KW : HW * (which + 1)]
        side = score_side(qk)
        scores = dot(side, qk[:half], 1, 1)
        weights = jnp.where(causal(False, half, BLOCK), silu_half(scores), 0.0).astype(BF16)
        mixed = dot(weights, values[:half], 1, 0)
        scores = dot(side[half:], qk[half:], 1, 1)
        weights = jnp.where(causal(False, half, half), silu_half(scores), 0.0).astype(BF16)
        lower = mixed[half:] + dot(weights, values[half:], 1, 0)
        mixed_ref[:half, VW * which : VW * (which + 1)] = mixed[:half]
        mixed_ref[half:, VW * which : VW * (which + 1)] = lower

        side_ref[:, 2 * KW * which : 2 * KW * (which + 1)] = side

    @pl.when(jnp.logical_and(step == 1, joined))
    def _():
        for which in range(H):
            first = HW * which
            side = side_ref[:, 2 * KW * which : 2 * KW * (which + 1)]
            scores = dot(side, seen_ref[:, first : first + 2 * KW], 1, 1)
            mixed_ref[:, VW * which : VW * (which + 1)] += dot(
                silu_half(scores).astype(BF16), seen_ref[:, first + 2 * KW : first + HW], 1, 0
            )

    @pl.when(step == 0)
    def _():
        seen_ref[...] = act

    out, gated, grad_gate, grad_mixed = head_out(
        x_ref[...],
        cot_ref[...],
        pout_ref[...],
        gate_u,
        slope_gate,
        mixed_ref[...] * share,
    )
    out_ref[...] = out
    grad_gate_ref[...] = grad_gate
    g_ref[...] = (grad_mixed.astype(BF16).astype(F32) * share).astype(BF16)
    gates = gated.shape[1]

    @pl.when(step == 0)
    def _():
        sum_ref[:, :gates] = dot(cot_ref[...], gated, 0, 0)
        sum_ref[:, gates:] = dot(turned_ref[...], grad_gate_ref[...], 1, 0)

    @pl.when(step == 1)
    def _():
        part = mine_ref.shape[0] // 2
        core = lax.rem(lax.axis_index("dp"), 2)
        for target, side in ((mine_ref, core), (other_ref, 1 - core)):
            for block, features in split_rows(part, side * part):
                here = slice(block * part, (block + 1) * part)
                total = sum_ref[features, :gates] + dot(cot_ref[:, features], gated, 0, 0)
                target[here, :gates] = total.astype(BF16)
                total = dot(turned_ref[features, :], grad_gate_ref[...], 1, 0)
                target[here, gates:] = (sum_ref[features, gates:] + total).astype(BF16)


def back_block(query_side, query_qk, key_qk, values, g_rows, mask):
    act, slope = silu_both(dot(key_qk, query_side, 1, 1))
    slopes = dot(values, g_rows, 1, 1) * slope
    if mask is not None:
        act = jnp.where(mask, act, 0.0)
        slopes = jnp.where(mask, slopes, 0.0)
    slopes = slopes.astype(BF16)
    grad_q = dot(slopes, key_qk, 0, 0)
    grad_k = dot(slopes, query_qk, 1, 0)
    grad_v = dot(act.astype(BF16), g_rows, 1, 0)
    return grad_q, grad_k, grad_v


def short_back_kernel(
    user_ref, qkv_ref, g_ref, slope_ref, turned_ref, grad_ref, mine_ref, other_ref, acc_ref, side_ref
):
    joined = user_ref[0, 0] == user_ref[0, 1]
    half = BLOCK // 2
    heads = range(qkv_ref.shape[1] // HW)
    for which in heads:
        first = HW * which
        qk = qkv_ref[:, first : first + 2 * KW]
        side = score_side(qk)
        values = qkv_ref[:, first + 2 * KW : first + HW]
        g_rows = g_ref[:, VW * which : VW * (which + 1)]
        lanes = low_lanes((half, 2 * KW))
        for block in range(qkv_ref.shape[0] // BLOCK):
            top = slice(block * BLOCK, block * BLOCK + half)
            end = slice(block * BLOCK + half, (block + 1) * BLOCK)
            both = slice(block * BLOCK, (block + 1) * BLOCK)
            dq_one, dk_one, dv_one = back_block(
                side[both], qk[both], qk[top], values[top], g_rows[both], causal(True, half, BLOCK)
            )
            dq_two, dk_two, dv_two = back_block(
                side[end], qk[end], qk[end], values[end], g_rows[end], causal(True, half, half)
            )
            acc_ref[top, first : first + 2 * KW] = jnp.where(lanes, dk_one, dq_one[:half])
            acc_ref[end, first : first + 2 * KW] = jnp.where(lanes, dk_two, dq_one[half:] + dq_two)
            acc_ref[top, first + 2 * KW : first + HW] = dv_one
            acc_ref[end, first + 2 * KW : first + HW] = dv_two
        side_ref[:, 2 * KW * which : 2 * KW * (which + 1)] = side[BLOCK:]

    @pl.when(joined)
    def _():
        one, two = slice(0, BLOCK), slice(BLOCK, 2 * BLOCK)
        for which in heads:
            first = HW * which
            pair = slice(first, first + 2 * KW)
            grad_q, grad_k, grad_v = back_block(
                side_ref[:, 2 * KW * which : 2 * KW * (which + 1)],
                qkv_ref[two, pair],
                qkv_ref[one, pair],
                qkv_ref[one, first + 2 * KW : first + HW],
                g_ref[two, VW * which : VW * (which + 1)],
                None,
            )
            lanes = low_lanes((BLOCK, 2 * KW))
            acc_ref[one, pair] += jnp.where(lanes, grad_k, 0.0)
            acc_ref[two, pair] += jnp.where(lanes, 0.0, grad_q)
            acc_ref[one, first + 2 * KW : first + HW] += grad_v

    for which in heads:
        first = HW * which
        pair, rest = slice(first, first + 2 * KW), slice(first + 2 * KW, first + HW)
        grads = turned(acc_ref[:, pair]) * HALF_SCALE
        grad_ref[:, pair] = (grads * slope_ref[:, pair].astype(F32)).astype(BF16)
        grad_ref[:, rest] = (acc_ref[:, rest] * slope_ref[:, rest].astype(F32)).astype(BF16)
    grad_pre = grad_ref[...]
    part = mine_ref.shape[0] // 2
    core = lax.rem(lax.axis_index("dp"), 2)
    for target, side in ((mine_ref, core), (other_ref, 1 - core)):
        for block, features in split_rows(part, side * part):
            total = dot(turned_ref[features, :], grad_pre, 1, 0)
            target[block * part : (block + 1) * part] = total.astype(BF16)


def rows_at(index):
    return pl.ds(pl.multiple_of(index * BLOCK, BLOCK), BLOCK)


def long_attend_kernel(blocks_smem, all_ref, *refs):
    mixed_refs, acc_ref = refs[:H], refs[H]
    mine, chunk, group = run_place()
    valid = blocks_smem[group]
    acc_ref[...] = jnp.zeros_like(acc_ref)

    @pl.when(chunk < valid)
    def _():
        side = score_side(all_ref[rows_at(chunk), : 2 * KW])

        @pl.loop(0, chunk)
        def _(index):
            scores = dot(side, all_ref[rows_at(index), : 2 * KW], 1, 1)
            acc_ref[...] += dot(
                silu_half(scores).astype(BF16), all_ref[rows_at(index), 2 * KW :], 1, 0
            )

        weights = silu_half(dot(side, all_ref[rows_at(chunk), : 2 * KW], 1, 1))
        weights = jnp.where(causal(False, BLOCK, BLOCK), weights, 0.0).astype(BF16)
        acc_ref[...] += dot(weights, all_ref[rows_at(chunk), 2 * KW :], 1, 0)

    coeff = 1.0 / (valid * BLOCK).astype(F32)
    rows = mixed_refs[0].shape[0]
    for bits in range(H):
        start = pl.multiple_of((mine ^ bits) * rows, rows)
        mixed_refs[bits][...] = (acc_ref[pl.ds(start, rows), :] * coeff).astype(BF16)


def long_back_kernel(blocks_smem, all_ref, g_ref, *refs):
    grad_refs, (dq_ref, dk_ref, dv_ref) = refs[:H], refs[H:]
    mine, chunk, group = run_place()
    valid = blocks_smem[group]
    dq_ref[...] = jnp.zeros_like(dq_ref)
    dk_ref[...] = jnp.zeros_like(dk_ref)
    dv_ref[...] = jnp.zeros_like(dv_ref)

    @pl.when(chunk < valid)
    def _():
        own = rows_at(chunk)
        qk = all_ref[own, : 2 * KW]
        side = score_side(qk)
        values = all_ref[own, 2 * KW :]
        g_own = g_ref[own, :]
        grad_q, grad_k, grad_v = back_block(
            side, qk, qk, values, g_own, causal(True, BLOCK, BLOCK)
        )
        dq_ref[...] = grad_q
        dk_ref[...] = grad_k
        dv_ref[...] = grad_v

        @pl.loop(0, chunk)
        def _(index):
            keys = all_ref[rows_at(index), : 2 * KW]
            act, slope = silu_both(dot(side, keys, 1, 1))
            slopes = dot(g_own, all_ref[rows_at(index), 2 * KW :], 1, 1) * slope
            dq_ref[...] += dot(slopes.astype(BF16), keys, 1, 0)

        @pl.loop(chunk + 1, valid)
        def _(index):
            g_rows = g_ref[rows_at(index), :]
            queries = all_ref[rows_at(index), : 2 * KW]
            act, slope = silu_both(dot(qk, score_side(queries), 1, 1))
            slopes = (dot(values, g_rows, 1, 1) * slope).astype(BF16)
            dk_ref[...] += dot(slopes, queries, 1, 0)
            dv_ref[...] += dot(act.astype(BF16), g_rows, 1, 0)

    coeff = 1.0 / (valid * BLOCK).astype(F32)
    rows = grad_refs[0].shape[0]
    lanes = low_lanes((rows, 2 * KW))
    for bits in range(H):
        part = pl.ds(pl.multiple_of((mine ^ bits) * rows, rows), rows)
        pair = turned(jnp.where(lanes, dk_ref[part, :], dq_ref[part, :])) * HALF_SCALE
        grad_refs[bits][:, : 2 * KW] = (pair * coeff).astype(BF16)
        grad_refs[bits][:, 2 * KW :] = (dv_ref[part, :] * coeff).astype(BF16)


def long_head_kernel(
    got_0,
    got_1,
    got_2,
    got_3,
    x_ref,
    cot_ref,
    pout_ref,
    gate_ref,
    slope_ref,
    out_ref,
    send_ref,
    mid_ref,
    mixed_ref,
):
    mine, _, _ = run_place()
    for bits, got in enumerate((got_0, got_1, got_2, got_3)):
        start = pl.multiple_of((mine ^ bits) * VW, VW)
        mixed_ref[:, pl.ds(start, VW)] = got[...].astype(F32)
    out, gated, grad_gate, grad_mixed = head_out(
        x_ref[...],
        cot_ref[...],
        pout_ref[...],
        gate_ref[...],
        slope_ref[...].astype(F32),
        mixed_ref[...],
    )
    out_ref[...] = out
    cols = gated.shape[1]
    mid_ref[:, :cols] = gated
    mid_ref[:, cols:] = grad_gate
    grad_mixed = grad_mixed.astype(BF16)
    for copy in range(send_ref.shape[0]):
        for which in range(H):
            send_ref[copy, which] = grad_mixed[:, VW * which : VW * (which + 1)]


def early_sums_kernel(
    xbf_ref, cot_ref, mid_ref, half_ref, mid_got, mine_ref, got_ref, sum_ref
):
    cols = mid_ref.shape[1] // 2
    part = sum_ref.shape[0] // 2
    core = lax.rem(lax.axis_index("dp"), 2)
    mid = jnp.concatenate([mid_ref[...], mid_got[...]], axis=0)
    for block, features in split_rows(part, core * part):
        here = slice(block * part, (block + 1) * part)
        for place, own in ((0, cot_ref), (1, xbf_ref)):
            start = (2 * place + block) * part
            rows = jnp.concatenate([own[:, features], half_ref[:, start : start + part]], axis=0)
            there = slice(place * cols, (place + 1) * cols)
            total = mine_ref[here, there].astype(F32) + got_ref[here, there].astype(F32)
            sum_ref[here, there] = (total + dot(rows, mid[:, there], 0, 0)).astype(BF16)


def long_slopes_kernel(got_0, got_1, got_2, got_3, slope_ref, grad_ref):
    mine, _, _ = run_place()
    for bits, got in enumerate((got_0, got_1, got_2, got_3)):
        there = pl.ds(pl.multiple_of((mine ^ bits) * HW, HW), HW)
        grads = got[...].astype(F32) * slope_ref[:, there].astype(F32)
        grad_ref[:, there] = grads.astype(BF16)


def late_sums_kernel(mine_ref, got_ref, xbf_ref, half_ref, grad_ref, grad_got, sum_ref):
    part = sum_ref.shape[0]
    core = lax.rem(lax.axis_index("dp"), 2)
    start = (core + 2 * pl.program_id(0)) * part
    features = pl.ds(pl.multiple_of(start, part), part)
    rows = jnp.concatenate([xbf_ref[:, features], half_ref[...]], axis=0)
    grads = jnp.concatenate([grad_ref[...], grad_got[...]], axis=0)
    total = mine_ref[...].astype(F32) + got_ref[...].astype(F32)
    sum_ref[...] = (total + dot(rows, grads, 0, 0)).astype(BF16)


def final_sums_kernel(factor, early_ref, late_ref, in_ref, out_ref):
    gates = out_ref.shape[1]
    out_ref[...] = early_ref[:, :gates] * factor
    in_ref[:, :gates] = early_ref[:, gates:] * factor
    late = late_ref[0].astype(F32)
    for step in range(1, late_ref.shape[0]):
        late += late_ref[step].astype(F32)
    late = late * factor
    low = low_lanes((late.shape[0], 2 * KW))
    for pair in range(H // 2):
        first = 2 * HW * pair
        even, odd = late[:, first : first + 2 * KW], late[:, first + HW : first + HW + 2 * KW]
        first_q = gates + 2 * KW * pair
        first_k = first_q + H * KW
        first_v = gates + 2 * H * KW + 2 * VW * pair
        in_ref[:, first_q : first_q + 2 * KW] = jnp.where(low, even, turned(odd))
        in_ref[:, first_k : first_k + 2 * KW] = jnp.where(low, turned(even), odd)
        in_ref[:, first_v : first_v + VW] = late[:, first + 2 * KW : first + HW]
        in_ref[:, first_v + VW : first_v + 2 * VW] = late[:, first + HW + 2 * KW : first + 2 * HW]


def input_back_kernel(
    grad_gate_ref,
    grad_ref,
    cot_ref,
    xbf_ref,
    inv_ref,
    pin_ref,
    proj_ref,
    long_gate_ref,
    long_grad_ref,
    long_cot_ref,
    long_xbf_ref,
    long_inv_ref,
    back_ref,
    long_back_ref,
):
    step = pl.program_id(0)

    def finish(gate, grad, cot, normed, inv, target):
        grad_norm = dot(gate[...], pin_ref[...], 1, 1) + dot(grad[...], proj_ref[...], 1, 1)
        back = norm_back(grad_norm, normed.astype(F32), inv[...])
        target[...] = (cot[...].astype(F32) + back).astype(BF16)

    @pl.when(step < 2)
    def _():
        finish(grad_gate_ref, grad_ref, cot_ref, xbf_ref[...], inv_ref, back_ref)

    @pl.when(step == 2)
    def _():
        finish(
            long_gate_ref,
            long_grad_ref,
            long_cot_ref,
            long_xbf_ref[...],
            long_inv_ref,
            long_back_ref,
        )


def shaped(shape, dtype=BF16):
    return jax.ShapeDtypeStruct(shape, dtype)


def in_hbm(shape, dtype=BF16):
    return pltpu.HBM(shape, dtype)


def call(kernel, out_shape, flops, moved, name, vmem=24, **kwargs):
    return pl.pallas_call(
        kernel,
        out_shape=out_shape,
        cost_estimate=pl.CostEstimate(flops=flops, bytes_accessed=moved, transcendentals=0),
        compiler_params=pltpu.CompilerParams(vmem_limit_bytes=vmem * MIB),
        name=name,
        **kwargs,
    )


SMEM = pl.BlockSpec(memory_space=pltpu.SMEM)
WHOLE = pl.BlockSpec(memory_space=pltpu.VMEM)


def rows_spec(rows, cols):
    return pl.BlockSpec((rows, cols), lambda step: (step, 0))


def cols_spec(rows, cols):
    return pl.BlockSpec((rows, cols), lambda step: (0, step))


def fixed_spec(rows, cols):
    return pl.BlockSpec((rows, cols), lambda step: (0, 0))


def swap_heads(pieces):
    size = lax.axis_size("sp")
    return [pieces[0]] + [
        lax.ppermute(pieces[bits], "sp", [(src, src ^ bits) for src in range(size)])
        for bits in range(1, H)
    ]


def spread_heads(sent):
    chunks, heads, rows, cols = sent.shape
    got = lax.all_to_all(sent.reshape(chunks * heads, rows, cols), "sp", 0, 0, tiled=True)
    return got.reshape(chunks * heads * rows, cols)


def swap_cores(half):
    size = lax.axis_size("dp")
    return lax.ppermute(half, "dp", [(src, src ^ 1) for src in range(size)])


def scatter_pairs(partial):
    runs, size = lax.axis_size("dp"), lax.axis_size("sp")
    groups = [
        [run * size + place for run in range(core, runs, 2) for place in range(size)]
        for core in range(2)
    ]
    count = len(groups[0])
    sent = partial.reshape(count, partial.shape[0] // count, partial.shape[1])
    return lax.all_to_all(sent, ("dp", "sp"), 0, 0, tiled=True, axis_index_groups=groups)


def body(x_long, x_short, long_blocks, short_user, proj_in, proj_out, cot_long, cot_short):
    sp_size = lax.axis_size("sp")
    long_rows, width = x_long.shape
    short_rows = x_short.shape[0]
    gates = proj_out.shape[0]
    cols = proj_in.shape[1]
    rest = cols - gates
    half = width // 2
    chunks = sp_size // H

    proj, sent, inv_long, xbf_long, slope_rest = call(
        long_project_kernel,
        (
            in_hbm((width, rest)),
            in_hbm((chunks, H, long_rows, HW)),
            in_hbm((long_rows, 1), F32),
            in_hbm((long_rows, width)),
            in_hbm((long_rows, rest)),
        ),
        2 * long_rows * width * rest,
        8 * 2**20,
        "long_project",
        vmem=60,
        grid=(2,),
        in_specs=[
            fixed_spec(long_rows, width),
            pl.BlockSpec((width, 2 * KW), lambda step: (0, step + gates // (2 * KW))),
            pl.BlockSpec((width, 2 * KW), lambda step: (0, step + (gates + H * KW) // (2 * KW))),
            pl.BlockSpec((width, 2 * VW), lambda step: (0, step + (gates + 2 * H * KW) // (2 * VW))),
        ],
        out_specs=[
            cols_spec(width, rest // 2),
            pl.BlockSpec((chunks, 2, long_rows, HW), lambda step: (0, step, 0, 0)),
            fixed_spec(long_rows, 1),
            fixed_spec(long_rows, width),
            cols_spec(long_rows, rest // 2),
        ],
    )(x_long, proj_in, proj_in, proj_in)
    whole = spread_heads(sent)
    gate_long, slope_long, half_other = call(
        long_gate_kernel,
        (
            shaped((long_rows, gates)),
            shaped((long_rows, gates)),
            in_hbm((long_rows, width)),
        ),
        2 * long_rows * width * gates,
        4 * 2**20,
        "long_gate",
        grid=(1,),
        in_specs=[
            fixed_spec(long_rows, width),
            fixed_spec(width, gates),
            fixed_spec(long_rows, width),
        ],
        out_specs=[
            fixed_spec(long_rows, gates),
            fixed_spec(long_rows, gates),
            fixed_spec(long_rows, width),
        ],
    )(xbf_long, proj_in, cot_long)

    short_out = call(
        short_forward_kernel,
        (
            in_hbm((short_rows, width)),
            in_hbm((short_rows, rest)),
            in_hbm((short_rows, gates)),
            in_hbm((short_rows, gates)),
            in_hbm((short_rows, rest)),
            in_hbm((short_rows, width)),
            in_hbm((width, short_rows)),
            in_hbm((short_rows, 1), F32),
            in_hbm((half, 2 * gates)),
            in_hbm((half, 2 * gates)),
        ),
        20 * 10**9,
        24 * 2**20,
        "short_forward",
        vmem=56,
        grid=(short_rows // BLOCK,),
        in_specs=[
            SMEM,
            rows_spec(BLOCK, width),
            rows_spec(BLOCK, width),
            fixed_spec(width, gates),
            fixed_spec(width, rest),
            fixed_spec(gates, width),
        ],
        out_specs=[
            rows_spec(BLOCK, width),
            rows_spec(BLOCK, rest),
            rows_spec(BLOCK, gates),
            rows_spec(BLOCK, gates),
            rows_spec(BLOCK, rest),
            rows_spec(BLOCK, width),
            cols_spec(width, BLOCK),
            rows_spec(BLOCK, 1),
            fixed_spec(half, 2 * gates),
            fixed_spec(half, 2 * gates),
        ],
        scratch_shapes=[
            pltpu.VMEM((width, 2 * gates), F32),
            pltpu.VMEM((BLOCK, rest), BF16),
            pltpu.VMEM((BLOCK, gates), F32),
            pltpu.VMEM((BLOCK, 2 * KW * H), BF16),
        ],
    )(short_user, x_short, cot_short, proj_in, proj, proj_out)
    out_short, qkv_short, g_short, gate_short, slope_short, xbf_short = short_out[:6]
    turned_short, inv_short, early_mine, early_other = short_out[6:]
    early_got = swap_cores(early_other)


    whole, early_got, out_short = lax.optimization_barrier((whole, early_got, out_short))
    mixed = call(
        long_attend_kernel,
        (shaped((long_rows, VW)),) * H,
        2 * 10**9,
        2 * 2**20,
        "long_attend",
        in_specs=[SMEM, WHOLE],
        scratch_shapes=[
            pltpu.VMEM((BLOCK, VW), F32),
        ],
    )(long_blocks, whole)
    out_long, sent, mid = call(
        long_head_kernel,
        (
            shaped((long_rows, width)),
            in_hbm((chunks, H, long_rows, VW)),
            in_hbm((long_rows, 2 * gates)),
        ),
        4 * long_rows * width * gates,
        3 * 2**20,
        "long_head",
        in_specs=[WHOLE] * 9,
        scratch_shapes=[pltpu.VMEM((long_rows, gates), F32)],
    )(*swap_heads(mixed), x_long, cot_long, proj_out, gate_long, slope_long)
    sent, qkv_short, mid, half_other = lax.optimization_barrier((sent, qkv_short, mid, half_other))
    all_g = spread_heads(sent)
    half_got = swap_cores(half_other)
    mid_got = swap_cores(mid)
    grad_short, short_mine, short_other = call(
        short_back_kernel,
        (in_hbm((short_rows, rest)), in_hbm((half, rest)), in_hbm((half, rest))),
        16 * 10**9,
        13 * 2**20,
        "short_back",
        vmem=56,
        grid=(2,),
        in_specs=[
            SMEM,
            cols_spec(short_rows, rest // 2),
            cols_spec(short_rows, gates // 2),
            cols_spec(short_rows, rest // 2),
            fixed_spec(width, short_rows),
        ],
        out_specs=[
            cols_spec(short_rows, rest // 2),
            cols_spec(half, rest // 2),
            cols_spec(half, rest // 2),
        ],
        scratch_shapes=[
            pltpu.VMEM((short_rows, rest // 2), F32),
            pltpu.VMEM((BLOCK, rest // 4), BF16),
        ],
    )(short_user, qkv_short, g_short, slope_short, turned_short)
    mid_got, half_got, grad_short = lax.optimization_barrier((mid_got, half_got, grad_short))
    short_got = swap_cores(short_other)
    early = call(
        early_sums_kernel,
        in_hbm((half, 2 * gates)),
        8 * long_rows * half * gates,
        5 * 2**20,
        "early_sums",
    )(xbf_long, cot_long, mid, half_got, mid_got, early_mine, early_got)
    all_g, early = lax.optimization_barrier((all_g, early))
    early = scatter_pairs(early)

    grads = call(
        long_back_kernel,
        (shaped((long_rows, HW)),) * H,
        6 * 10**9,
        4 * 2**20,
        "long_back",
        in_specs=[SMEM, WHOLE, WHOLE],
        scratch_shapes=[
            pltpu.VMEM((BLOCK, 2 * KW), F32),
            pltpu.VMEM((BLOCK, 2 * KW), F32),
            pltpu.VMEM((BLOCK, VW), F32),
        ],
    )(long_blocks, whole, all_g)
    grad_long = call(
        long_slopes_kernel,
        shaped((long_rows, rest)),
        long_rows * rest,
        2**20,
        "long_slopes",
    )(*swap_heads(grads), slope_rest)
    late = call(
        late_sums_kernel,
        in_hbm((half, rest)),
        4 * long_rows * half * rest,
        5 * 2**20,
        "late_sums",
        grid=(2,),
        in_specs=[
            rows_spec(half // 2, rest),
            rows_spec(half // 2, rest),
            fixed_spec(long_rows, width),
            pl.BlockSpec((long_rows, half // 2), lambda step: (0, step + 2)),
            fixed_spec(long_rows, rest),
            fixed_spec(long_rows, rest),
        ],
        out_specs=rows_spec(half // 2, rest),
    )(short_mine, short_got, xbf_long, half_got, grad_long, swap_cores(grad_long))
    late, gate_short = lax.optimization_barrier((late, gate_short))
    late = scatter_pairs(late)

    def short_rows_spec(cols):
        return pl.BlockSpec((BLOCK, cols), lambda step: (jnp.minimum(step, 1), 0))

    back_short, back_long = call(
        input_back_kernel,
        (in_hbm((short_rows, width)), in_hbm((long_rows, width))),
        2 * (short_rows + long_rows) * width * cols,
        14 * 2**20,
        "input_back",
        vmem=60,
        grid=(short_rows // BLOCK + 1,),
        in_specs=[
            short_rows_spec(gates),
            short_rows_spec(rest),
            short_rows_spec(width),
            short_rows_spec(width),
            short_rows_spec(1),
            fixed_spec(width, gates),
            fixed_spec(width, rest),
        ]
        + [
            pl.BlockSpec((long_rows, gates), lambda step: (0, 1)),
            fixed_spec(long_rows, rest),
            fixed_spec(long_rows, width),
            fixed_spec(long_rows, width),
            fixed_spec(long_rows, 1),
        ],
        out_specs=[short_rows_spec(width), fixed_spec(long_rows, width)],
    )(
        gate_short,
        grad_short,
        cot_short,
        xbf_short,
        inv_short,
        proj_in,
        proj,
        mid,
        grad_long,
        cot_long,
        xbf_long,
        inv_long,
    )
    total_rows = lax.axis_size("dp") * sp_size * (long_rows + short_rows)
    early = jnp.sum(early.astype(F32), axis=0)
    sum_in, sum_out = call(
        functools.partial(final_sums_kernel, float(total_rows) ** (-0.5)),
        (shaped((early.shape[0], cols), F32), shaped((early.shape[0], gates), F32)),
        128 * 2**10,
        2**20,
        "final_sums",
    )(early, late)
    return (out_long, out_short, back_long, back_short, sum_in, sum_out)


def solution(mesh):
    rows = P(("dp", "sp"), None)
    return jax.shard_map(
        body,
        mesh=mesh,
        in_specs=(rows, rows, P(), rows, P(), P(), rows, rows),
        out_specs=(rows,) * 6,
        check_vma=False,
    )
```

```python
import functools

import jax
import jax.numpy as jnp
from jax import lax
from jax.experimental import pallas as pl
from jax.experimental.pallas import tpu as pltpu
from jax.sharding import PartitionSpec as P

H = 4
BLOCK = 512
KW = 64
VW = 128
HW = 2 * KW + VW
EPS = 1e-05
HALF_SCALE = 0.5 * KW**-0.5
F32 = jnp.float32
BF16 = jnp.bfloat16
MIB = 1024 * 1024


def dot(first, second, first_dim, second_dim):
    return lax.dot_general(
        first, second, (((first_dim,), (second_dim,)), ((), ())), preferred_element_type=F32
    )


def norm_rows(rows):
    center = rows - jnp.mean(rows, axis=-1, keepdims=True)
    inv_root = lax.rsqrt(jnp.mean(center * center, axis=-1, keepdims=True) + EPS)
    return center * inv_root, inv_root


def norm_back(upstream, normed, inv_root):
    return inv_root * (
        upstream
        - jnp.mean(upstream, axis=-1, keepdims=True)
        - normed * jnp.mean(upstream * normed, axis=-1, keepdims=True)
    )


def silu_half(half):
    return half * (1.0 + jnp.tanh(half))


def silu_both(half):
    curve = jnp.tanh(half)
    above = 1.0 + curve
    act = half * above
    return act, above + act * (1.0 - curve)


def low_lanes(shape):
    return lax.broadcasted_iota(jnp.int32, shape, 1) < KW


def turned(pair):
    return pltpu.roll(pair.astype(F32), KW, 1)


def score_side(qk):
    return jnp.where(low_lanes(qk.shape), 0.0, turned(qk) * HALF_SCALE).astype(BF16)


def causal(keys_first, keys, queries, key_start=0, query_start=0):
    shape = (keys, queries) if keys_first else (queries, keys)
    key_pos = key_start + lax.broadcasted_iota(jnp.int32, shape, 0 if keys_first else 1)
    query_pos = query_start + lax.broadcasted_iota(jnp.int32, shape, 1 if keys_first else 0)
    return key_pos <= query_pos


def project(x_bf, proj):
    act, slope = silu_both(0.5 * dot(x_bf, proj, 1, 0))
    return act.astype(BF16), 0.5 * slope


def head_out(x_rows, cot, proj_out, gate_u, slope_gate, mixed):
    mixed_n, inv_mix = norm_rows(mixed)
    gate_f = gate_u.astype(F32)
    gated = (mixed_n * gate_f).astype(BF16)
    out = (x_rows.astype(F32) + dot(gated, proj_out, 1, 0)).astype(BF16)
    grad_g = dot(cot, proj_out, 1, 1)
    grad_mixed = norm_back(grad_g * gate_f, mixed_n, inv_mix)
    grad_gate = (grad_g * mixed_n * slope_gate).astype(BF16)
    return out, gated, grad_gate, grad_mixed


def run_place():
    index = lax.axis_index("sp")
    return lax.rem(index, H), lax.div(index, H), lax.axis_index("dp")


def split_rows(part, start):
    for block in range(2):
        yield block, pl.ds(pl.multiple_of(start + 2 * part * block, part), part)


def long_project_kernel(
    x_ref, pin_q_ref, pin_k_ref, pin_v_ref, proj_ref, send_ref, inv_ref, xbf_ref, slope_ref
):
    @pl.when(pl.program_id(0) == 0)
    def _():
        normed, inv_std = norm_rows(x_ref[...].astype(F32))
        xbf_ref[...] = normed.astype(BF16)
        inv_ref[...] = inv_std

    q_pair, k_pair = pin_q_ref[...], pin_k_ref[...]
    low = low_lanes(q_pair.shape)
    even = jnp.where(low, q_pair.astype(F32), turned(k_pair)).astype(BF16)
    odd = jnp.where(low, turned(q_pair), k_pair.astype(F32)).astype(BF16)
    proj = jnp.concatenate([even, pin_v_ref[:, :VW], odd, pin_v_ref[:, VW:]], axis=1)
    proj_ref[...] = proj
    act, slope = project(xbf_ref[...], proj)
    slope_ref[...] = slope.astype(BF16)
    for copy in range(send_ref.shape[0]):
        for which in range(2):
            send_ref[copy, which] = act[:, HW * which : HW * (which + 1)]


def long_gate_kernel(xbf_ref, pin_ref, cot_ref, gate_ref, slope_gate_ref, half_ref):
    _, _, group = run_place()
    part = xbf_ref.shape[1] // 4
    act, slope = project(xbf_ref[...], pin_ref[...])
    gate_ref[...] = act
    slope_gate_ref[...] = slope.astype(BF16)
    for block, features in split_rows(part, (1 - lax.rem(group, 2)) * part):
        half_ref[:, block * part : (block + 1) * part] = cot_ref[:, features]
        half_ref[:, (block + 2) * part : (block + 3) * part] = xbf_ref[:, features]


def head_lanes(which):
    first = pl.multiple_of(which * HW, HW)
    last = pl.multiple_of(which * HW + 2 * KW, VW)
    return pl.ds(first, 2 * KW), pl.ds(last, VW), pl.ds(pl.multiple_of(which * VW, VW), VW)


def back_block(query_side, query_qk, key_qk, values, g_rows, mask):
    act, slope = silu_both(dot(key_qk, query_side, 1, 1))
    slopes = dot(values, g_rows, 1, 1) * slope
    if mask is not None:
        act = jnp.where(mask, act, 0.0)
        slopes = jnp.where(mask, slopes, 0.0)
    slopes = slopes.astype(BF16)
    grad_q = dot(slopes, key_qk, 0, 0)
    grad_k = dot(slopes, query_qk, 1, 0)
    grad_v = dot(act.astype(BF16), g_rows, 1, 0)
    return grad_q, grad_k, grad_v


def short_forward_kernel(
    user_ref,
    x_ref,
    cot_ref,
    pin_ref,
    proj_ref,
    pout_ref,
    out_ref,
    qkv_ref,
    g_ref,
    grad_gate_ref,
    slope_ref,
    xbf_ref,
    turned_ref,
    inv_ref,
    mine_ref,
    other_ref,
    join_ref,
    sum_ref,
    seen_ref,
    mixed_ref,
    side_ref,
):
    step = pl.program_id(0)
    joined = user_ref[0, 0] == user_ref[0, 1]
    share = jnp.where(joined, 0.5 / BLOCK, 1.0 / BLOCK)
    normed, inv_std = norm_rows(x_ref[...].astype(F32))
    x_bf = normed.astype(BF16)
    xbf_ref[...] = x_bf
    turned_ref[...] = x_bf.T
    inv_ref[...] = inv_std
    act, slope = project(x_bf, proj_ref[...])
    slope_ref[...] = slope.astype(BF16)
    qkv_ref[...] = act
    gate_u, slope_gate = project(x_bf, pin_ref[...])
    half = BLOCK // 2
    for which in range(H):
        qk = act[:, HW * which : HW * which + 2 * KW]
        values = act[:, HW * which + 2 * KW : HW * (which + 1)]
        side = score_side(qk)
        scores = dot(side, qk[:half], 1, 1)
        weights = jnp.where(causal(False, half, BLOCK), silu_half(scores), 0.0).astype(BF16)
        mixed = dot(weights, values[:half], 1, 0)
        scores = dot(side[half:], qk[half:], 1, 1)
        weights = jnp.where(causal(False, half, half), silu_half(scores), 0.0).astype(BF16)
        lower = mixed[half:] + dot(weights, values[half:], 1, 0)
        mixed_ref[:half, VW * which : VW * (which + 1)] = mixed[:half]
        mixed_ref[half:, VW * which : VW * (which + 1)] = lower

        side_ref[:, 2 * KW * which : 2 * KW * (which + 1)] = side

    @pl.when(jnp.logical_and(step == 1, joined))
    def _():
        @pl.loop(0, H)
        def _(which):
            pair, rest, narrow = head_lanes(which)
            scores = dot(side_ref[:, narrow], seen_ref[:, pair], 1, 1)
            weights = silu_half(scores).astype(BF16)
            mixed_ref[:, narrow] += dot(weights, seen_ref[:, rest], 1, 0)

    @pl.when(step == 0)
    def _():
        seen_ref[...] = act

    out, gated, grad_gate, grad_mixed = head_out(
        x_ref[...],
        cot_ref[...],
        pout_ref[...],
        gate_u,
        slope_gate,
        mixed_ref[...] * share,
    )
    out_ref[...] = out
    grad_gate_ref[...] = grad_gate
    g_ref[...] = (grad_mixed.astype(BF16).astype(F32) * share).astype(BF16)
    gates = gated.shape[1]

    @pl.when(jnp.logical_and(step == 1, joined))
    def _():
        lanes = low_lanes((BLOCK, 2 * KW))

        @pl.loop(0, H)
        def _(which):
            pair, rest, narrow = head_lanes(which)
            grad_q, grad_k, grad_v = back_block(
                side_ref[:, narrow],
                qkv_ref[:, pair],
                seen_ref[:, pair],
                seen_ref[:, rest],
                g_ref[:, narrow],
                None,
            )
            join_ref[:BLOCK, pair] = jnp.where(lanes, grad_k, 0.0).astype(BF16)
            join_ref[:BLOCK, rest] = grad_v.astype(BF16)
            join_ref[BLOCK:, pair] = jnp.where(lanes, 0.0, grad_q).astype(BF16)
            join_ref[BLOCK:, rest] = jnp.zeros(grad_v.shape, BF16)

    @pl.when(step == 0)
    def _():
        sum_ref[:, :gates] = dot(cot_ref[...], gated, 0, 0)
        sum_ref[:, gates:] = dot(turned_ref[...], grad_gate_ref[...], 1, 0)

    @pl.when(step == 1)
    def _():
        part = mine_ref.shape[0] // 2
        core = lax.rem(lax.axis_index("dp"), 2)
        for target, side in ((mine_ref, core), (other_ref, 1 - core)):
            for block, features in split_rows(part, side * part):
                here = slice(block * part, (block + 1) * part)
                total = sum_ref[features, :gates] + dot(cot_ref[:, features], gated, 0, 0)
                target[here, :gates] = total.astype(BF16)
                total = dot(turned_ref[features, :], grad_gate_ref[...], 1, 0)
                target[here, gates:] = (sum_ref[features, gates:] + total).astype(BF16)


def short_back_kernel(
    user_ref, qkv_ref, g_ref, slope_ref, turned_ref, join_ref, grad_ref, mine_ref, other_ref, acc_ref
):
    joined = user_ref[0, 0] == user_ref[0, 1]
    half = BLOCK // 2
    heads = range(qkv_ref.shape[1] // HW)
    for which in heads:
        first = HW * which
        qk = qkv_ref[:, first : first + 2 * KW]
        side = score_side(qk)
        values = qkv_ref[:, first + 2 * KW : first + HW]
        g_rows = g_ref[:, VW * which : VW * (which + 1)]
        lanes = low_lanes((half, 2 * KW))
        for block in range(qkv_ref.shape[0] // BLOCK):
            top = slice(block * BLOCK, block * BLOCK + half)
            end = slice(block * BLOCK + half, (block + 1) * BLOCK)
            both = slice(block * BLOCK, (block + 1) * BLOCK)
            dq_one, dk_one, dv_one = back_block(
                side[both], qk[both], qk[top], values[top], g_rows[both], causal(True, half, BLOCK)
            )
            dq_two, dk_two, dv_two = back_block(
                side[end], qk[end], qk[end], values[end], g_rows[end], causal(True, half, half)
            )
            acc_ref[top, first : first + 2 * KW] = jnp.where(lanes, dk_one, dq_one[:half])
            acc_ref[end, first : first + 2 * KW] = jnp.where(lanes, dk_two, dq_one[half:] + dq_two)
            acc_ref[top, first + 2 * KW : first + HW] = dv_one
            acc_ref[end, first + 2 * KW : first + HW] = dv_two

    @pl.when(joined)
    def _():
        acc_ref[...] += join_ref[...].astype(F32)

    for which in heads:
        first = HW * which
        pair, rest = slice(first, first + 2 * KW), slice(first + 2 * KW, first + HW)
        grads = turned(acc_ref[:, pair]) * HALF_SCALE
        grad_ref[:, pair] = (grads * slope_ref[:, pair].astype(F32)).astype(BF16)
        grad_ref[:, rest] = (acc_ref[:, rest] * slope_ref[:, rest].astype(F32)).astype(BF16)
    grad_pre = grad_ref[...]
    part = mine_ref.shape[0] // 2
    core = lax.rem(lax.axis_index("dp"), 2)
    for target, side in ((mine_ref, core), (other_ref, 1 - core)):
        for block, features in split_rows(part, side * part):
            total = dot(turned_ref[features, :], grad_pre, 1, 0)
            target[block * part : (block + 1) * part] = total.astype(BF16)


def rows_at(index):
    return pl.ds(pl.multiple_of(index * BLOCK, BLOCK), BLOCK)


def long_attend_kernel(blocks_smem, all_ref, *refs):
    mixed_refs, acc_ref = refs[:H], refs[H]
    mine, chunk, group = run_place()
    valid = blocks_smem[group]
    acc_ref[...] = jnp.zeros_like(acc_ref)

    @pl.when(chunk < valid)
    def _():
        side = score_side(all_ref[rows_at(chunk), : 2 * KW])

        @pl.loop(0, chunk)
        def _(index):
            scores = dot(side, all_ref[rows_at(index), : 2 * KW], 1, 1)
            acc_ref[...] += dot(
                silu_half(scores).astype(BF16), all_ref[rows_at(index), 2 * KW :], 1, 0
            )

        weights = silu_half(dot(side, all_ref[rows_at(chunk), : 2 * KW], 1, 1))
        weights = jnp.where(causal(False, BLOCK, BLOCK), weights, 0.0).astype(BF16)
        acc_ref[...] += dot(weights, all_ref[rows_at(chunk), 2 * KW :], 1, 0)

    coeff = 1.0 / (valid * BLOCK).astype(F32)
    rows = mixed_refs[0].shape[0]
    for bits in range(H):
        start = pl.multiple_of((mine ^ bits) * rows, rows)
        mixed_refs[bits][...] = (acc_ref[pl.ds(start, rows), :] * coeff).astype(BF16)


def long_back_kernel(blocks_smem, all_ref, g_ref, *refs):
    grad_refs, (dq_ref, dk_ref, dv_ref) = refs[:H], refs[H:]
    mine, chunk, group = run_place()
    valid = blocks_smem[group]
    dq_ref[...] = jnp.zeros_like(dq_ref)
    dk_ref[...] = jnp.zeros_like(dk_ref)
    dv_ref[...] = jnp.zeros_like(dv_ref)

    @pl.when(chunk < valid)
    def _():
        own = rows_at(chunk)
        qk = all_ref[own, : 2 * KW]
        side = score_side(qk)
        values = all_ref[own, 2 * KW :]
        g_own = g_ref[own, :]
        grad_q, grad_k, grad_v = back_block(
            side, qk, qk, values, g_own, causal(True, BLOCK, BLOCK)
        )
        dq_ref[...] = grad_q
        dk_ref[...] = grad_k
        dv_ref[...] = grad_v

        @pl.loop(0, chunk)
        def _(index):
            keys = all_ref[rows_at(index), : 2 * KW]
            act, slope = silu_both(dot(side, keys, 1, 1))
            slopes = dot(g_own, all_ref[rows_at(index), 2 * KW :], 1, 1) * slope
            dq_ref[...] += dot(slopes.astype(BF16), keys, 1, 0)

        @pl.loop(chunk + 1, valid)
        def _(index):
            g_rows = g_ref[rows_at(index), :]
            queries = all_ref[rows_at(index), : 2 * KW]
            act, slope = silu_both(dot(qk, score_side(queries), 1, 1))
            slopes = (dot(values, g_rows, 1, 1) * slope).astype(BF16)
            dk_ref[...] += dot(slopes, queries, 1, 0)
            dv_ref[...] += dot(act.astype(BF16), g_rows, 1, 0)

    coeff = 1.0 / (valid * BLOCK).astype(F32)
    rows = grad_refs[0].shape[0]
    lanes = low_lanes((rows, 2 * KW))
    for bits in range(H):
        part = pl.ds(pl.multiple_of((mine ^ bits) * rows, rows), rows)
        pair = turned(jnp.where(lanes, dk_ref[part, :], dq_ref[part, :])) * HALF_SCALE
        grad_refs[bits][:, : 2 * KW] = (pair * coeff).astype(BF16)
        grad_refs[bits][:, 2 * KW :] = (dv_ref[part, :] * coeff).astype(BF16)


def long_head_kernel(
    got_0,
    got_1,
    got_2,
    got_3,
    x_ref,
    cot_ref,
    pout_ref,
    gate_ref,
    slope_ref,
    out_ref,
    send_ref,
    mid_ref,
    mixed_ref,
):
    mine, _, _ = run_place()
    for bits, got in enumerate((got_0, got_1, got_2, got_3)):
        start = pl.multiple_of((mine ^ bits) * VW, VW)
        mixed_ref[:, pl.ds(start, VW)] = got[...].astype(F32)
    out, gated, grad_gate, grad_mixed = head_out(
        x_ref[...],
        cot_ref[...],
        pout_ref[...],
        gate_ref[...],
        slope_ref[...].astype(F32),
        mixed_ref[...],
    )
    out_ref[...] = out
    cols = gated.shape[1]
    mid_ref[:, :cols] = gated
    mid_ref[:, cols:] = grad_gate
    grad_mixed = grad_mixed.astype(BF16)
    for copy in range(send_ref.shape[0]):
        for which in range(H):
            send_ref[copy, which] = grad_mixed[:, VW * which : VW * (which + 1)]


def early_sums_kernel(
    xbf_ref, cot_ref, mid_ref, half_ref, mid_got, mine_ref, got_ref, sum_ref
):
    cols = mid_ref.shape[1] // 2
    part = sum_ref.shape[0] // 2
    core = lax.rem(lax.axis_index("dp"), 2)
    mid = jnp.concatenate([mid_ref[...], mid_got[...]], axis=0)
    for block, features in split_rows(part, core * part):
        here = slice(block * part, (block + 1) * part)
        for place, own in ((0, cot_ref), (1, xbf_ref)):
            start = (2 * place + block) * part
            rows = jnp.concatenate([own[:, features], half_ref[:, start : start + part]], axis=0)
            there = slice(place * cols, (place + 1) * cols)
            total = mine_ref[here, there].astype(F32) + got_ref[here, there].astype(F32)
            sum_ref[here, there] = (total + dot(rows, mid[:, there], 0, 0)).astype(BF16)


def long_slopes_kernel(got_0, got_1, got_2, got_3, slope_ref, grad_ref):
    mine, _, _ = run_place()
    for bits, got in enumerate((got_0, got_1, got_2, got_3)):
        there = pl.ds(pl.multiple_of((mine ^ bits) * HW, HW), HW)
        grads = got[...].astype(F32) * slope_ref[:, there].astype(F32)
        grad_ref[:, there] = grads.astype(BF16)


def late_sums_kernel(mine_ref, got_ref, xbf_ref, half_ref, grad_ref, grad_got, sum_ref):
    part = sum_ref.shape[0]
    core = lax.rem(lax.axis_index("dp"), 2)
    start = (core + 2 * pl.program_id(0)) * part
    features = pl.ds(pl.multiple_of(start, part), part)
    rows = jnp.concatenate([xbf_ref[:, features], half_ref[...]], axis=0)
    grads = jnp.concatenate([grad_ref[...], grad_got[...]], axis=0)
    total = mine_ref[...].astype(F32) + got_ref[...].astype(F32)
    sum_ref[...] = (total + dot(rows, grads, 0, 0)).astype(BF16)


def final_sums_kernel(factor, early_ref, late_ref, in_ref, out_ref):
    gates = out_ref.shape[1]
    out_ref[...] = early_ref[:, :gates] * factor
    in_ref[:, :gates] = early_ref[:, gates:] * factor
    late = late_ref[0].astype(F32)
    for step in range(1, late_ref.shape[0]):
        late += late_ref[step].astype(F32)
    late = late * factor
    low = low_lanes((late.shape[0], 2 * KW))
    for pair in range(H // 2):
        first = 2 * HW * pair
        even, odd = late[:, first : first + 2 * KW], late[:, first + HW : first + HW + 2 * KW]
        first_q = gates + 2 * KW * pair
        first_k = first_q + H * KW
        first_v = gates + 2 * H * KW + 2 * VW * pair
        in_ref[:, first_q : first_q + 2 * KW] = jnp.where(low, even, turned(odd))
        in_ref[:, first_k : first_k + 2 * KW] = jnp.where(low, turned(even), odd)
        in_ref[:, first_v : first_v + VW] = late[:, first + 2 * KW : first + HW]
        in_ref[:, first_v + VW : first_v + 2 * VW] = late[:, first + HW + 2 * KW : first + 2 * HW]


def input_back_kernel(
    grad_gate_ref,
    grad_ref,
    cot_ref,
    xbf_ref,
    inv_ref,
    pin_ref,
    proj_ref,
    long_gate_ref,
    long_grad_ref,
    long_cot_ref,
    long_xbf_ref,
    long_inv_ref,
    back_ref,
    long_back_ref,
):
    step = pl.program_id(0)

    def finish(gate, grad, cot, normed, inv, target):
        grad_norm = dot(gate[...], pin_ref[...], 1, 1) + dot(grad[...], proj_ref[...], 1, 1)
        back = norm_back(grad_norm, normed.astype(F32), inv[...])
        target[...] = (cot[...].astype(F32) + back).astype(BF16)

    @pl.when(step < 2)
    def _():
        finish(grad_gate_ref, grad_ref, cot_ref, xbf_ref[...], inv_ref, back_ref)

    @pl.when(step == 2)
    def _():
        finish(
            long_gate_ref,
            long_grad_ref,
            long_cot_ref,
            long_xbf_ref[...],
            long_inv_ref,
            long_back_ref,
        )


def shaped(shape, dtype=BF16):
    return jax.ShapeDtypeStruct(shape, dtype)


def in_hbm(shape, dtype=BF16):
    return pltpu.HBM(shape, dtype)


def call(kernel, out_shape, flops, moved, name, vmem=24, **kwargs):
    return pl.pallas_call(
        kernel,
        out_shape=out_shape,
        cost_estimate=pl.CostEstimate(flops=flops, bytes_accessed=moved, transcendentals=0),
        compiler_params=pltpu.CompilerParams(vmem_limit_bytes=vmem * MIB),
        name=name,
        **kwargs,
    )


SMEM = pl.BlockSpec(memory_space=pltpu.SMEM)
WHOLE = pl.BlockSpec(memory_space=pltpu.VMEM)


def rows_spec(rows, cols):
    return pl.BlockSpec((rows, cols), lambda step: (step, 0))


def cols_spec(rows, cols):
    return pl.BlockSpec((rows, cols), lambda step: (0, step))


def fixed_spec(rows, cols):
    return pl.BlockSpec((rows, cols), lambda step: (0, 0))


def swap_heads(pieces):
    size = lax.axis_size("sp")
    return [pieces[0]] + [
        lax.ppermute(pieces[bits], "sp", [(src, src ^ bits) for src in range(size)])
        for bits in range(1, H)
    ]


def spread_heads(sent):
    chunks, heads, rows, cols = sent.shape
    got = lax.all_to_all(sent.reshape(chunks * heads, rows, cols), "sp", 0, 0, tiled=True)
    return got.reshape(chunks * heads * rows, cols)


def swap_cores(half):
    size = lax.axis_size("dp")
    return lax.ppermute(half, "dp", [(src, src ^ 1) for src in range(size)])


def scatter_pairs(partial):
    runs, size = lax.axis_size("dp"), lax.axis_size("sp")
    groups = [
        [run * size + place for run in range(core, runs, 2) for place in range(size)]
        for core in range(2)
    ]
    count = len(groups[0])
    sent = partial.reshape(count, partial.shape[0] // count, partial.shape[1])
    return lax.all_to_all(sent, ("dp", "sp"), 0, 0, tiled=True, axis_index_groups=groups)


def body(x_long, x_short, long_blocks, short_user, proj_in, proj_out, cot_long, cot_short):
    sp_size = lax.axis_size("sp")
    long_rows, width = x_long.shape
    short_rows = x_short.shape[0]
    gates = proj_out.shape[0]
    cols = proj_in.shape[1]
    rest = cols - gates
    half = width // 2
    chunks = sp_size // H

    proj, sent, inv_long, xbf_long, slope_rest = call(
        long_project_kernel,
        (
            in_hbm((width, rest)),
            in_hbm((chunks, H, long_rows, HW)),
            in_hbm((long_rows, 1), F32),
            in_hbm((long_rows, width)),
            in_hbm((long_rows, rest)),
        ),
        2 * long_rows * width * rest,
        8 * 2**20,
        "long_project",
        vmem=60,
        grid=(2,),
        in_specs=[
            fixed_spec(long_rows, width),
            pl.BlockSpec((width, 2 * KW), lambda step: (0, step + gates // (2 * KW))),
            pl.BlockSpec((width, 2 * KW), lambda step: (0, step + (gates + H * KW) // (2 * KW))),
            pl.BlockSpec((width, 2 * VW), lambda step: (0, step + (gates + 2 * H * KW) // (2 * VW))),
        ],
        out_specs=[
            cols_spec(width, rest // 2),
            pl.BlockSpec((chunks, 2, long_rows, HW), lambda step: (0, step, 0, 0)),
            fixed_spec(long_rows, 1),
            fixed_spec(long_rows, width),
            cols_spec(long_rows, rest // 2),
        ],
    )(x_long, proj_in, proj_in, proj_in)
    whole = spread_heads(sent)
    gate_long, slope_long, half_other = call(
        long_gate_kernel,
        (
            shaped((long_rows, gates)),
            shaped((long_rows, gates)),
            in_hbm((long_rows, width)),
        ),
        2 * long_rows * width * gates,
        4 * 2**20,
        "long_gate",
        vmem=60,
        grid=(1,),
        in_specs=[
            fixed_spec(long_rows, width),
            fixed_spec(width, gates),
            fixed_spec(long_rows, width),
        ],
        out_specs=[
            fixed_spec(long_rows, gates),
            fixed_spec(long_rows, gates),
            fixed_spec(long_rows, width),
        ],
    )(xbf_long, proj_in, cot_long)

    short_out = call(
        short_forward_kernel,
        (
            in_hbm((short_rows, width)),
            in_hbm((short_rows, rest)),
            in_hbm((short_rows, gates)),
            in_hbm((short_rows, gates)),
            in_hbm((short_rows, rest)),
            in_hbm((short_rows, width)),
            in_hbm((width, short_rows)),
            in_hbm((short_rows, 1), F32),
            in_hbm((half, 2 * gates)),
            in_hbm((half, 2 * gates)),
            in_hbm((short_rows, rest)),
        ),
        20 * 10**9,
        24 * 2**20,
        "short_forward",
        vmem=56,
        grid=(short_rows // BLOCK,),
        in_specs=[
            SMEM,
            rows_spec(BLOCK, width),
            rows_spec(BLOCK, width),
            fixed_spec(width, gates),
            fixed_spec(width, rest),
            fixed_spec(gates, width),
        ],
        out_specs=[
            rows_spec(BLOCK, width),
            rows_spec(BLOCK, rest),
            rows_spec(BLOCK, gates),
            rows_spec(BLOCK, gates),
            rows_spec(BLOCK, rest),
            rows_spec(BLOCK, width),
            cols_spec(width, BLOCK),
            rows_spec(BLOCK, 1),
            fixed_spec(half, 2 * gates),
            fixed_spec(half, 2 * gates),
            fixed_spec(short_rows, rest),
        ],
        scratch_shapes=[
            pltpu.VMEM((width, 2 * gates), F32),
            pltpu.VMEM((BLOCK, rest), BF16),
            pltpu.VMEM((BLOCK, gates), F32),
            pltpu.VMEM((BLOCK, 2 * KW * H), BF16),
        ],
    )(short_user, x_short, cot_short, proj_in, proj, proj_out)
    out_short, qkv_short, g_short, gate_short, slope_short, xbf_short = short_out[:6]
    turned_short, inv_short, early_mine, early_other, join_short = short_out[6:]

    whole, out_short = lax.optimization_barrier((whole, out_short))
    mixed = call(
        long_attend_kernel,
        (shaped((long_rows, VW)),) * H,
        2 * 10**9,
        2 * 2**20,
        "long_attend",
        vmem=62,
        in_specs=[SMEM, WHOLE],
        scratch_shapes=[
            pltpu.VMEM((BLOCK, VW), F32),
        ],
    )(long_blocks, whole)
    out_long, sent, mid = call(
        long_head_kernel,
        (
            shaped((long_rows, width)),
            in_hbm((chunks, H, long_rows, VW)),
            in_hbm((long_rows, 2 * gates)),
        ),
        4 * long_rows * width * gates,
        3 * 2**20,
        "long_head",
        vmem=60,
        in_specs=[WHOLE] * 9,
        scratch_shapes=[pltpu.VMEM((long_rows, gates), F32)],
    )(*swap_heads(mixed), x_long, cot_long, proj_out, gate_long, slope_long)
    sent, qkv_short, mid, half_other, early_other = lax.optimization_barrier(
        (sent, qkv_short, mid, half_other, early_other)
    )
    all_g = spread_heads(sent)
    half_got = swap_cores(half_other)
    early_got = swap_cores(early_other)
    mid_got = swap_cores(mid)
    grad_short, short_mine, short_other = call(
        short_back_kernel,
        (in_hbm((short_rows, rest)), in_hbm((half, rest)), in_hbm((half, rest))),
        16 * 10**9,
        13 * 2**20,
        "short_back",
        vmem=58,
        grid=(2,),
        in_specs=[
            SMEM,
            cols_spec(short_rows, rest // 2),
            cols_spec(short_rows, gates // 2),
            cols_spec(short_rows, rest // 2),
            fixed_spec(width, short_rows),
            cols_spec(short_rows, rest // 2),
        ],
        out_specs=[
            cols_spec(short_rows, rest // 2),
            cols_spec(half, rest // 2),
            cols_spec(half, rest // 2),
        ],
        scratch_shapes=[
            pltpu.VMEM((short_rows, rest // 2), F32),
        ],
    )(short_user, qkv_short, g_short, slope_short, turned_short, join_short)
    mid_got, half_got, early_got, grad_short = lax.optimization_barrier(
        (mid_got, half_got, early_got, grad_short)
    )
    short_got = swap_cores(short_other)
    early = call(
        early_sums_kernel,
        in_hbm((half, 2 * gates)),
        8 * long_rows * half * gates,
        5 * 2**20,
        "early_sums",
    )(xbf_long, cot_long, mid, half_got, mid_got, early_mine, early_got)
    all_g, early = lax.optimization_barrier((all_g, early))
    early = scatter_pairs(early)

    grads = call(
        long_back_kernel,
        (shaped((long_rows, HW)),) * H,
        6 * 10**9,
        4 * 2**20,
        "long_back",
        vmem=62,
        in_specs=[SMEM, WHOLE, WHOLE],
        scratch_shapes=[
            pltpu.VMEM((BLOCK, 2 * KW), F32),
            pltpu.VMEM((BLOCK, 2 * KW), F32),
            pltpu.VMEM((BLOCK, VW), F32),
        ],
    )(long_blocks, whole, all_g)
    grad_long = call(
        long_slopes_kernel,
        shaped((long_rows, rest)),
        long_rows * rest,
        2**20,
        "long_slopes",
    )(*swap_heads(grads), slope_rest)
    late = call(
        late_sums_kernel,
        in_hbm((half, rest)),
        4 * long_rows * half * rest,
        5 * 2**20,
        "late_sums",
        grid=(2,),
        in_specs=[
            rows_spec(half // 2, rest),
            rows_spec(half // 2, rest),
            fixed_spec(long_rows, width),
            pl.BlockSpec((long_rows, half // 2), lambda step: (0, step + 2)),
            fixed_spec(long_rows, rest),
            fixed_spec(long_rows, rest),
        ],
        out_specs=rows_spec(half // 2, rest),
    )(short_mine, short_got, xbf_long, half_got, grad_long, swap_cores(grad_long))
    late, gate_short = lax.optimization_barrier((late, gate_short))
    late = scatter_pairs(late)

    def short_rows_spec(cols):
        return pl.BlockSpec((BLOCK, cols), lambda step: (jnp.minimum(step, 1), 0))

    back_short, back_long = call(
        input_back_kernel,
        (in_hbm((short_rows, width)), in_hbm((long_rows, width))),
        2 * (short_rows + long_rows) * width * cols,
        14 * 2**20,
        "input_back",
        vmem=60,
        grid=(short_rows // BLOCK + 1,),
        in_specs=[
            short_rows_spec(gates),
            short_rows_spec(rest),
            short_rows_spec(width),
            short_rows_spec(width),
            short_rows_spec(1),
            fixed_spec(width, gates),
            fixed_spec(width, rest),
        ]
        + [
            pl.BlockSpec((long_rows, gates), lambda step: (0, 1)),
            fixed_spec(long_rows, rest),
            fixed_spec(long_rows, width),
            fixed_spec(long_rows, width),
            fixed_spec(long_rows, 1),
        ],
        out_specs=[short_rows_spec(width), fixed_spec(long_rows, width)],
    )(
        gate_short,
        grad_short,
        cot_short,
        xbf_short,
        inv_short,
        proj_in,
        proj,
        mid,
        grad_long,
        cot_long,
        xbf_long,
        inv_long,
    )
    total_rows = lax.axis_size("dp") * sp_size * (long_rows + short_rows)
    early = jnp.sum(early.astype(F32), axis=0)
    sum_in, sum_out = call(
        functools.partial(final_sums_kernel, float(total_rows) ** (-0.5)),
        (shaped((early.shape[0], cols), F32), shaped((early.shape[0], gates), F32)),
        128 * 2**10,
        2**20,
        "final_sums",
    )(early, late)
    return (out_long, out_short, back_long, back_short, sum_in, sum_out)


def solution(mesh):
    rows = P(("dp", "sp"), None)
    return jax.shard_map(
        body,
        mesh=mesh,
        in_specs=(rows, rows, P(), rows, P(), P(), rows, rows),
        out_specs=(rows,) * 6,
        check_vma=False,
    )
```

```python
import functools

import jax
import jax.numpy as jnp
from jax import lax
from jax.experimental import pallas as pl
from jax.experimental.pallas import tpu as pltpu
from jax.sharding import PartitionSpec as P

H = 4
BLOCK = 512
KW = 64
VW = 128
HW = 2 * KW + VW
EPS = 1e-05
HALF_SCALE = 0.5 * KW**-0.5
F32 = jnp.float32
BF16 = jnp.bfloat16
MIB = 1024 * 1024


def dot(first, second, first_dim, second_dim):
    return lax.dot_general(
        first, second, (((first_dim,), (second_dim,)), ((), ())), preferred_element_type=F32
    )


def norm_rows(rows):
    center = rows - jnp.mean(rows, axis=-1, keepdims=True)
    inv_root = lax.rsqrt(jnp.mean(center * center, axis=-1, keepdims=True) + EPS)
    return center * inv_root, inv_root


def norm_back(upstream, normed, inv_root):
    return inv_root * (
        upstream
        - jnp.mean(upstream, axis=-1, keepdims=True)
        - normed * jnp.mean(upstream * normed, axis=-1, keepdims=True)
    )


def silu_half(half):
    return half * (1.0 + jnp.tanh(half))


def silu_both(half):
    curve = jnp.tanh(half)
    above = 1.0 + curve
    act = half * above
    return act, above + act * (1.0 - curve)


def low_lanes(shape):
    return lax.broadcasted_iota(jnp.int32, shape, 1) < KW


def turned(pair):
    return pltpu.roll(pair.astype(F32), KW, 1)


def score_side(qk):
    return jnp.where(low_lanes(qk.shape), 0.0, turned(qk) * HALF_SCALE).astype(BF16)


def causal(keys_first, keys, queries, key_start=0, query_start=0):
    shape = (keys, queries) if keys_first else (queries, keys)
    key_pos = key_start + lax.broadcasted_iota(jnp.int32, shape, 0 if keys_first else 1)
    query_pos = query_start + lax.broadcasted_iota(jnp.int32, shape, 1 if keys_first else 0)
    return key_pos <= query_pos


def project(x_bf, proj):
    act, slope = silu_both(0.5 * dot(x_bf, proj, 1, 0))
    return act.astype(BF16), 0.5 * slope


def head_out(x_rows, cot, proj_out, gate_u, slope_gate, mixed):
    mixed_n, inv_mix = norm_rows(mixed)
    gate_f = gate_u.astype(F32)
    gated = (mixed_n * gate_f).astype(BF16)
    out = (x_rows.astype(F32) + dot(gated, proj_out, 1, 0)).astype(BF16)
    grad_g = dot(cot, proj_out, 1, 1)
    grad_mixed = norm_back(grad_g * gate_f, mixed_n, inv_mix)
    grad_gate = (grad_g * mixed_n * slope_gate).astype(BF16)
    return out, gated, grad_gate, grad_mixed


def run_place():
    index = lax.axis_index("sp")
    return lax.rem(index, H), lax.div(index, H), lax.axis_index("dp")


def split_rows(part, start):
    for block in range(2):
        yield block, pl.ds(pl.multiple_of(start + 2 * part * block, part), part)


def long_project_kernel(
    x_ref, pin_q_ref, pin_k_ref, pin_v_ref, proj_ref, send_ref, inv_ref, xbf_ref, slope_ref
):
    @pl.when(pl.program_id(0) == 0)
    def _():
        normed, inv_std = norm_rows(x_ref[...].astype(F32))
        xbf_ref[...] = normed.astype(BF16)
        inv_ref[...] = inv_std

    q_pair, k_pair = pin_q_ref[...], pin_k_ref[...]
    low = low_lanes(q_pair.shape)
    even = jnp.where(low, q_pair.astype(F32), turned(k_pair)).astype(BF16)
    odd = jnp.where(low, turned(q_pair), k_pair.astype(F32)).astype(BF16)
    proj = jnp.concatenate([even, pin_v_ref[:, :VW], odd, pin_v_ref[:, VW:]], axis=1)
    proj_ref[...] = proj
    act, slope = project(xbf_ref[...], proj)
    slope_ref[...] = slope.astype(BF16)
    for copy in range(send_ref.shape[0]):
        for which in range(2):
            send_ref[copy, which] = act[:, HW * which : HW * (which + 1)]


def long_gate_kernel(xbf_ref, pin_ref, cot_ref, gate_ref, slope_gate_ref, half_ref):
    _, _, group = run_place()
    part = xbf_ref.shape[1] // 4
    act, slope = project(xbf_ref[...], pin_ref[...])
    gate_ref[...] = act
    slope_gate_ref[...] = slope.astype(BF16)
    for block, features in split_rows(part, (1 - lax.rem(group, 2)) * part):
        half_ref[:, block * part : (block + 1) * part] = cot_ref[:, features]
        half_ref[:, (block + 2) * part : (block + 3) * part] = xbf_ref[:, features]


def head_lanes(which):
    first = pl.multiple_of(which * HW, HW)
    last = pl.multiple_of(which * HW + 2 * KW, VW)
    return pl.ds(first, 2 * KW), pl.ds(last, VW), pl.ds(pl.multiple_of(which * VW, VW), VW)


def back_block(query_side, query_qk, key_qk, values, g_rows, mask):
    act, slope = silu_both(dot(key_qk, query_side, 1, 1))
    slopes = dot(values, g_rows, 1, 1) * slope
    if mask is not None:
        act = jnp.where(mask, act, 0.0)
        slopes = jnp.where(mask, slopes, 0.0)
    slopes = slopes.astype(BF16)
    grad_q = dot(slopes, key_qk, 0, 0)
    grad_k = dot(slopes, query_qk, 1, 0)
    grad_v = dot(act.astype(BF16), g_rows, 1, 0)
    return grad_q, grad_k, grad_v


def short_forward_kernel(
    user_ref,
    x_ref,
    cot_ref,
    pin_ref,
    proj_ref,
    pout_ref,
    out_ref,
    qkv_ref,
    g_ref,
    grad_gate_ref,
    slope_ref,
    xbf_ref,
    turned_ref,
    inv_ref,
    mine_ref,
    other_ref,
    join_ref,
    sum_ref,
    seen_ref,
    mixed_ref,
    side_ref,
):
    step = pl.program_id(0)
    joined = user_ref[0, 0] == user_ref[0, 1]
    share = jnp.where(joined, 0.5 / BLOCK, 1.0 / BLOCK)
    normed, inv_std = norm_rows(x_ref[...].astype(F32))
    x_bf = normed.astype(BF16)
    xbf_ref[...] = x_bf
    turned_ref[...] = x_bf.T
    inv_ref[...] = inv_std
    act, slope = project(x_bf, proj_ref[...])
    slope_ref[...] = slope.astype(BF16)
    qkv_ref[...] = act
    gate_u, slope_gate = project(x_bf, pin_ref[...])
    half = BLOCK // 2
    for which in range(H):
        qk = act[:, HW * which : HW * which + 2 * KW]
        values = act[:, HW * which + 2 * KW : HW * (which + 1)]
        side = score_side(qk)
        scores = dot(side, qk[:half], 1, 1)
        weights = jnp.where(causal(False, half, BLOCK), silu_half(scores), 0.0).astype(BF16)
        mixed = dot(weights, values[:half], 1, 0)
        scores = dot(side[half:], qk[half:], 1, 1)
        weights = jnp.where(causal(False, half, half), silu_half(scores), 0.0).astype(BF16)
        lower = mixed[half:] + dot(weights, values[half:], 1, 0)
        mixed_ref[:half, VW * which : VW * (which + 1)] = mixed[:half]
        mixed_ref[half:, VW * which : VW * (which + 1)] = lower

        side_ref[:, 2 * KW * which : 2 * KW * (which + 1)] = side

    @pl.when(jnp.logical_and(step == 1, joined))
    def _():
        @pl.loop(0, H)
        def _(which):
            pair, rest, narrow = head_lanes(which)
            scores = dot(side_ref[:, narrow], seen_ref[:, pair], 1, 1)
            weights = silu_half(scores).astype(BF16)
            mixed_ref[:, narrow] += dot(weights, seen_ref[:, rest], 1, 0)

    @pl.when(step == 0)
    def _():
        seen_ref[...] = act

    out, gated, grad_gate, grad_mixed = head_out(
        x_ref[...],
        cot_ref[...],
        pout_ref[...],
        gate_u,
        slope_gate,
        mixed_ref[...] * share,
    )
    out_ref[...] = out
    grad_gate_ref[...] = grad_gate
    g_ref[...] = (grad_mixed.astype(BF16).astype(F32) * share).astype(BF16)
    gates = gated.shape[1]

    @pl.when(jnp.logical_and(step == 1, joined))
    def _():
        lanes = low_lanes((BLOCK, 2 * KW))

        @pl.loop(0, H // 2)
        def _(two):
            for which in (2 * two, 2 * two + 1):
                pair, rest, narrow = head_lanes(which)
                grad_q, grad_k, grad_v = back_block(
                    side_ref[:, narrow],
                    qkv_ref[:, pair],
                    seen_ref[:, pair],
                    seen_ref[:, rest],
                    g_ref[:, narrow],
                    None,
                )
                join_ref[:BLOCK, pair] = jnp.where(lanes, grad_k, 0.0).astype(BF16)
                join_ref[:BLOCK, rest] = grad_v.astype(BF16)
                join_ref[BLOCK:, pair] = jnp.where(lanes, 0.0, grad_q).astype(BF16)
                join_ref[BLOCK:, rest] = jnp.zeros(grad_v.shape, BF16)

    @pl.when(step == 0)
    def _():
        sum_ref[:, :gates] = dot(cot_ref[...], gated, 0, 0)
        sum_ref[:, gates:] = dot(turned_ref[...], grad_gate_ref[...], 1, 0)

    @pl.when(step == 1)
    def _():
        part = mine_ref.shape[0] // 2
        core = lax.rem(lax.axis_index("dp"), 2)
        for target, side in ((mine_ref, core), (other_ref, 1 - core)):
            for block, features in split_rows(part, side * part):
                here = slice(block * part, (block + 1) * part)
                total = sum_ref[features, :gates] + dot(cot_ref[:, features], gated, 0, 0)
                target[here, :gates] = total.astype(BF16)
                total = dot(turned_ref[features, :], grad_gate_ref[...], 1, 0)
                target[here, gates:] = (sum_ref[features, gates:] + total).astype(BF16)


def short_back_kernel(
    user_ref, qkv_ref, g_ref, slope_ref, turned_ref, join_ref, grad_ref, mine_ref, other_ref, acc_ref
):
    joined = user_ref[0, 0] == user_ref[0, 1]
    half = BLOCK // 2
    heads = range(qkv_ref.shape[1] // HW)
    for which in heads:
        first = HW * which
        qk = qkv_ref[:, first : first + 2 * KW]
        side = score_side(qk)
        values = qkv_ref[:, first + 2 * KW : first + HW]
        g_rows = g_ref[:, VW * which : VW * (which + 1)]
        lanes = low_lanes((half, 2 * KW))
        for block in range(qkv_ref.shape[0] // BLOCK):
            top = slice(block * BLOCK, block * BLOCK + half)
            end = slice(block * BLOCK + half, (block + 1) * BLOCK)
            both = slice(block * BLOCK, (block + 1) * BLOCK)
            dq_one, dk_one, dv_one = back_block(
                side[both], qk[both], qk[top], values[top], g_rows[both], causal(True, half, BLOCK)
            )
            dq_two, dk_two, dv_two = back_block(
                side[end], qk[end], qk[end], values[end], g_rows[end], causal(True, half, half)
            )
            acc_ref[top, first : first + 2 * KW] = jnp.where(lanes, dk_one, dq_one[:half])
            acc_ref[end, first : first + 2 * KW] = jnp.where(lanes, dk_two, dq_one[half:] + dq_two)
            acc_ref[top, first + 2 * KW : first + HW] = dv_one
            acc_ref[end, first + 2 * KW : first + HW] = dv_two

    @pl.when(joined)
    def _():
        acc_ref[...] += join_ref[...].astype(F32)

    for which in heads:
        first = HW * which
        pair, rest = slice(first, first + 2 * KW), slice(first + 2 * KW, first + HW)
        grads = turned(acc_ref[:, pair]) * HALF_SCALE
        grad_ref[:, pair] = (grads * slope_ref[:, pair].astype(F32)).astype(BF16)
        grad_ref[:, rest] = (acc_ref[:, rest] * slope_ref[:, rest].astype(F32)).astype(BF16)
    grad_pre = grad_ref[...]
    part = mine_ref.shape[0] // 2
    core = lax.rem(lax.axis_index("dp"), 2)
    for target, side in ((mine_ref, core), (other_ref, 1 - core)):
        for block, features in split_rows(part, side * part):
            total = dot(turned_ref[features, :], grad_pre, 1, 0)
            target[block * part : (block + 1) * part] = total.astype(BF16)


def rows_at(index):
    return pl.ds(pl.multiple_of(index * BLOCK, BLOCK), BLOCK)


def long_attend_kernel(blocks_smem, all_hbm, *refs):
    mixed_refs, (acc_ref, all_ref, sems) = refs[:H], refs[H:]
    mine, chunk, group = run_place()
    valid = blocks_smem[group]

    def block_copy(index):
        rows = rows_at(index)
        return pltpu.make_async_copy(all_hbm.at[rows], all_ref.at[rows], sems.at[index])

    block_copy(chunk).start()

    @pl.loop(0, chunk)
    def _(index):
        block_copy(index).start()

    acc_ref[...] = jnp.zeros_like(acc_ref)
    block_copy(chunk).wait()

    @pl.when(chunk >= valid)
    def _():
        @pl.loop(0, chunk)
        def _(index):
            block_copy(index).wait()

    @pl.when(chunk < valid)
    def _():
        side = score_side(all_ref[rows_at(chunk), : 2 * KW])

        @pl.loop(0, chunk)
        def _(index):
            block_copy(index).wait()
            scores = dot(side, all_ref[rows_at(index), : 2 * KW], 1, 1)
            acc_ref[...] += dot(
                silu_half(scores).astype(BF16), all_ref[rows_at(index), 2 * KW :], 1, 0
            )

        weights = silu_half(dot(side, all_ref[rows_at(chunk), : 2 * KW], 1, 1))
        weights = jnp.where(causal(False, BLOCK, BLOCK), weights, 0.0).astype(BF16)
        acc_ref[...] += dot(weights, all_ref[rows_at(chunk), 2 * KW :], 1, 0)

    coeff = 1.0 / (valid * BLOCK).astype(F32)
    rows = mixed_refs[0].shape[0]
    for bits in range(H):
        start = pl.multiple_of((mine ^ bits) * rows, rows)
        mixed_refs[bits][...] = (acc_ref[pl.ds(start, rows), :] * coeff).astype(BF16)


def long_back_kernel(blocks_smem, all_ref, g_ref, *refs):
    grad_refs, (dq_ref, dk_ref, dv_ref) = refs[:H], refs[H:]
    mine, chunk, group = run_place()
    valid = blocks_smem[group]
    dq_ref[...] = jnp.zeros_like(dq_ref)
    dk_ref[...] = jnp.zeros_like(dk_ref)
    dv_ref[...] = jnp.zeros_like(dv_ref)

    @pl.when(chunk < valid)
    def _():
        own = rows_at(chunk)
        qk = all_ref[own, : 2 * KW]
        side = score_side(qk)
        values = all_ref[own, 2 * KW :]
        g_own = g_ref[own, :]
        grad_q, grad_k, grad_v = back_block(
            side, qk, qk, values, g_own, causal(True, BLOCK, BLOCK)
        )
        dq_ref[...] = grad_q
        dk_ref[...] = grad_k
        dv_ref[...] = grad_v

        @pl.loop(0, chunk)
        def _(index):
            keys = all_ref[rows_at(index), : 2 * KW]
            act, slope = silu_both(dot(side, keys, 1, 1))
            slopes = dot(g_own, all_ref[rows_at(index), 2 * KW :], 1, 1) * slope
            dq_ref[...] += dot(slopes.astype(BF16), keys, 1, 0)

        @pl.loop(chunk + 1, valid)
        def _(index):
            g_rows = g_ref[rows_at(index), :]
            queries = all_ref[rows_at(index), : 2 * KW]
            act, slope = silu_both(dot(qk, score_side(queries), 1, 1))
            slopes = (dot(values, g_rows, 1, 1) * slope).astype(BF16)
            dk_ref[...] += dot(slopes, queries, 1, 0)
            dv_ref[...] += dot(act.astype(BF16), g_rows, 1, 0)

    coeff = 1.0 / (valid * BLOCK).astype(F32)
    rows = grad_refs[0].shape[0]
    lanes = low_lanes((rows, 2 * KW))
    for bits in range(H):
        part = pl.ds(pl.multiple_of((mine ^ bits) * rows, rows), rows)
        pair = turned(jnp.where(lanes, dk_ref[part, :], dq_ref[part, :])) * HALF_SCALE
        grad_refs[bits][:, : 2 * KW] = (pair * coeff).astype(BF16)
        grad_refs[bits][:, 2 * KW :] = (dv_ref[part, :] * coeff).astype(BF16)


def long_head_kernel(
    got_0,
    got_1,
    got_2,
    got_3,
    x_ref,
    cot_ref,
    pout_ref,
    gate_ref,
    slope_ref,
    out_ref,
    send_ref,
    mid_ref,
    mixed_ref,
):
    mine, _, _ = run_place()
    for bits, got in enumerate((got_0, got_1, got_2, got_3)):
        start = pl.multiple_of((mine ^ bits) * VW, VW)
        mixed_ref[:, pl.ds(start, VW)] = got[...].astype(F32)
    out, gated, grad_gate, grad_mixed = head_out(
        x_ref[...],
        cot_ref[...],
        pout_ref[...],
        gate_ref[...],
        slope_ref[...].astype(F32),
        mixed_ref[...],
    )
    out_ref[...] = out
    cols = gated.shape[1]
    mid_ref[:, :cols] = gated
    mid_ref[:, cols:] = grad_gate
    grad_mixed = grad_mixed.astype(BF16)
    for copy in range(send_ref.shape[0]):
        for which in range(H):
            send_ref[copy, which] = grad_mixed[:, VW * which : VW * (which + 1)]


def early_sums_kernel(
    xbf_ref, cot_ref, mid_ref, half_ref, mid_got, mine_ref, got_ref, sum_ref
):
    cols = mid_ref.shape[1] // 2
    part = sum_ref.shape[0] // 2
    core = lax.rem(lax.axis_index("dp"), 2)
    mid = jnp.concatenate([mid_ref[...], mid_got[...]], axis=0)
    for block, features in split_rows(part, core * part):
        here = slice(block * part, (block + 1) * part)
        for place, own in ((0, cot_ref), (1, xbf_ref)):
            start = (2 * place + block) * part
            rows = jnp.concatenate([own[:, features], half_ref[:, start : start + part]], axis=0)
            there = slice(place * cols, (place + 1) * cols)
            total = mine_ref[here, there].astype(F32) + got_ref[here, there].astype(F32)
            sum_ref[here, there] = (total + dot(rows, mid[:, there], 0, 0)).astype(BF16)


def long_slopes_kernel(got_0, got_1, got_2, got_3, slope_ref, grad_ref):
    mine, _, _ = run_place()
    for bits, got in enumerate((got_0, got_1, got_2, got_3)):
        there = pl.ds(pl.multiple_of((mine ^ bits) * HW, HW), HW)
        grads = got[...].astype(F32) * slope_ref[:, there].astype(F32)
        grad_ref[:, there] = grads.astype(BF16)


def late_sums_kernel(mine_ref, got_ref, xbf_ref, half_ref, grad_ref, grad_got, sum_ref):
    part = sum_ref.shape[0]
    core = lax.rem(lax.axis_index("dp"), 2)
    start = (core + 2 * pl.program_id(0)) * part
    features = pl.ds(pl.multiple_of(start, part), part)
    rows = jnp.concatenate([xbf_ref[:, features], half_ref[...]], axis=0)
    grads = jnp.concatenate([grad_ref[...], grad_got[...]], axis=0)
    total = mine_ref[...].astype(F32) + got_ref[...].astype(F32)
    sum_ref[...] = (total + dot(rows, grads, 0, 0)).astype(BF16)


def final_sums_kernel(factor, early_ref, late_ref, in_ref, out_ref):
    gates = out_ref.shape[1]
    out_ref[...] = early_ref[:, :gates] * factor
    in_ref[:, :gates] = early_ref[:, gates:] * factor
    late = late_ref[0].astype(F32)
    for step in range(1, late_ref.shape[0]):
        late += late_ref[step].astype(F32)
    late = late * factor
    low = low_lanes((late.shape[0], 2 * KW))
    for pair in range(H // 2):
        first = 2 * HW * pair
        even, odd = late[:, first : first + 2 * KW], late[:, first + HW : first + HW + 2 * KW]
        first_q = gates + 2 * KW * pair
        first_k = first_q + H * KW
        first_v = gates + 2 * H * KW + 2 * VW * pair
        in_ref[:, first_q : first_q + 2 * KW] = jnp.where(low, even, turned(odd))
        in_ref[:, first_k : first_k + 2 * KW] = jnp.where(low, turned(even), odd)
        in_ref[:, first_v : first_v + VW] = late[:, first + 2 * KW : first + HW]
        in_ref[:, first_v + VW : first_v + 2 * VW] = late[:, first + HW + 2 * KW : first + 2 * HW]


def input_back_kernel(
    grad_gate_ref,
    grad_ref,
    cot_ref,
    xbf_ref,
    inv_ref,
    pin_ref,
    proj_ref,
    long_gate_ref,
    long_grad_ref,
    long_cot_ref,
    long_xbf_ref,
    long_inv_ref,
    back_ref,
    long_back_ref,
):
    step = pl.program_id(0)

    def finish(gate, grad, cot, normed, inv, target):
        grad_norm = dot(gate[...], pin_ref[...], 1, 1) + dot(grad[...], proj_ref[...], 1, 1)
        back = norm_back(grad_norm, normed.astype(F32), inv[...])
        target[...] = (cot[...].astype(F32) + back).astype(BF16)

    @pl.when(step < 2)
    def _():
        finish(grad_gate_ref, grad_ref, cot_ref, xbf_ref[...], inv_ref, back_ref)

    @pl.when(step == 2)
    def _():
        finish(
            long_gate_ref,
            long_grad_ref,
            long_cot_ref,
            long_xbf_ref[...],
            long_inv_ref,
            long_back_ref,
        )


def shaped(shape, dtype=BF16):
    return jax.ShapeDtypeStruct(shape, dtype)


def in_hbm(shape, dtype=BF16):
    return pltpu.HBM(shape, dtype)


def call(kernel, out_shape, flops, moved, name, vmem=24, **kwargs):
    return pl.pallas_call(
        kernel,
        out_shape=out_shape,
        cost_estimate=pl.CostEstimate(flops=flops, bytes_accessed=moved, transcendentals=0),
        compiler_params=pltpu.CompilerParams(vmem_limit_bytes=vmem * MIB),
        name=name,
        **kwargs,
    )


SMEM = pl.BlockSpec(memory_space=pltpu.SMEM)
WHOLE = pl.BlockSpec(memory_space=pltpu.VMEM)


def rows_spec(rows, cols):
    return pl.BlockSpec((rows, cols), lambda step: (step, 0))


def cols_spec(rows, cols):
    return pl.BlockSpec((rows, cols), lambda step: (0, step))


def fixed_spec(rows, cols):
    return pl.BlockSpec((rows, cols), lambda step: (0, 0))


def swap_heads(pieces):
    size = lax.axis_size("sp")
    return [pieces[0]] + [
        lax.ppermute(pieces[bits], "sp", [(src, src ^ bits) for src in range(size)])
        for bits in range(1, H)
    ]


def spread_heads(sent):
    chunks, heads, rows, cols = sent.shape
    got = lax.all_to_all(sent.reshape(chunks * heads, rows, cols), "sp", 0, 0, tiled=True)
    return got.reshape(chunks * heads * rows, cols)


def swap_cores(half):
    size = lax.axis_size("dp")
    return lax.ppermute(half, "dp", [(src, src ^ 1) for src in range(size)])


def scatter_pairs(partial):
    runs, size = lax.axis_size("dp"), lax.axis_size("sp")
    groups = [
        [run * size + place for run in range(core, runs, 2) for place in range(size)]
        for core in range(2)
    ]
    count = len(groups[0])
    sent = partial.reshape(count, partial.shape[0] // count, partial.shape[1])
    return lax.all_to_all(sent, ("dp", "sp"), 0, 0, tiled=True, axis_index_groups=groups)


def body(x_long, x_short, long_blocks, short_user, proj_in, proj_out, cot_long, cot_short):
    sp_size = lax.axis_size("sp")
    long_rows, width = x_long.shape
    short_rows = x_short.shape[0]
    gates = proj_out.shape[0]
    cols = proj_in.shape[1]
    rest = cols - gates
    half = width // 2
    chunks = sp_size // H

    proj, sent, inv_long, xbf_long, slope_rest = call(
        long_project_kernel,
        (
            in_hbm((width, rest)),
            in_hbm((chunks, H, long_rows, HW)),
            in_hbm((long_rows, 1), F32),
            in_hbm((long_rows, width)),
            in_hbm((long_rows, rest)),
        ),
        2 * long_rows * width * rest,
        8 * 2**20,
        "long_project",
        vmem=60,
        grid=(2,),
        in_specs=[
            fixed_spec(long_rows, width),
            pl.BlockSpec((width, 2 * KW), lambda step: (0, step + gates // (2 * KW))),
            pl.BlockSpec((width, 2 * KW), lambda step: (0, step + (gates + H * KW) // (2 * KW))),
            pl.BlockSpec((width, 2 * VW), lambda step: (0, step + (gates + 2 * H * KW) // (2 * VW))),
        ],
        out_specs=[
            cols_spec(width, rest // 2),
            pl.BlockSpec((chunks, 2, long_rows, HW), lambda step: (0, step, 0, 0)),
            fixed_spec(long_rows, 1),
            fixed_spec(long_rows, width),
            cols_spec(long_rows, rest // 2),
        ],
    )(x_long, proj_in, proj_in, proj_in)
    whole = spread_heads(sent)
    gate_long, slope_long, half_other = call(
        long_gate_kernel,
        (
            shaped((long_rows, gates)),
            shaped((long_rows, gates)),
            in_hbm((long_rows, width)),
        ),
        2 * long_rows * width * gates,
        4 * 2**20,
        "long_gate",
        grid=(1,),
        in_specs=[
            fixed_spec(long_rows, width),
            fixed_spec(width, gates),
            fixed_spec(long_rows, width),
        ],
        out_specs=[
            fixed_spec(long_rows, gates),
            fixed_spec(long_rows, gates),
            fixed_spec(long_rows, width),
        ],
    )(xbf_long, proj_in, cot_long)

    short_out = call(
        short_forward_kernel,
        (
            in_hbm((short_rows, width)),
            in_hbm((short_rows, rest)),
            in_hbm((short_rows, gates)),
            in_hbm((short_rows, gates)),
            in_hbm((short_rows, rest)),
            in_hbm((short_rows, width)),
            in_hbm((width, short_rows)),
            in_hbm((short_rows, 1), F32),
            in_hbm((half, 2 * gates)),
            in_hbm((half, 2 * gates)),
            in_hbm((short_rows, rest)),
        ),
        20 * 10**9,
        24 * 2**20,
        "short_forward",
        vmem=56,
        grid=(short_rows // BLOCK,),
        in_specs=[
            SMEM,
            rows_spec(BLOCK, width),
            rows_spec(BLOCK, width),
            fixed_spec(width, gates),
            fixed_spec(width, rest),
            fixed_spec(gates, width),
        ],
        out_specs=[
            rows_spec(BLOCK, width),
            rows_spec(BLOCK, rest),
            rows_spec(BLOCK, gates),
            rows_spec(BLOCK, gates),
            rows_spec(BLOCK, rest),
            rows_spec(BLOCK, width),
            cols_spec(width, BLOCK),
            rows_spec(BLOCK, 1),
            fixed_spec(half, 2 * gates),
            fixed_spec(half, 2 * gates),
            fixed_spec(short_rows, rest),
        ],
        scratch_shapes=[
            pltpu.VMEM((width, 2 * gates), F32),
            pltpu.VMEM((BLOCK, rest), BF16),
            pltpu.VMEM((BLOCK, gates), F32),
            pltpu.VMEM((BLOCK, 2 * KW * H), BF16),
        ],
    )(short_user, x_short, cot_short, proj_in, proj, proj_out)
    out_short, qkv_short, g_short, gate_short, slope_short, xbf_short = short_out[:6]
    turned_short, inv_short, early_mine, early_other, join_short = short_out[6:]

    whole, out_short = lax.optimization_barrier((whole, out_short))
    mixed = call(
        long_attend_kernel,
        (shaped((long_rows, VW)),) * H,
        2 * 10**9,
        2 * 2**20,
        "long_attend",
        in_specs=[SMEM, pl.BlockSpec(memory_space=pl.ANY)],
        scratch_shapes=[
            pltpu.VMEM((BLOCK, VW), F32),
            pltpu.VMEM((chunks * BLOCK, HW), BF16),
            pltpu.SemaphoreType.DMA((chunks,)),
        ],
    )(long_blocks, whole)
    out_long, sent, mid = call(
        long_head_kernel,
        (
            shaped((long_rows, width)),
            in_hbm((chunks, H, long_rows, VW)),
            in_hbm((long_rows, 2 * gates)),
        ),
        4 * long_rows * width * gates,
        3 * 2**20,
        "long_head",
        in_specs=[WHOLE] * 9,
        scratch_shapes=[pltpu.VMEM((long_rows, gates), F32)],
    )(*swap_heads(mixed), x_long, cot_long, proj_out, gate_long, slope_long)
    sent, qkv_short, mid, half_other, early_other = lax.optimization_barrier(
        (sent, qkv_short, mid, half_other, early_other)
    )
    all_g = spread_heads(sent)
    half_got = swap_cores(half_other)
    early_got = swap_cores(early_other)
    mid_got = swap_cores(mid)
    grad_short, short_mine, short_other = call(
        short_back_kernel,
        (in_hbm((short_rows, rest)), in_hbm((half, rest)), in_hbm((half, rest))),
        16 * 10**9,
        13 * 2**20,
        "short_back",
        vmem=58,
        grid=(2,),
        in_specs=[
            SMEM,
            cols_spec(short_rows, rest // 2),
            cols_spec(short_rows, gates // 2),
            cols_spec(short_rows, rest // 2),
            fixed_spec(width, short_rows),
            cols_spec(short_rows, rest // 2),
        ],
        out_specs=[
            cols_spec(short_rows, rest // 2),
            cols_spec(half, rest // 2),
            cols_spec(half, rest // 2),
        ],
        scratch_shapes=[
            pltpu.VMEM((short_rows, rest // 2), F32),
        ],
    )(short_user, qkv_short, g_short, slope_short, turned_short, join_short)
    mid_got, half_got, early_got, grad_short = lax.optimization_barrier(
        (mid_got, half_got, early_got, grad_short)
    )
    short_got = swap_cores(short_other)
    early = call(
        early_sums_kernel,
        in_hbm((half, 2 * gates)),
        8 * long_rows * half * gates,
        5 * 2**20,
        "early_sums",
    )(xbf_long, cot_long, mid, half_got, mid_got, early_mine, early_got)
    all_g, early = lax.optimization_barrier((all_g, early))
    early = scatter_pairs(early)

    grads = call(
        long_back_kernel,
        (shaped((long_rows, HW)),) * H,
        6 * 10**9,
        4 * 2**20,
        "long_back",
        vmem=62,
        in_specs=[SMEM, WHOLE, WHOLE],
        scratch_shapes=[
            pltpu.VMEM((BLOCK, 2 * KW), F32),
            pltpu.VMEM((BLOCK, 2 * KW), F32),
            pltpu.VMEM((BLOCK, VW), F32),
        ],
    )(long_blocks, whole, all_g)
    grad_long = call(
        long_slopes_kernel,
        shaped((long_rows, rest)),
        long_rows * rest,
        2**20,
        "long_slopes",
    )(*swap_heads(grads), slope_rest)
    late = call(
        late_sums_kernel,
        in_hbm((half, rest)),
        4 * long_rows * half * rest,
        5 * 2**20,
        "late_sums",
        grid=(2,),
        in_specs=[
            rows_spec(half // 2, rest),
            rows_spec(half // 2, rest),
            fixed_spec(long_rows, width),
            pl.BlockSpec((long_rows, half // 2), lambda step: (0, step + 2)),
            fixed_spec(long_rows, rest),
            fixed_spec(long_rows, rest),
        ],
        out_specs=rows_spec(half // 2, rest),
    )(short_mine, short_got, xbf_long, half_got, grad_long, swap_cores(grad_long))
    late, gate_short = lax.optimization_barrier((late, gate_short))
    late = scatter_pairs(late)

    def short_rows_spec(cols):
        return pl.BlockSpec((BLOCK, cols), lambda step: (jnp.minimum(step, 1), 0))

    back_short, back_long = call(
        input_back_kernel,
        (in_hbm((short_rows, width)), in_hbm((long_rows, width))),
        2 * (short_rows + long_rows) * width * cols,
        14 * 2**20,
        "input_back",
        vmem=60,
        grid=(short_rows // BLOCK + 1,),
        in_specs=[
            short_rows_spec(gates),
            short_rows_spec(rest),
            short_rows_spec(width),
            short_rows_spec(width),
            short_rows_spec(1),
            fixed_spec(width, gates),
            fixed_spec(width, rest),
        ]
        + [
            pl.BlockSpec((long_rows, gates), lambda step: (0, 1)),
            fixed_spec(long_rows, rest),
            fixed_spec(long_rows, width),
            fixed_spec(long_rows, width),
            fixed_spec(long_rows, 1),
        ],
        out_specs=[short_rows_spec(width), fixed_spec(long_rows, width)],
    )(
        gate_short,
        grad_short,
        cot_short,
        xbf_short,
        inv_short,
        proj_in,
        proj,
        mid,
        grad_long,
        cot_long,
        xbf_long,
        inv_long,
    )
    total_rows = lax.axis_size("dp") * sp_size * (long_rows + short_rows)
    early = jnp.sum(early.astype(F32), axis=0)
    sum_in, sum_out = call(
        functools.partial(final_sums_kernel, float(total_rows) ** (-0.5)),
        (shaped((early.shape[0], cols), F32), shaped((early.shape[0], gates), F32)),
        128 * 2**10,
        2**20,
        "final_sums",
    )(early, late)
    return (out_long, out_short, back_long, back_short, sum_in, sum_out)


def solution(mesh):
    rows = P(("dp", "sp"), None)
    return jax.shard_map(
        body,
        mesh=mesh,
        in_specs=(rows, rows, P(), rows, P(), P(), rows, rows),
        out_specs=(rows,) * 6,
        check_vma=False,
    )
```

```python
import functools

import jax
import jax.numpy as jnp
from jax import lax
from jax.experimental import pallas as pl
from jax.experimental.pallas import tpu as pltpu
from jax.sharding import PartitionSpec as P

H = 4
BLOCK = 512
KW = 64
VW = 128
HW = 2 * KW + VW
EPS = 1e-05
HALF_SCALE = 0.5 * KW**-0.5
F32 = jnp.float32
BF16 = jnp.bfloat16
MIB = 1024 * 1024


def dot(first, second, first_dim, second_dim):
    return lax.dot_general(
        first, second, (((first_dim,), (second_dim,)), ((), ())), preferred_element_type=F32
    )


def norm_rows(rows):
    center = rows - jnp.mean(rows, axis=-1, keepdims=True)
    inv_root = lax.rsqrt(jnp.mean(center * center, axis=-1, keepdims=True) + EPS)
    return center * inv_root, inv_root


def norm_back(upstream, normed, inv_root):
    return inv_root * (
        upstream
        - jnp.mean(upstream, axis=-1, keepdims=True)
        - normed * jnp.mean(upstream * normed, axis=-1, keepdims=True)
    )


def silu_half(half):
    return half * (1.0 + jnp.tanh(half))


def silu_both(half):
    curve = jnp.tanh(half)
    above = 1.0 + curve
    act = half * above
    return act, above + act * (1.0 - curve)


def low_lanes(shape):
    return lax.broadcasted_iota(jnp.int32, shape, 1) < KW


def turned(pair):
    return pltpu.roll(pair.astype(F32), KW, 1)


def score_side(qk):
    return jnp.where(low_lanes(qk.shape), 0.0, turned(qk) * HALF_SCALE).astype(BF16)


def causal(keys_first, keys, queries, key_start=0, query_start=0):
    shape = (keys, queries) if keys_first else (queries, keys)
    key_pos = key_start + lax.broadcasted_iota(jnp.int32, shape, 0 if keys_first else 1)
    query_pos = query_start + lax.broadcasted_iota(jnp.int32, shape, 1 if keys_first else 0)
    return key_pos <= query_pos


def project(x_bf, proj):
    act, slope = silu_both(0.5 * dot(x_bf, proj, 1, 0))
    return act.astype(BF16), 0.5 * slope


def head_out(x_rows, cot, proj_out, gate_u, slope_gate, mixed):
    mixed_n, inv_mix = norm_rows(mixed)
    gate_f = gate_u.astype(F32)
    gated = (mixed_n * gate_f).astype(BF16)
    out = (x_rows.astype(F32) + dot(gated, proj_out, 1, 0)).astype(BF16)
    grad_g = dot(cot, proj_out, 1, 1)
    grad_mixed = norm_back(grad_g * gate_f, mixed_n, inv_mix)
    grad_gate = (grad_g * mixed_n * slope_gate).astype(BF16)
    return out, gated, grad_gate, grad_mixed


def run_place():
    index = lax.axis_index("sp")
    return lax.rem(index, H), lax.div(index, H), lax.axis_index("dp")


def split_rows(part, start):
    for block in range(2):
        yield block, pl.ds(pl.multiple_of(start + 2 * part * block, part), part)


def long_project_kernel(
    x_ref, pin_q_ref, pin_k_ref, pin_v_ref, proj_ref, send_ref, inv_ref, xbf_ref, slope_ref
):
    @pl.when(pl.program_id(0) == 0)
    def _():
        normed, inv_std = norm_rows(x_ref[...].astype(F32))
        xbf_ref[...] = normed.astype(BF16)
        inv_ref[...] = inv_std

    q_pair, k_pair = pin_q_ref[...], pin_k_ref[...]
    low = low_lanes(q_pair.shape)
    even = jnp.where(low, q_pair.astype(F32), turned(k_pair)).astype(BF16)
    odd = jnp.where(low, turned(q_pair), k_pair.astype(F32)).astype(BF16)
    proj = jnp.concatenate([even, pin_v_ref[:, :VW], odd, pin_v_ref[:, VW:]], axis=1)
    proj_ref[...] = proj
    act, slope = project(xbf_ref[...], proj)
    slope_ref[...] = slope.astype(BF16)
    for copy in range(send_ref.shape[0]):
        for which in range(2):
            send_ref[copy, which] = act[:, HW * which : HW * (which + 1)]


def short_forward_kernel(
    user_ref,
    x_ref,
    cot_ref,
    pin_ref,
    proj_ref,
    pout_ref,
    long_xbf_ref,
    long_cot_ref,
    out_ref,
    qkv_ref,
    g_ref,
    grad_gate_ref,
    slope_ref,
    xbf_ref,
    turned_ref,
    inv_ref,
    mine_ref,
    other_ref,
    long_gate_ref,
    long_slope_ref,
    half_ref,
    sum_ref,
    seen_ref,
    mixed_ref,
    side_ref,
):
    step = pl.program_id(0)

    @pl.when(step == 0)
    def _():
        _, _, group = run_place()
        part = long_xbf_ref.shape[1] // 4
        act, slope = project(long_xbf_ref[...], pin_ref[...])
        long_gate_ref[...] = act
        long_slope_ref[...] = slope.astype(BF16)
        for block, features in split_rows(part, (1 - lax.rem(group, 2)) * part):
            half_ref[:, block * part : (block + 1) * part] = long_cot_ref[:, features]
            half_ref[:, (block + 2) * part : (block + 3) * part] = long_xbf_ref[:, features]

    joined = user_ref[0, 0] == user_ref[0, 1]
    share = jnp.where(joined, 0.5 / BLOCK, 1.0 / BLOCK)
    normed, inv_std = norm_rows(x_ref[...].astype(F32))
    x_bf = normed.astype(BF16)
    xbf_ref[...] = x_bf
    turned_ref[...] = x_bf.T
    inv_ref[...] = inv_std
    act, slope = project(x_bf, proj_ref[...])
    slope_ref[...] = slope.astype(BF16)
    qkv_ref[...] = act
    gate_u, slope_gate = project(x_bf, pin_ref[...])
    half = BLOCK // 2
    for which in range(H):
        qk = act[:, HW * which : HW * which + 2 * KW]
        values = act[:, HW * which + 2 * KW : HW * (which + 1)]
        side = score_side(qk)
        scores = dot(side, qk[:half], 1, 1)
        weights = jnp.where(causal(False, half, BLOCK), silu_half(scores), 0.0).astype(BF16)
        mixed = dot(weights, values[:half], 1, 0)
        scores = dot(side[half:], qk[half:], 1, 1)
        weights = jnp.where(causal(False, half, half), silu_half(scores), 0.0).astype(BF16)
        lower = mixed[half:] + dot(weights, values[half:], 1, 0)
        mixed_ref[:half, VW * which : VW * (which + 1)] = mixed[:half]
        mixed_ref[half:, VW * which : VW * (which + 1)] = lower

        side_ref[:, 2 * KW * which : 2 * KW * (which + 1)] = side

    @pl.when(jnp.logical_and(step == 1, joined))
    def _():
        for which in range(H):
            first = HW * which
            side = side_ref[:, 2 * KW * which : 2 * KW * (which + 1)]
            scores = dot(side, seen_ref[:, first : first + 2 * KW], 1, 1)
            mixed_ref[:, VW * which : VW * (which + 1)] += dot(
                silu_half(scores).astype(BF16), seen_ref[:, first + 2 * KW : first + HW], 1, 0
            )

    @pl.when(step == 0)
    def _():
        seen_ref[...] = act

    out, gated, grad_gate, grad_mixed = head_out(
        x_ref[...],
        cot_ref[...],
        pout_ref[...],
        gate_u,
        slope_gate,
        mixed_ref[...] * share,
    )
    out_ref[...] = out
    grad_gate_ref[...] = grad_gate
    g_ref[...] = (grad_mixed.astype(BF16).astype(F32) * share).astype(BF16)
    gates = gated.shape[1]

    @pl.when(step == 0)
    def _():
        sum_ref[:, :gates] = dot(cot_ref[...], gated, 0, 0)
        sum_ref[:, gates:] = dot(turned_ref[...], grad_gate_ref[...], 1, 0)

    @pl.when(step == 1)
    def _():
        part = mine_ref.shape[0] // 2
        core = lax.rem(lax.axis_index("dp"), 2)
        for target, side in ((mine_ref, core), (other_ref, 1 - core)):
            for block, features in split_rows(part, side * part):
                here = slice(block * part, (block + 1) * part)
                total = sum_ref[features, :gates] + dot(cot_ref[:, features], gated, 0, 0)
                target[here, :gates] = total.astype(BF16)
                total = dot(turned_ref[features, :], grad_gate_ref[...], 1, 0)
                target[here, gates:] = (sum_ref[features, gates:] + total).astype(BF16)


def back_block(query_side, query_qk, key_qk, values, g_rows, mask):
    act, slope = silu_both(dot(key_qk, query_side, 1, 1))
    slopes = dot(values, g_rows, 1, 1) * slope
    if mask is not None:
        act = jnp.where(mask, act, 0.0)
        slopes = jnp.where(mask, slopes, 0.0)
    slopes = slopes.astype(BF16)
    grad_q = dot(slopes, key_qk, 0, 0)
    grad_k = dot(slopes, query_qk, 1, 0)
    grad_v = dot(act.astype(BF16), g_rows, 1, 0)
    return grad_q, grad_k, grad_v


def short_back_kernel(
    user_ref, qkv_ref, g_ref, slope_ref, turned_ref, grad_ref, mine_ref, other_ref, acc_ref, side_ref
):
    joined = user_ref[0, 0] == user_ref[0, 1]
    half = BLOCK // 2
    heads = range(qkv_ref.shape[1] // HW)
    for which in heads:
        first = HW * which
        qk = qkv_ref[:, first : first + 2 * KW]
        side = score_side(qk)
        values = qkv_ref[:, first + 2 * KW : first + HW]
        g_rows = g_ref[:, VW * which : VW * (which + 1)]
        lanes = low_lanes((half, 2 * KW))
        for block in range(qkv_ref.shape[0] // BLOCK):
            top = slice(block * BLOCK, block * BLOCK + half)
            end = slice(block * BLOCK + half, (block + 1) * BLOCK)
            both = slice(block * BLOCK, (block + 1) * BLOCK)
            dq_one, dk_one, dv_one = back_block(
                side[both], qk[both], qk[top], values[top], g_rows[both], causal(True, half, BLOCK)
            )
            dq_two, dk_two, dv_two = back_block(
                side[end], qk[end], qk[end], values[end], g_rows[end], causal(True, half, half)
            )
            acc_ref[top, first : first + 2 * KW] = jnp.where(lanes, dk_one, dq_one[:half])
            acc_ref[end, first : first + 2 * KW] = jnp.where(lanes, dk_two, dq_one[half:] + dq_two)
            acc_ref[top, first + 2 * KW : first + HW] = dv_one
            acc_ref[end, first + 2 * KW : first + HW] = dv_two
        side_ref[:, 2 * KW * which : 2 * KW * (which + 1)] = side[BLOCK:]

    @pl.when(joined)
    def _():
        one, two = slice(0, BLOCK), slice(BLOCK, 2 * BLOCK)
        for which in heads:
            first = HW * which
            pair = slice(first, first + 2 * KW)
            grad_q, grad_k, grad_v = back_block(
                side_ref[:, 2 * KW * which : 2 * KW * (which + 1)],
                qkv_ref[two, pair],
                qkv_ref[one, pair],
                qkv_ref[one, first + 2 * KW : first + HW],
                g_ref[two, VW * which : VW * (which + 1)],
                None,
            )
            lanes = low_lanes((BLOCK, 2 * KW))
            acc_ref[one, pair] += jnp.where(lanes, grad_k, 0.0)
            acc_ref[two, pair] += jnp.where(lanes, 0.0, grad_q)
            acc_ref[one, first + 2 * KW : first + HW] += grad_v

    for which in heads:
        first = HW * which
        pair, rest = slice(first, first + 2 * KW), slice(first + 2 * KW, first + HW)
        grads = turned(acc_ref[:, pair]) * HALF_SCALE
        grad_ref[:, pair] = (grads * slope_ref[:, pair].astype(F32)).astype(BF16)
        grad_ref[:, rest] = (acc_ref[:, rest] * slope_ref[:, rest].astype(F32)).astype(BF16)
    grad_pre = grad_ref[...]
    part = mine_ref.shape[0] // 2
    core = lax.rem(lax.axis_index("dp"), 2)
    for target, side in ((mine_ref, core), (other_ref, 1 - core)):
        for block, features in split_rows(part, side * part):
            total = dot(turned_ref[features, :], grad_pre, 1, 0)
            target[block * part : (block + 1) * part] = total.astype(BF16)


def rows_at(index):
    return pl.ds(pl.multiple_of(index * BLOCK, BLOCK), BLOCK)


def long_attend_kernel(blocks_smem, all_hbm, *refs):
    mixed_refs, (acc_ref, all_ref, sems) = refs[:H], refs[H:]
    mine, chunk, group = run_place()
    valid = blocks_smem[group]

    def block_copy(index):
        rows = rows_at(index)
        return pltpu.make_async_copy(all_hbm.at[rows], all_ref.at[rows], sems.at[index])

    block_copy(chunk).start()

    @pl.loop(0, chunk)
    def _(index):
        block_copy(index).start()

    acc_ref[...] = jnp.zeros_like(acc_ref)
    block_copy(chunk).wait()

    @pl.when(chunk >= valid)
    def _():
        @pl.loop(0, chunk)
        def _(index):
            block_copy(index).wait()

    @pl.when(chunk < valid)
    def _():
        side = score_side(all_ref[rows_at(chunk), : 2 * KW])

        @pl.loop(0, chunk)
        def _(index):
            block_copy(index).wait()
            scores = dot(side, all_ref[rows_at(index), : 2 * KW], 1, 1)
            acc_ref[...] += dot(
                silu_half(scores).astype(BF16), all_ref[rows_at(index), 2 * KW :], 1, 0
            )

        weights = silu_half(dot(side, all_ref[rows_at(chunk), : 2 * KW], 1, 1))
        weights = jnp.where(causal(False, BLOCK, BLOCK), weights, 0.0).astype(BF16)
        acc_ref[...] += dot(weights, all_ref[rows_at(chunk), 2 * KW :], 1, 0)

    coeff = 1.0 / (valid * BLOCK).astype(F32)
    rows = mixed_refs[0].shape[0]
    for bits in range(H):
        start = pl.multiple_of((mine ^ bits) * rows, rows)
        mixed_refs[bits][...] = (acc_ref[pl.ds(start, rows), :] * coeff).astype(BF16)


def long_back_kernel(blocks_smem, all_ref, g_ref, *refs):
    grad_refs, (dq_ref, dk_ref, dv_ref) = refs[:H], refs[H:]
    mine, chunk, group = run_place()
    valid = blocks_smem[group]
    dq_ref[...] = jnp.zeros_like(dq_ref)
    dk_ref[...] = jnp.zeros_like(dk_ref)
    dv_ref[...] = jnp.zeros_like(dv_ref)

    @pl.when(chunk < valid)
    def _():
        own = rows_at(chunk)
        qk = all_ref[own, : 2 * KW]
        side = score_side(qk)
        values = all_ref[own, 2 * KW :]
        g_own = g_ref[own, :]
        grad_q, grad_k, grad_v = back_block(
            side, qk, qk, values, g_own, causal(True, BLOCK, BLOCK)
        )
        dq_ref[...] = grad_q
        dk_ref[...] = grad_k
        dv_ref[...] = grad_v

        @pl.loop(0, chunk)
        def _(index):
            keys = all_ref[rows_at(index), : 2 * KW]
            act, slope = silu_both(dot(side, keys, 1, 1))
            slopes = dot(g_own, all_ref[rows_at(index), 2 * KW :], 1, 1) * slope
            dq_ref[...] += dot(slopes.astype(BF16), keys, 1, 0)

        @pl.loop(chunk + 1, valid)
        def _(index):
            g_rows = g_ref[rows_at(index), :]
            queries = all_ref[rows_at(index), : 2 * KW]
            act, slope = silu_both(dot(qk, score_side(queries), 1, 1))
            slopes = (dot(values, g_rows, 1, 1) * slope).astype(BF16)
            dk_ref[...] += dot(slopes, queries, 1, 0)
            dv_ref[...] += dot(act.astype(BF16), g_rows, 1, 0)

    coeff = 1.0 / (valid * BLOCK).astype(F32)
    rows = grad_refs[0].shape[0]
    lanes = low_lanes((rows, 2 * KW))
    for bits in range(H):
        part = pl.ds(pl.multiple_of((mine ^ bits) * rows, rows), rows)
        pair = turned(jnp.where(lanes, dk_ref[part, :], dq_ref[part, :])) * HALF_SCALE
        grad_refs[bits][:, : 2 * KW] = (pair * coeff).astype(BF16)
        grad_refs[bits][:, 2 * KW :] = (dv_ref[part, :] * coeff).astype(BF16)


def long_head_kernel(
    got_0,
    got_1,
    got_2,
    got_3,
    x_ref,
    cot_ref,
    pout_ref,
    gate_ref,
    slope_ref,
    out_ref,
    send_ref,
    mid_ref,
    mixed_ref,
):
    mine, _, _ = run_place()
    for bits, got in enumerate((got_0, got_1, got_2, got_3)):
        start = pl.multiple_of((mine ^ bits) * VW, VW)
        mixed_ref[:, pl.ds(start, VW)] = got[...].astype(F32)
    out, gated, grad_gate, grad_mixed = head_out(
        x_ref[...],
        cot_ref[...],
        pout_ref[...],
        gate_ref[...],
        slope_ref[...].astype(F32),
        mixed_ref[...],
    )
    out_ref[...] = out
    cols = gated.shape[1]
    mid_ref[:, :cols] = gated
    mid_ref[:, cols:] = grad_gate
    grad_mixed = grad_mixed.astype(BF16)
    for copy in range(send_ref.shape[0]):
        for which in range(H):
            send_ref[copy, which] = grad_mixed[:, VW * which : VW * (which + 1)]


def early_sums_kernel(
    xbf_ref, cot_ref, mid_ref, half_ref, mid_got, mine_ref, got_ref, sum_ref
):
    cols = mid_ref.shape[1] // 2
    part = sum_ref.shape[0] // 2
    core = lax.rem(lax.axis_index("dp"), 2)
    mid = jnp.concatenate([mid_ref[...], mid_got[...]], axis=0)
    for block, features in split_rows(part, core * part):
        here = slice(block * part, (block + 1) * part)
        for place, own in ((0, cot_ref), (1, xbf_ref)):
            start = (2 * place + block) * part
            rows = jnp.concatenate([own[:, features], half_ref[:, start : start + part]], axis=0)
            there = slice(place * cols, (place + 1) * cols)
            total = mine_ref[here, there].astype(F32) + got_ref[here, there].astype(F32)
            sum_ref[here, there] = (total + dot(rows, mid[:, there], 0, 0)).astype(BF16)


def long_slopes_kernel(got_0, got_1, got_2, got_3, slope_ref, grad_ref):
    mine, _, _ = run_place()
    for bits, got in enumerate((got_0, got_1, got_2, got_3)):
        there = pl.ds(pl.multiple_of((mine ^ bits) * HW, HW), HW)
        grads = got[...].astype(F32) * slope_ref[:, there].astype(F32)
        grad_ref[:, there] = grads.astype(BF16)


def late_sums_kernel(mine_ref, got_ref, xbf_ref, half_ref, grad_ref, grad_got, sum_ref):
    part = sum_ref.shape[0]
    core = lax.rem(lax.axis_index("dp"), 2)
    start = (core + 2 * pl.program_id(0)) * part
    features = pl.ds(pl.multiple_of(start, part), part)
    rows = jnp.concatenate([xbf_ref[:, features], half_ref[...]], axis=0)
    grads = jnp.concatenate([grad_ref[...], grad_got[...]], axis=0)
    total = mine_ref[...].astype(F32) + got_ref[...].astype(F32)
    sum_ref[...] = (total + dot(rows, grads, 0, 0)).astype(BF16)


def final_sums_kernel(factor, early_ref, late_ref, in_ref, out_ref):
    gates = out_ref.shape[1]
    out_ref[...] = early_ref[:, :gates] * factor
    in_ref[:, :gates] = early_ref[:, gates:] * factor
    late = late_ref[0].astype(F32)
    for step in range(1, late_ref.shape[0]):
        late += late_ref[step].astype(F32)
    late = late * factor
    low = low_lanes((late.shape[0], 2 * KW))
    for pair in range(H // 2):
        first = 2 * HW * pair
        even, odd = late[:, first : first + 2 * KW], late[:, first + HW : first + HW + 2 * KW]
        first_q = gates + 2 * KW * pair
        first_k = first_q + H * KW
        first_v = gates + 2 * H * KW + 2 * VW * pair
        in_ref[:, first_q : first_q + 2 * KW] = jnp.where(low, even, turned(odd))
        in_ref[:, first_k : first_k + 2 * KW] = jnp.where(low, turned(even), odd)
        in_ref[:, first_v : first_v + VW] = late[:, first + 2 * KW : first + HW]
        in_ref[:, first_v + VW : first_v + 2 * VW] = late[:, first + HW + 2 * KW : first + 2 * HW]


def input_back_kernel(
    grad_gate_ref,
    grad_ref,
    cot_ref,
    xbf_ref,
    inv_ref,
    pin_ref,
    proj_ref,
    long_gate_ref,
    long_grad_ref,
    long_cot_ref,
    long_xbf_ref,
    long_inv_ref,
    back_ref,
    long_back_ref,
):
    step = pl.program_id(0)

    def finish(gate, grad, cot, normed, inv, target):
        grad_norm = dot(gate[...], pin_ref[...], 1, 1) + dot(grad[...], proj_ref[...], 1, 1)
        back = norm_back(grad_norm, normed.astype(F32), inv[...])
        target[...] = (cot[...].astype(F32) + back).astype(BF16)

    @pl.when(step < 2)
    def _():
        finish(grad_gate_ref, grad_ref, cot_ref, xbf_ref[...], inv_ref, back_ref)

    @pl.when(step == 2)
    def _():
        finish(
            long_gate_ref,
            long_grad_ref,
            long_cot_ref,
            long_xbf_ref[...],
            long_inv_ref,
            long_back_ref,
        )


def shaped(shape, dtype=BF16):
    return jax.ShapeDtypeStruct(shape, dtype)


def in_hbm(shape, dtype=BF16):
    return pltpu.HBM(shape, dtype)


def call(kernel, out_shape, flops, moved, name, vmem=24, **kwargs):
    return pl.pallas_call(
        kernel,
        out_shape=out_shape,
        cost_estimate=pl.CostEstimate(flops=flops, bytes_accessed=moved, transcendentals=0),
        compiler_params=pltpu.CompilerParams(vmem_limit_bytes=vmem * MIB),
        name=name,
        **kwargs,
    )


SMEM = pl.BlockSpec(memory_space=pltpu.SMEM)
WHOLE = pl.BlockSpec(memory_space=pltpu.VMEM)


def rows_spec(rows, cols):
    return pl.BlockSpec((rows, cols), lambda step: (step, 0))


def cols_spec(rows, cols):
    return pl.BlockSpec((rows, cols), lambda step: (0, step))


def fixed_spec(rows, cols):
    return pl.BlockSpec((rows, cols), lambda step: (0, 0))


def swap_heads(pieces):
    size = lax.axis_size("sp")
    return [pieces[0]] + [
        lax.ppermute(pieces[bits], "sp", [(src, src ^ bits) for src in range(size)])
        for bits in range(1, H)
    ]


def spread_heads(sent):
    chunks, heads, rows, cols = sent.shape
    got = lax.all_to_all(sent.reshape(chunks * heads, rows, cols), "sp", 0, 0, tiled=True)
    return got.reshape(chunks * heads * rows, cols)


def swap_cores(half):
    size = lax.axis_size("dp")
    return lax.ppermute(half, "dp", [(src, src ^ 1) for src in range(size)])


def scatter_pairs(partial):
    runs, size = lax.axis_size("dp"), lax.axis_size("sp")
    groups = [
        [run * size + place for run in range(core, runs, 2) for place in range(size)]
        for core in range(2)
    ]
    count = len(groups[0])
    sent = partial.reshape(count, partial.shape[0] // count, partial.shape[1])
    return lax.all_to_all(sent, ("dp", "sp"), 0, 0, tiled=True, axis_index_groups=groups)


def body(x_long, x_short, long_blocks, short_user, proj_in, proj_out, cot_long, cot_short):
    sp_size = lax.axis_size("sp")
    long_rows, width = x_long.shape
    short_rows = x_short.shape[0]
    gates = proj_out.shape[0]
    cols = proj_in.shape[1]
    rest = cols - gates
    half = width // 2
    chunks = sp_size // H

    proj, sent, inv_long, xbf_long, slope_rest = call(
        long_project_kernel,
        (
            in_hbm((width, rest)),
            in_hbm((chunks, H, long_rows, HW)),
            in_hbm((long_rows, 1), F32),
            in_hbm((long_rows, width)),
            in_hbm((long_rows, rest)),
        ),
        2 * long_rows * width * rest,
        8 * 2**20,
        "long_project",
        vmem=60,
        grid=(2,),
        in_specs=[
            fixed_spec(long_rows, width),
            pl.BlockSpec((width, 2 * KW), lambda step: (0, step + gates // (2 * KW))),
            pl.BlockSpec((width, 2 * KW), lambda step: (0, step + (gates + H * KW) // (2 * KW))),
            pl.BlockSpec((width, 2 * VW), lambda step: (0, step + (gates + 2 * H * KW) // (2 * VW))),
        ],
        out_specs=[
            cols_spec(width, rest // 2),
            pl.BlockSpec((chunks, 2, long_rows, HW), lambda step: (0, step, 0, 0)),
            fixed_spec(long_rows, 1),
            fixed_spec(long_rows, width),
            cols_spec(long_rows, rest // 2),
        ],
    )(x_long, proj_in, proj_in, proj_in)
    whole = spread_heads(sent)
    short_out = call(
        short_forward_kernel,
        (
            in_hbm((short_rows, width)),
            in_hbm((short_rows, rest)),
            in_hbm((short_rows, gates)),
            in_hbm((short_rows, gates)),
            in_hbm((short_rows, rest)),
            in_hbm((short_rows, width)),
            in_hbm((width, short_rows)),
            in_hbm((short_rows, 1), F32),
            in_hbm((half, 2 * gates)),
            in_hbm((half, 2 * gates)),
            in_hbm((long_rows, gates)),
            in_hbm((long_rows, gates)),
            in_hbm((long_rows, width)),
        ),
        20 * 10**9,
        24 * 2**20,
        "short_forward",
        vmem=56,
        grid=(short_rows // BLOCK,),
        in_specs=[
            SMEM,
            rows_spec(BLOCK, width),
            rows_spec(BLOCK, width),
            fixed_spec(width, gates),
            fixed_spec(width, rest),
            fixed_spec(gates, width),
            fixed_spec(long_rows, width),
            fixed_spec(long_rows, width),
        ],
        out_specs=[
            rows_spec(BLOCK, width),
            rows_spec(BLOCK, rest),
            rows_spec(BLOCK, gates),
            rows_spec(BLOCK, gates),
            rows_spec(BLOCK, rest),
            rows_spec(BLOCK, width),
            cols_spec(width, BLOCK),
            rows_spec(BLOCK, 1),
            fixed_spec(half, 2 * gates),
            fixed_spec(half, 2 * gates),
            fixed_spec(long_rows, gates),
            fixed_spec(long_rows, gates),
            fixed_spec(long_rows, width),
        ],
        scratch_shapes=[
            pltpu.VMEM((width, 2 * gates), F32),
            pltpu.VMEM((BLOCK, rest), BF16),
            pltpu.VMEM((BLOCK, gates), F32),
            pltpu.VMEM((BLOCK, 2 * KW * H), BF16),
        ],
    )(short_user, x_short, cot_short, proj_in, proj, proj_out, xbf_long, cot_long)
    out_short, qkv_short, g_short, gate_short, slope_short, xbf_short = short_out[:6]
    turned_short, inv_short, early_mine, early_other = short_out[6:10]
    gate_long, slope_long, half_other = short_out[10:]
    early_got = swap_cores(early_other)


    whole, early_got, out_short = lax.optimization_barrier((whole, early_got, out_short))
    mixed = call(
        long_attend_kernel,
        (shaped((long_rows, VW)),) * H,
        2 * 10**9,
        2 * 2**20,
        "long_attend",
        vmem=62,
        in_specs=[SMEM, pl.BlockSpec(memory_space=pl.ANY)],
        scratch_shapes=[
            pltpu.VMEM((BLOCK, VW), F32),
            pltpu.VMEM((chunks * BLOCK, HW), BF16),
            pltpu.SemaphoreType.DMA((chunks,)),
        ],
    )(long_blocks, whole)
    out_long, sent, mid = call(
        long_head_kernel,
        (
            shaped((long_rows, width)),
            in_hbm((chunks, H, long_rows, VW)),
            in_hbm((long_rows, 2 * gates)),
        ),
        4 * long_rows * width * gates,
        3 * 2**20,
        "long_head",
        in_specs=[WHOLE] * 9,
        scratch_shapes=[pltpu.VMEM((long_rows, gates), F32)],
    )(*swap_heads(mixed), x_long, cot_long, proj_out, gate_long, slope_long)
    sent, qkv_short, mid, half_other = lax.optimization_barrier((sent, qkv_short, mid, half_other))
    all_g = spread_heads(sent)
    half_got = swap_cores(half_other)
    mid_got = swap_cores(mid)
    grad_short, short_mine, short_other = call(
        short_back_kernel,
        (in_hbm((short_rows, rest)), in_hbm((half, rest)), in_hbm((half, rest))),
        16 * 10**9,
        13 * 2**20,
        "short_back",
        vmem=56,
        grid=(2,),
        in_specs=[
            SMEM,
            cols_spec(short_rows, rest // 2),
            cols_spec(short_rows, gates // 2),
            cols_spec(short_rows, rest // 2),
            fixed_spec(width, short_rows),
        ],
        out_specs=[
            cols_spec(short_rows, rest // 2),
            cols_spec(half, rest // 2),
            cols_spec(half, rest // 2),
        ],
        scratch_shapes=[
            pltpu.VMEM((short_rows, rest // 2), F32),
            pltpu.VMEM((BLOCK, rest // 4), BF16),
        ],
    )(short_user, qkv_short, g_short, slope_short, turned_short)
    mid_got, half_got, grad_short = lax.optimization_barrier((mid_got, half_got, grad_short))
    short_got = swap_cores(short_other)
    early = call(
        early_sums_kernel,
        in_hbm((half, 2 * gates)),
        8 * long_rows * half * gates,
        5 * 2**20,
        "early_sums",
    )(xbf_long, cot_long, mid, half_got, mid_got, early_mine, early_got)
    all_g, early = lax.optimization_barrier((all_g, early))
    early = scatter_pairs(early)

    grads = call(
        long_back_kernel,
        (shaped((long_rows, HW)),) * H,
        6 * 10**9,
        4 * 2**20,
        "long_back",
        vmem=62,
        in_specs=[SMEM, WHOLE, WHOLE],
        scratch_shapes=[
            pltpu.VMEM((BLOCK, 2 * KW), F32),
            pltpu.VMEM((BLOCK, 2 * KW), F32),
            pltpu.VMEM((BLOCK, VW), F32),
        ],
    )(long_blocks, whole, all_g)
    grad_long = call(
        long_slopes_kernel,
        shaped((long_rows, rest)),
        long_rows * rest,
        2**20,
        "long_slopes",
    )(*swap_heads(grads), slope_rest)
    late = call(
        late_sums_kernel,
        in_hbm((half, rest)),
        4 * long_rows * half * rest,
        5 * 2**20,
        "late_sums",
        grid=(2,),
        in_specs=[
            rows_spec(half // 2, rest),
            rows_spec(half // 2, rest),
            fixed_spec(long_rows, width),
            pl.BlockSpec((long_rows, half // 2), lambda step: (0, step + 2)),
            fixed_spec(long_rows, rest),
            fixed_spec(long_rows, rest),
        ],
        out_specs=rows_spec(half // 2, rest),
    )(short_mine, short_got, xbf_long, half_got, grad_long, swap_cores(grad_long))
    late, gate_short = lax.optimization_barrier((late, gate_short))
    late = scatter_pairs(late)

    def short_rows_spec(cols):
        return pl.BlockSpec((BLOCK, cols), lambda step: (jnp.minimum(step, 1), 0))

    back_short, back_long = call(
        input_back_kernel,
        (in_hbm((short_rows, width)), in_hbm((long_rows, width))),
        2 * (short_rows + long_rows) * width * cols,
        14 * 2**20,
        "input_back",
        vmem=60,
        grid=(short_rows // BLOCK + 1,),
        in_specs=[
            short_rows_spec(gates),
            short_rows_spec(rest),
            short_rows_spec(width),
            short_rows_spec(width),
            short_rows_spec(1),
            fixed_spec(width, gates),
            fixed_spec(width, rest),
        ]
        + [
            pl.BlockSpec((long_rows, gates), lambda step: (0, 1)),
            fixed_spec(long_rows, rest),
            fixed_spec(long_rows, width),
            fixed_spec(long_rows, width),
            fixed_spec(long_rows, 1),
        ],
        out_specs=[short_rows_spec(width), fixed_spec(long_rows, width)],
    )(
        gate_short,
        grad_short,
        cot_short,
        xbf_short,
        inv_short,
        proj_in,
        proj,
        mid,
        grad_long,
        cot_long,
        xbf_long,
        inv_long,
    )
    total_rows = lax.axis_size("dp") * sp_size * (long_rows + short_rows)
    early = jnp.sum(early.astype(F32), axis=0)
    sum_in, sum_out = call(
        functools.partial(final_sums_kernel, float(total_rows) ** (-0.5)),
        (shaped((early.shape[0], cols), F32), shaped((early.shape[0], gates), F32)),
        128 * 2**10,
        2**20,
        "final_sums",
    )(early, late)
    return (out_long, out_short, back_long, back_short, sum_in, sum_out)


def solution(mesh):
    rows = P(("dp", "sp"), None)
    return jax.shard_map(
        body,
        mesh=mesh,
        in_specs=(rows, rows, P(), rows, P(), P(), rows, rows),
        out_specs=(rows,) * 6,
        check_vma=False,
    )
```

```python
import functools

import jax
import jax.numpy as jnp
from jax import lax
from jax.experimental import pallas as pl
from jax.experimental.pallas import tpu as pltpu
from jax.sharding import PartitionSpec as P

H = 4
BLOCK = 512
KW = 64
VW = 128
HW = 2 * KW + VW
EPS = 1e-05
HALF_SCALE = 0.5 * KW**-0.5
F32 = jnp.float32
BF16 = jnp.bfloat16
MIB = 1024 * 1024


def dot(first, second, first_dim, second_dim):
    return lax.dot_general(
        first, second, (((first_dim,), (second_dim,)), ((), ())), preferred_element_type=F32
    )


def norm_rows(rows):
    center = rows - jnp.mean(rows, axis=-1, keepdims=True)
    inv_root = lax.rsqrt(jnp.mean(center * center, axis=-1, keepdims=True) + EPS)
    return center * inv_root, inv_root


def norm_back(upstream, normed, inv_root):
    return inv_root * (
        upstream
        - jnp.mean(upstream, axis=-1, keepdims=True)
        - normed * jnp.mean(upstream * normed, axis=-1, keepdims=True)
    )


def silu_half(half):
    return half * (1.0 + jnp.tanh(half))


def silu_both(half):
    curve = jnp.tanh(half)
    above = 1.0 + curve
    act = half * above
    return act, above + act * (1.0 - curve)


def low_lanes(shape):
    return lax.broadcasted_iota(jnp.int32, shape, 1) < KW


def turned(pair):
    return pltpu.roll(pair.astype(F32), KW, 1)


def score_side(qk):
    return jnp.where(low_lanes(qk.shape), 0.0, turned(qk) * HALF_SCALE).astype(BF16)


def causal(keys_first, keys, queries, key_start=0, query_start=0):
    shape = (keys, queries) if keys_first else (queries, keys)
    key_pos = key_start + lax.broadcasted_iota(jnp.int32, shape, 0 if keys_first else 1)
    query_pos = query_start + lax.broadcasted_iota(jnp.int32, shape, 1 if keys_first else 0)
    return key_pos <= query_pos


def project(x_bf, proj):
    act, slope = silu_both(0.5 * dot(x_bf, proj, 1, 0))
    return act.astype(BF16), 0.5 * slope


def head_out(x_rows, cot, proj_out, gate_u, slope_gate, mixed):
    mixed_n, inv_mix = norm_rows(mixed)
    gate_f = gate_u.astype(F32)
    gated = (mixed_n * gate_f).astype(BF16)
    out = (x_rows.astype(F32) + dot(gated, proj_out, 1, 0)).astype(BF16)
    grad_g = dot(cot, proj_out, 1, 1)
    grad_mixed = norm_back(grad_g * gate_f, mixed_n, inv_mix)
    grad_gate = (grad_g * mixed_n * slope_gate).astype(BF16)
    return out, gated, grad_gate, grad_mixed


def run_place():
    index = lax.axis_index("sp")
    return lax.rem(index, H), lax.div(index, H), lax.axis_index("dp")


def split_rows(part, start):
    for block in range(2):
        yield block, pl.ds(pl.multiple_of(start + 2 * part * block, part), part)


def long_project_kernel(
    x_ref, pin_q_ref, pin_k_ref, pin_v_ref, proj_ref, send_ref, inv_ref, xbf_ref, slope_ref
):
    @pl.when(pl.program_id(0) == 0)
    def _():
        normed, inv_std = norm_rows(x_ref[...].astype(F32))
        xbf_ref[...] = normed.astype(BF16)
        inv_ref[...] = inv_std

    q_pair, k_pair = pin_q_ref[...], pin_k_ref[...]
    low = low_lanes(q_pair.shape)
    even = jnp.where(low, q_pair.astype(F32), turned(k_pair)).astype(BF16)
    odd = jnp.where(low, turned(q_pair), k_pair.astype(F32)).astype(BF16)
    proj = jnp.concatenate([even, pin_v_ref[:, :VW], odd, pin_v_ref[:, VW:]], axis=1)
    proj_ref[...] = proj
    act, slope = project(xbf_ref[...], proj)
    slope_ref[...] = slope.astype(BF16)
    for copy in range(send_ref.shape[0]):
        for which in range(2):
            send_ref[copy, which] = act[:, HW * which : HW * (which + 1)]


def short_forward_kernel(
    user_ref,
    x_ref,
    cot_ref,
    pin_ref,
    proj_ref,
    pout_ref,
    long_xbf_ref,
    long_cot_ref,
    out_ref,
    qkv_ref,
    g_ref,
    grad_gate_ref,
    slope_ref,
    xbf_ref,
    turned_ref,
    inv_ref,
    mine_ref,
    other_ref,
    long_gate_ref,
    long_slope_ref,
    half_ref,
    sum_ref,
    seen_ref,
    mixed_ref,
    side_ref,
):
    step = pl.program_id(0)

    @pl.when(step == 0)
    def _():
        _, _, group = run_place()
        part = long_xbf_ref.shape[1] // 4
        act, slope = project(long_xbf_ref[...], pin_ref[...])
        long_gate_ref[...] = act
        long_slope_ref[...] = slope.astype(BF16)
        for block, features in split_rows(part, (1 - lax.rem(group, 2)) * part):
            half_ref[:, block * part : (block + 1) * part] = long_cot_ref[:, features]
            half_ref[:, (block + 2) * part : (block + 3) * part] = long_xbf_ref[:, features]

    joined = user_ref[0, 0] == user_ref[0, 1]
    share = jnp.where(joined, 0.5 / BLOCK, 1.0 / BLOCK)
    normed, inv_std = norm_rows(x_ref[...].astype(F32))
    x_bf = normed.astype(BF16)
    xbf_ref[...] = x_bf
    turned_ref[...] = x_bf.T
    inv_ref[...] = inv_std
    act, slope = project(x_bf, proj_ref[...])
    slope_ref[...] = slope.astype(BF16)
    qkv_ref[...] = act
    gate_u, slope_gate = project(x_bf, pin_ref[...])
    half = BLOCK // 2
    for which in range(H):
        qk = act[:, HW * which : HW * which + 2 * KW]
        values = act[:, HW * which + 2 * KW : HW * (which + 1)]
        side = score_side(qk)
        scores = dot(side, qk[:half], 1, 1)
        weights = jnp.where(causal(False, half, BLOCK), silu_half(scores), 0.0).astype(BF16)
        mixed = dot(weights, values[:half], 1, 0)
        scores = dot(side[half:], qk[half:], 1, 1)
        weights = jnp.where(causal(False, half, half), silu_half(scores), 0.0).astype(BF16)
        lower = mixed[half:] + dot(weights, values[half:], 1, 0)
        mixed_ref[:half, VW * which : VW * (which + 1)] = mixed[:half]
        mixed_ref[half:, VW * which : VW * (which + 1)] = lower

        side_ref[:, 2 * KW * which : 2 * KW * (which + 1)] = side

    @pl.when(jnp.logical_and(step == 1, joined))
    def _():
        for which in range(H):
            first = HW * which
            side = side_ref[:, 2 * KW * which : 2 * KW * (which + 1)]
            scores = dot(side, seen_ref[:, first : first + 2 * KW], 1, 1)
            mixed_ref[:, VW * which : VW * (which + 1)] += dot(
                silu_half(scores).astype(BF16), seen_ref[:, first + 2 * KW : first + HW], 1, 0
            )

    @pl.when(step == 0)
    def _():
        seen_ref[...] = act

    out, gated, grad_gate, grad_mixed = head_out(
        x_ref[...],
        cot_ref[...],
        pout_ref[...],
        gate_u,
        slope_gate,
        mixed_ref[...] * share,
    )
    out_ref[...] = out
    grad_gate_ref[...] = grad_gate
    g_ref[...] = (grad_mixed.astype(BF16).astype(F32) * share).astype(BF16)
    gates = gated.shape[1]

    @pl.when(step == 0)
    def _():
        sum_ref[:, :gates] = dot(cot_ref[...], gated, 0, 0)
        sum_ref[:, gates:] = dot(turned_ref[...], grad_gate_ref[...], 1, 0)

    @pl.when(step == 1)
    def _():
        part = mine_ref.shape[0] // 2
        core = lax.rem(lax.axis_index("dp"), 2)
        for target, side in ((mine_ref, core), (other_ref, 1 - core)):
            for block, features in split_rows(part, side * part):
                here = slice(block * part, (block + 1) * part)
                total = sum_ref[features, :gates] + dot(cot_ref[:, features], gated, 0, 0)
                target[here, :gates] = total.astype(BF16)
                total = dot(turned_ref[features, :], grad_gate_ref[...], 1, 0)
                target[here, gates:] = (sum_ref[features, gates:] + total).astype(BF16)


def back_block(query_side, query_qk, key_qk, values, g_rows, mask):
    act, slope = silu_both(dot(key_qk, query_side, 1, 1))
    slopes = dot(values, g_rows, 1, 1) * slope
    if mask is not None:
        act = jnp.where(mask, act, 0.0)
        slopes = jnp.where(mask, slopes, 0.0)
    slopes = slopes.astype(BF16)
    grad_q = dot(slopes, key_qk, 0, 0)
    grad_k = dot(slopes, query_qk, 1, 0)
    grad_v = dot(act.astype(BF16), g_rows, 1, 0)
    return grad_q, grad_k, grad_v


def short_back_kernel(
    user_ref, qkv_ref, g_ref, slope_ref, turned_ref, grad_ref, mine_ref, other_ref, acc_ref, side_ref
):
    joined = user_ref[0, 0] == user_ref[0, 1]
    half = BLOCK // 2
    heads = range(qkv_ref.shape[1] // HW)
    for which in heads:
        first = HW * which
        qk = qkv_ref[:, first : first + 2 * KW]
        side = score_side(qk)
        values = qkv_ref[:, first + 2 * KW : first + HW]
        g_rows = g_ref[:, VW * which : VW * (which + 1)]
        lanes = low_lanes((half, 2 * KW))
        for block in range(qkv_ref.shape[0] // BLOCK):
            top = slice(block * BLOCK, block * BLOCK + half)
            end = slice(block * BLOCK + half, (block + 1) * BLOCK)
            both = slice(block * BLOCK, (block + 1) * BLOCK)
            dq_one, dk_one, dv_one = back_block(
                side[both], qk[both], qk[top], values[top], g_rows[both], causal(True, half, BLOCK)
            )
            dq_two, dk_two, dv_two = back_block(
                side[end], qk[end], qk[end], values[end], g_rows[end], causal(True, half, half)
            )
            acc_ref[top, first : first + 2 * KW] = jnp.where(lanes, dk_one, dq_one[:half])
            acc_ref[end, first : first + 2 * KW] = jnp.where(lanes, dk_two, dq_one[half:] + dq_two)
            acc_ref[top, first + 2 * KW : first + HW] = dv_one
            acc_ref[end, first + 2 * KW : first + HW] = dv_two
        side_ref[:, 2 * KW * which : 2 * KW * (which + 1)] = side[BLOCK:]

    @pl.when(joined)
    def _():
        one, two = slice(0, BLOCK), slice(BLOCK, 2 * BLOCK)
        for which in heads:
            first = HW * which
            pair = slice(first, first + 2 * KW)
            grad_q, grad_k, grad_v = back_block(
                side_ref[:, 2 * KW * which : 2 * KW * (which + 1)],
                qkv_ref[two, pair],
                qkv_ref[one, pair],
                qkv_ref[one, first + 2 * KW : first + HW],
                g_ref[two, VW * which : VW * (which + 1)],
                None,
            )
            lanes = low_lanes((BLOCK, 2 * KW))
            acc_ref[one, pair] += jnp.where(lanes, grad_k, 0.0)
            acc_ref[two, pair] += jnp.where(lanes, 0.0, grad_q)
            acc_ref[one, first + 2 * KW : first + HW] += grad_v

    for which in heads:
        first = HW * which
        pair, rest = slice(first, first + 2 * KW), slice(first + 2 * KW, first + HW)
        grads = turned(acc_ref[:, pair]) * HALF_SCALE
        grad_ref[:, pair] = (grads * slope_ref[:, pair].astype(F32)).astype(BF16)
        grad_ref[:, rest] = (acc_ref[:, rest] * slope_ref[:, rest].astype(F32)).astype(BF16)
    grad_pre = grad_ref[...]
    part = mine_ref.shape[0] // 2
    core = lax.rem(lax.axis_index("dp"), 2)
    for target, side in ((mine_ref, core), (other_ref, 1 - core)):
        for block, features in split_rows(part, side * part):
            total = dot(turned_ref[features, :], grad_pre, 1, 0)
            target[block * part : (block + 1) * part] = total.astype(BF16)


def rows_at(index):
    return pl.ds(pl.multiple_of(index * BLOCK, BLOCK), BLOCK)


def long_attend_kernel(blocks_smem, all_ref, *refs):
    mixed_refs, acc_ref = refs[:H], refs[H]
    mine, chunk, group = run_place()
    valid = blocks_smem[group]
    acc_ref[...] = jnp.zeros_like(acc_ref)

    @pl.when(chunk < valid)
    def _():
        side = score_side(all_ref[rows_at(chunk), : 2 * KW])

        @pl.loop(0, chunk)
        def _(index):
            scores = dot(side, all_ref[rows_at(index), : 2 * KW], 1, 1)
            acc_ref[...] += dot(
                silu_half(scores).astype(BF16), all_ref[rows_at(index), 2 * KW :], 1, 0
            )

        weights = silu_half(dot(side, all_ref[rows_at(chunk), : 2 * KW], 1, 1))
        weights = jnp.where(causal(False, BLOCK, BLOCK), weights, 0.0).astype(BF16)
        acc_ref[...] += dot(weights, all_ref[rows_at(chunk), 2 * KW :], 1, 0)

    coeff = 1.0 / (valid * BLOCK).astype(F32)
    rows = mixed_refs[0].shape[0]
    for bits in range(H):
        start = pl.multiple_of((mine ^ bits) * rows, rows)
        mixed_refs[bits][...] = (acc_ref[pl.ds(start, rows), :] * coeff).astype(BF16)


def long_back_kernel(blocks_smem, all_ref, g_ref, *refs):
    grad_refs, (dq_ref, dk_ref, dv_ref) = refs[:H], refs[H:]
    mine, chunk, group = run_place()
    valid = blocks_smem[group]
    dq_ref[...] = jnp.zeros_like(dq_ref)
    dk_ref[...] = jnp.zeros_like(dk_ref)
    dv_ref[...] = jnp.zeros_like(dv_ref)

    @pl.when(chunk < valid)
    def _():
        own = rows_at(chunk)
        qk = all_ref[own, : 2 * KW]
        side = score_side(qk)
        values = all_ref[own, 2 * KW :]
        g_own = g_ref[own, :]
        grad_q, grad_k, grad_v = back_block(
            side, qk, qk, values, g_own, causal(True, BLOCK, BLOCK)
        )
        dq_ref[...] = grad_q
        dk_ref[...] = grad_k
        dv_ref[...] = grad_v

        @pl.loop(0, chunk)
        def _(index):
            keys = all_ref[rows_at(index), : 2 * KW]
            act, slope = silu_both(dot(side, keys, 1, 1))
            slopes = dot(g_own, all_ref[rows_at(index), 2 * KW :], 1, 1) * slope
            dq_ref[...] += dot(slopes.astype(BF16), keys, 1, 0)

        @pl.loop(chunk + 1, valid)
        def _(index):
            g_rows = g_ref[rows_at(index), :]
            queries = all_ref[rows_at(index), : 2 * KW]
            act, slope = silu_both(dot(qk, score_side(queries), 1, 1))
            slopes = (dot(values, g_rows, 1, 1) * slope).astype(BF16)
            dk_ref[...] += dot(slopes, queries, 1, 0)
            dv_ref[...] += dot(act.astype(BF16), g_rows, 1, 0)

    coeff = 1.0 / (valid * BLOCK).astype(F32)
    rows = grad_refs[0].shape[0]
    lanes = low_lanes((rows, 2 * KW))
    for bits in range(H):
        part = pl.ds(pl.multiple_of((mine ^ bits) * rows, rows), rows)
        pair = turned(jnp.where(lanes, dk_ref[part, :], dq_ref[part, :])) * HALF_SCALE
        grad_refs[bits][:, : 2 * KW] = (pair * coeff).astype(BF16)
        grad_refs[bits][:, 2 * KW :] = (dv_ref[part, :] * coeff).astype(BF16)


def long_head_kernel(
    got_0,
    got_1,
    got_2,
    got_3,
    x_ref,
    cot_ref,
    pout_ref,
    gate_ref,
    slope_ref,
    out_ref,
    send_ref,
    mid_ref,
    mixed_ref,
):
    mine, _, _ = run_place()
    for bits, got in enumerate((got_0, got_1, got_2, got_3)):
        start = pl.multiple_of((mine ^ bits) * VW, VW)
        mixed_ref[:, pl.ds(start, VW)] = got[...].astype(F32)
    out, gated, grad_gate, grad_mixed = head_out(
        x_ref[...],
        cot_ref[...],
        pout_ref[...],
        gate_ref[...],
        slope_ref[...].astype(F32),
        mixed_ref[...],
    )
    out_ref[...] = out
    cols = gated.shape[1]
    mid_ref[:, :cols] = gated
    mid_ref[:, cols:] = grad_gate
    grad_mixed = grad_mixed.astype(BF16)
    for copy in range(send_ref.shape[0]):
        for which in range(H):
            send_ref[copy, which] = grad_mixed[:, VW * which : VW * (which + 1)]


def early_sums_kernel(
    xbf_ref, cot_ref, mid_ref, half_ref, mid_got, mine_ref, got_ref, sum_ref
):
    cols = mid_ref.shape[1] // 2
    part = sum_ref.shape[0] // 2
    core = lax.rem(lax.axis_index("dp"), 2)
    mid = jnp.concatenate([mid_ref[...], mid_got[...]], axis=0)
    for block, features in split_rows(part, core * part):
        here = slice(block * part, (block + 1) * part)
        for place, own in ((0, cot_ref), (1, xbf_ref)):
            start = (2 * place + block) * part
            rows = jnp.concatenate([own[:, features], half_ref[:, start : start + part]], axis=0)
            there = slice(place * cols, (place + 1) * cols)
            total = mine_ref[here, there].astype(F32) + got_ref[here, there].astype(F32)
            sum_ref[here, there] = (total + dot(rows, mid[:, there], 0, 0)).astype(BF16)


def long_slopes_kernel(got_0, got_1, got_2, got_3, slope_ref, grad_ref):
    mine, _, _ = run_place()
    for bits, got in enumerate((got_0, got_1, got_2, got_3)):
        there = pl.ds(pl.multiple_of((mine ^ bits) * HW, HW), HW)
        grads = got[...].astype(F32) * slope_ref[:, there].astype(F32)
        grad_ref[:, there] = grads.astype(BF16)


def late_sums_kernel(mine_ref, got_ref, xbf_ref, half_ref, grad_ref, grad_got, sum_ref):
    part = sum_ref.shape[0]
    core = lax.rem(lax.axis_index("dp"), 2)
    start = (core + 2 * pl.program_id(0)) * part
    features = pl.ds(pl.multiple_of(start, part), part)
    rows = jnp.concatenate([xbf_ref[:, features], half_ref[...]], axis=0)
    grads = jnp.concatenate([grad_ref[...], grad_got[...]], axis=0)
    total = mine_ref[...].astype(F32) + got_ref[...].astype(F32)
    sum_ref[...] = (total + dot(rows, grads, 0, 0)).astype(BF16)


def final_sums_kernel(factor, early_ref, late_ref, in_ref, out_ref):
    gates = out_ref.shape[1]
    out_ref[...] = early_ref[:, :gates] * factor
    in_ref[:, :gates] = early_ref[:, gates:] * factor
    late = late_ref[0].astype(F32)
    for step in range(1, late_ref.shape[0]):
        late += late_ref[step].astype(F32)
    late = late * factor
    low = low_lanes((late.shape[0], 2 * KW))
    for pair in range(H // 2):
        first = 2 * HW * pair
        even, odd = late[:, first : first + 2 * KW], late[:, first + HW : first + HW + 2 * KW]
        first_q = gates + 2 * KW * pair
        first_k = first_q + H * KW
        first_v = gates + 2 * H * KW + 2 * VW * pair
        in_ref[:, first_q : first_q + 2 * KW] = jnp.where(low, even, turned(odd))
        in_ref[:, first_k : first_k + 2 * KW] = jnp.where(low, turned(even), odd)
        in_ref[:, first_v : first_v + VW] = late[:, first + 2 * KW : first + HW]
        in_ref[:, first_v + VW : first_v + 2 * VW] = late[:, first + HW + 2 * KW : first + 2 * HW]


def input_back_kernel(
    grad_gate_ref,
    grad_ref,
    cot_ref,
    xbf_ref,
    inv_ref,
    pin_ref,
    proj_ref,
    long_gate_ref,
    long_grad_ref,
    long_cot_ref,
    long_xbf_ref,
    long_inv_ref,
    back_ref,
    long_back_ref,
):
    step = pl.program_id(0)

    def finish(gate, grad, cot, normed, inv, target):
        grad_norm = dot(gate[...], pin_ref[...], 1, 1) + dot(grad[...], proj_ref[...], 1, 1)
        back = norm_back(grad_norm, normed.astype(F32), inv[...])
        target[...] = (cot[...].astype(F32) + back).astype(BF16)

    @pl.when(step < 2)
    def _():
        finish(grad_gate_ref, grad_ref, cot_ref, xbf_ref[...], inv_ref, back_ref)

    @pl.when(step == 2)
    def _():
        finish(
            long_gate_ref,
            long_grad_ref,
            long_cot_ref,
            long_xbf_ref[...],
            long_inv_ref,
            long_back_ref,
        )


def shaped(shape, dtype=BF16):
    return jax.ShapeDtypeStruct(shape, dtype)


def in_hbm(shape, dtype=BF16):
    return pltpu.HBM(shape, dtype)


def call(kernel, out_shape, flops, moved, name, vmem=24, **kwargs):
    return pl.pallas_call(
        kernel,
        out_shape=out_shape,
        cost_estimate=pl.CostEstimate(flops=flops, bytes_accessed=moved, transcendentals=0),
        compiler_params=pltpu.CompilerParams(vmem_limit_bytes=vmem * MIB),
        name=name,
        **kwargs,
    )


SMEM = pl.BlockSpec(memory_space=pltpu.SMEM)
WHOLE = pl.BlockSpec(memory_space=pltpu.VMEM)


def rows_spec(rows, cols):
    return pl.BlockSpec((rows, cols), lambda step: (step, 0))


def cols_spec(rows, cols):
    return pl.BlockSpec((rows, cols), lambda step: (0, step))


def fixed_spec(rows, cols):
    return pl.BlockSpec((rows, cols), lambda step: (0, 0))


def swap_heads(pieces):
    size = lax.axis_size("sp")
    return [pieces[0]] + [
        lax.ppermute(pieces[bits], "sp", [(src, src ^ bits) for src in range(size)])
        for bits in range(1, H)
    ]


def spread_heads(sent):
    chunks, heads, rows, cols = sent.shape
    got = lax.all_to_all(sent.reshape(chunks * heads, rows, cols), "sp", 0, 0, tiled=True)
    return got.reshape(chunks * heads * rows, cols)


def swap_cores(half):
    size = lax.axis_size("dp")
    return lax.ppermute(half, "dp", [(src, src ^ 1) for src in range(size)])


def scatter_pairs(partial):
    runs, size = lax.axis_size("dp"), lax.axis_size("sp")
    groups = [
        [run * size + place for run in range(core, runs, 2) for place in range(size)]
        for core in range(2)
    ]
    count = len(groups[0])
    sent = partial.reshape(count, partial.shape[0] // count, partial.shape[1])
    return lax.all_to_all(sent, ("dp", "sp"), 0, 0, tiled=True, axis_index_groups=groups)


def body(x_long, x_short, long_blocks, short_user, proj_in, proj_out, cot_long, cot_short):
    sp_size = lax.axis_size("sp")
    long_rows, width = x_long.shape
    short_rows = x_short.shape[0]
    gates = proj_out.shape[0]
    cols = proj_in.shape[1]
    rest = cols - gates
    half = width // 2
    chunks = sp_size // H

    proj, sent, inv_long, xbf_long, slope_rest = call(
        long_project_kernel,
        (
            in_hbm((width, rest)),
            in_hbm((chunks, H, long_rows, HW)),
            in_hbm((long_rows, 1), F32),
            in_hbm((long_rows, width)),
            in_hbm((long_rows, rest)),
        ),
        2 * long_rows * width * rest,
        8 * 2**20,
        "long_project",
        vmem=60,
        grid=(2,),
        in_specs=[
            fixed_spec(long_rows, width),
            pl.BlockSpec((width, 2 * KW), lambda step: (0, step + gates // (2 * KW))),
            pl.BlockSpec((width, 2 * KW), lambda step: (0, step + (gates + H * KW) // (2 * KW))),
            pl.BlockSpec((width, 2 * VW), lambda step: (0, step + (gates + 2 * H * KW) // (2 * VW))),
        ],
        out_specs=[
            cols_spec(width, rest // 2),
            pl.BlockSpec((chunks, 2, long_rows, HW), lambda step: (0, step, 0, 0)),
            fixed_spec(long_rows, 1),
            fixed_spec(long_rows, width),
            cols_spec(long_rows, rest // 2),
        ],
    )(x_long, proj_in, proj_in, proj_in)
    whole = spread_heads(sent)
    short_out = call(
        short_forward_kernel,
        (
            in_hbm((short_rows, width)),
            in_hbm((short_rows, rest)),
            in_hbm((short_rows, gates)),
            in_hbm((short_rows, gates)),
            in_hbm((short_rows, rest)),
            in_hbm((short_rows, width)),
            in_hbm((width, short_rows)),
            in_hbm((short_rows, 1), F32),
            in_hbm((half, 2 * gates)),
            in_hbm((half, 2 * gates)),
            in_hbm((long_rows, gates)),
            in_hbm((long_rows, gates)),
            in_hbm((long_rows, width)),
        ),
        20 * 10**9,
        24 * 2**20,
        "short_forward",
        vmem=56,
        grid=(short_rows // BLOCK,),
        in_specs=[
            SMEM,
            rows_spec(BLOCK, width),
            rows_spec(BLOCK, width),
            fixed_spec(width, gates),
            fixed_spec(width, rest),
            fixed_spec(gates, width),
            fixed_spec(long_rows, width),
            fixed_spec(long_rows, width),
        ],
        out_specs=[
            rows_spec(BLOCK, width),
            rows_spec(BLOCK, rest),
            rows_spec(BLOCK, gates),
            rows_spec(BLOCK, gates),
            rows_spec(BLOCK, rest),
            rows_spec(BLOCK, width),
            cols_spec(width, BLOCK),
            rows_spec(BLOCK, 1),
            fixed_spec(half, 2 * gates),
            fixed_spec(half, 2 * gates),
            fixed_spec(long_rows, gates),
            fixed_spec(long_rows, gates),
            fixed_spec(long_rows, width),
        ],
        scratch_shapes=[
            pltpu.VMEM((width, 2 * gates), F32),
            pltpu.VMEM((BLOCK, rest), BF16),
            pltpu.VMEM((BLOCK, gates), F32),
            pltpu.VMEM((BLOCK, 2 * KW * H), BF16),
        ],
    )(short_user, x_short, cot_short, proj_in, proj, proj_out, xbf_long, cot_long)
    out_short, qkv_short, g_short, gate_short, slope_short, xbf_short = short_out[:6]
    turned_short, inv_short, early_mine, early_other = short_out[6:10]
    gate_long, slope_long, half_other = short_out[10:]
    early_got = swap_cores(early_other)


    whole, early_got, out_short = lax.optimization_barrier((whole, early_got, out_short))
    mixed = call(
        long_attend_kernel,
        (shaped((long_rows, VW)),) * H,
        2 * 10**9,
        2 * 2**20,
        "long_attend",
        in_specs=[SMEM, WHOLE],
        scratch_shapes=[pltpu.VMEM((BLOCK, VW), F32)],
    )(long_blocks, whole)
    out_long, sent, mid = call(
        long_head_kernel,
        (
            shaped((long_rows, width)),
            in_hbm((chunks, H, long_rows, VW)),
            in_hbm((long_rows, 2 * gates)),
        ),
        4 * long_rows * width * gates,
        3 * 2**20,
        "long_head",
        in_specs=[WHOLE] * 9,
        scratch_shapes=[pltpu.VMEM((long_rows, gates), F32)],
    )(*swap_heads(mixed), x_long, cot_long, proj_out, gate_long, slope_long)
    sent, qkv_short, mid, half_other = lax.optimization_barrier((sent, qkv_short, mid, half_other))
    all_g = spread_heads(sent)
    half_got = swap_cores(half_other)
    mid_got = swap_cores(mid)
    grad_short, short_mine, short_other = call(
        short_back_kernel,
        (in_hbm((short_rows, rest)), in_hbm((half, rest)), in_hbm((half, rest))),
        16 * 10**9,
        13 * 2**20,
        "short_back",
        vmem=56,
        grid=(2,),
        in_specs=[
            SMEM,
            cols_spec(short_rows, rest // 2),
            cols_spec(short_rows, gates // 2),
            cols_spec(short_rows, rest // 2),
            fixed_spec(width, short_rows),
        ],
        out_specs=[
            cols_spec(short_rows, rest // 2),
            cols_spec(half, rest // 2),
            cols_spec(half, rest // 2),
        ],
        scratch_shapes=[
            pltpu.VMEM((short_rows, rest // 2), F32),
            pltpu.VMEM((BLOCK, rest // 4), BF16),
        ],
    )(short_user, qkv_short, g_short, slope_short, turned_short)
    mid_got, half_got, grad_short = lax.optimization_barrier((mid_got, half_got, grad_short))
    short_got = swap_cores(short_other)
    early = call(
        early_sums_kernel,
        in_hbm((half, 2 * gates)),
        8 * long_rows * half * gates,
        5 * 2**20,
        "early_sums",
    )(xbf_long, cot_long, mid, half_got, mid_got, early_mine, early_got)
    all_g, early = lax.optimization_barrier((all_g, early))
    early = scatter_pairs(early)

    grads = call(
        long_back_kernel,
        (shaped((long_rows, HW)),) * H,
        6 * 10**9,
        4 * 2**20,
        "long_back",
        in_specs=[SMEM, WHOLE, WHOLE],
        scratch_shapes=[
            pltpu.VMEM((BLOCK, 2 * KW), F32),
            pltpu.VMEM((BLOCK, 2 * KW), F32),
            pltpu.VMEM((BLOCK, VW), F32),
        ],
    )(long_blocks, whole, all_g)
    grad_long = call(
        long_slopes_kernel,
        shaped((long_rows, rest)),
        long_rows * rest,
        2**20,
        "long_slopes",
    )(*swap_heads(grads), slope_rest)
    late = call(
        late_sums_kernel,
        in_hbm((half, rest)),
        4 * long_rows * half * rest,
        5 * 2**20,
        "late_sums",
        grid=(2,),
        in_specs=[
            rows_spec(half // 2, rest),
            rows_spec(half // 2, rest),
            fixed_spec(long_rows, width),
            pl.BlockSpec((long_rows, half // 2), lambda step: (0, step + 2)),
            fixed_spec(long_rows, rest),
            fixed_spec(long_rows, rest),
        ],
        out_specs=rows_spec(half // 2, rest),
    )(short_mine, short_got, xbf_long, half_got, grad_long, swap_cores(grad_long))
    late, gate_short = lax.optimization_barrier((late, gate_short))
    late = scatter_pairs(late)

    def short_rows_spec(cols):
        return pl.BlockSpec((BLOCK, cols), lambda step: (jnp.minimum(step, 1), 0))

    back_short, back_long = call(
        input_back_kernel,
        (in_hbm((short_rows, width)), in_hbm((long_rows, width))),
        2 * (short_rows + long_rows) * width * cols,
        14 * 2**20,
        "input_back",
        vmem=60,
        grid=(short_rows // BLOCK + 1,),
        in_specs=[
            short_rows_spec(gates),
            short_rows_spec(rest),
            short_rows_spec(width),
            short_rows_spec(width),
            short_rows_spec(1),
            fixed_spec(width, gates),
            fixed_spec(width, rest),
        ]
        + [
            pl.BlockSpec((long_rows, gates), lambda step: (0, 1)),
            fixed_spec(long_rows, rest),
            fixed_spec(long_rows, width),
            fixed_spec(long_rows, width),
            fixed_spec(long_rows, 1),
        ],
        out_specs=[short_rows_spec(width), fixed_spec(long_rows, width)],
    )(
        gate_short,
        grad_short,
        cot_short,
        xbf_short,
        inv_short,
        proj_in,
        proj,
        mid,
        grad_long,
        cot_long,
        xbf_long,
        inv_long,
    )
    total_rows = lax.axis_size("dp") * sp_size * (long_rows + short_rows)
    early = jnp.sum(early.astype(F32), axis=0)
    sum_in, sum_out = call(
        functools.partial(final_sums_kernel, float(total_rows) ** (-0.5)),
        (shaped((early.shape[0], cols), F32), shaped((early.shape[0], gates), F32)),
        128 * 2**10,
        2**20,
        "final_sums",
    )(early, late)
    return (out_long, out_short, back_long, back_short, sum_in, sum_out)


def solution(mesh):
    rows = P(("dp", "sp"), None)
    return jax.shard_map(
        body,
        mesh=mesh,
        in_specs=(rows, rows, P(), rows, P(), P(), rows, rows),
        out_specs=(rows,) * 6,
        check_vma=False,
    )
```

```python
import functools

import jax
import jax.numpy as jnp
from jax import lax
from jax.experimental import pallas as pl
from jax.experimental.pallas import tpu as pltpu
from jax.sharding import PartitionSpec as P

H = 4
BLOCK = 512
KW = 64
VW = 128
HW = 2 * KW + VW
EPS = 1e-05
HALF_SCALE = 0.5 * KW**-0.5
F32 = jnp.float32
BF16 = jnp.bfloat16
MIB = 1024 * 1024


def dot(first, second, first_dim, second_dim):
    return lax.dot_general(
        first, second, (((first_dim,), (second_dim,)), ((), ())), preferred_element_type=F32
    )


def norm_rows(rows):
    center = rows - jnp.mean(rows, axis=-1, keepdims=True)
    inv_root = lax.rsqrt(jnp.mean(center * center, axis=-1, keepdims=True) + EPS)
    return center * inv_root, inv_root


def norm_back(upstream, normed, inv_root):
    return inv_root * (
        upstream
        - jnp.mean(upstream, axis=-1, keepdims=True)
        - normed * jnp.mean(upstream * normed, axis=-1, keepdims=True)
    )


def silu_half(half):
    return half * (1.0 + jnp.tanh(half))


def silu_both(half):
    curve = jnp.tanh(half)
    above = 1.0 + curve
    act = half * above
    return act, above + act * (1.0 - curve)


def low_lanes(shape):
    return lax.broadcasted_iota(jnp.int32, shape, 1) < KW


def turned(pair):
    return pltpu.roll(pair.astype(F32), KW, 1)


def score_side(qk):
    return jnp.where(low_lanes(qk.shape), 0.0, turned(qk) * HALF_SCALE).astype(BF16)


def causal(keys_first, keys, queries, key_start=0, query_start=0):
    shape = (keys, queries) if keys_first else (queries, keys)
    key_pos = key_start + lax.broadcasted_iota(jnp.int32, shape, 0 if keys_first else 1)
    query_pos = query_start + lax.broadcasted_iota(jnp.int32, shape, 1 if keys_first else 0)
    return key_pos <= query_pos


def project(x_bf, proj):
    act, slope = silu_both(0.5 * dot(x_bf, proj, 1, 0))
    return act.astype(BF16), 0.5 * slope


def head_out(x_rows, cot, proj_out, gate_u, slope_gate, mixed):
    mixed_n, inv_mix = norm_rows(mixed)
    gate_f = gate_u.astype(F32)
    gated = (mixed_n * gate_f).astype(BF16)
    out = (x_rows.astype(F32) + dot(gated, proj_out, 1, 0)).astype(BF16)
    grad_g = dot(cot, proj_out, 1, 1)
    grad_mixed = norm_back(grad_g * gate_f, mixed_n, inv_mix)
    grad_gate = (grad_g * mixed_n * slope_gate).astype(BF16)
    return out, gated, grad_gate, grad_mixed


def run_place():
    index = lax.axis_index("sp")
    return lax.rem(index, H), lax.div(index, H), lax.axis_index("dp")


def split_rows(part, start):
    for block in range(2):
        yield block, pl.ds(pl.multiple_of(start + 2 * part * block, part), part)


def long_project_kernel(
    x_ref, pin_q_ref, pin_k_ref, pin_v_ref, proj_ref, send_ref, inv_ref, xbf_ref, slope_ref
):
    @pl.when(pl.program_id(0) == 0)
    def _():
        normed, inv_std = norm_rows(x_ref[...].astype(F32))
        xbf_ref[...] = normed.astype(BF16)
        inv_ref[...] = inv_std

    q_pair, k_pair = pin_q_ref[...], pin_k_ref[...]
    low = low_lanes(q_pair.shape)
    even = jnp.where(low, q_pair.astype(F32), turned(k_pair)).astype(BF16)
    odd = jnp.where(low, turned(q_pair), k_pair.astype(F32)).astype(BF16)
    proj = jnp.concatenate([even, pin_v_ref[:, :VW], odd, pin_v_ref[:, VW:]], axis=1)
    proj_ref[...] = proj
    act, slope = project(xbf_ref[...], proj)
    slope_ref[...] = slope.astype(BF16)
    for copy in range(send_ref.shape[0]):
        for which in range(2):
            send_ref[copy, which] = act[:, HW * which : HW * (which + 1)]


def short_forward_kernel(
    user_ref,
    x_ref,
    cot_ref,
    pin_ref,
    proj_ref,
    pout_ref,
    long_xbf_ref,
    long_cot_ref,
    out_ref,
    qkv_ref,
    g_ref,
    grad_gate_ref,
    slope_ref,
    xbf_ref,
    turned_ref,
    inv_ref,
    mine_ref,
    other_ref,
    long_gate_ref,
    long_slope_ref,
    half_ref,
    sum_ref,
    seen_ref,
    mixed_ref,
    side_ref,
):
    step = pl.program_id(0)

    @pl.when(step == 0)
    def _():
        _, _, group = run_place()
        part = long_xbf_ref.shape[1] // 4
        act, slope = project(long_xbf_ref[...], pin_ref[...])
        long_gate_ref[...] = act
        long_slope_ref[...] = slope.astype(BF16)
        for block, features in split_rows(part, (1 - lax.rem(group, 2)) * part):
            half_ref[:, block * part : (block + 1) * part] = long_cot_ref[:, features]
            half_ref[:, (block + 2) * part : (block + 3) * part] = long_xbf_ref[:, features]

    joined = user_ref[0, 0] == user_ref[0, 1]
    share = jnp.where(joined, 0.5 / BLOCK, 1.0 / BLOCK)
    normed, inv_std = norm_rows(x_ref[...].astype(F32))
    x_bf = normed.astype(BF16)
    xbf_ref[...] = x_bf
    turned_ref[...] = x_bf.T
    inv_ref[...] = inv_std
    act, slope = project(x_bf, proj_ref[...])
    slope_ref[...] = slope.astype(BF16)
    qkv_ref[...] = act
    gate_u, slope_gate = project(x_bf, pin_ref[...])
    half = BLOCK // 2
    for which in range(H):
        qk = act[:, HW * which : HW * which + 2 * KW]
        values = act[:, HW * which + 2 * KW : HW * (which + 1)]
        side = score_side(qk)
        scores = dot(side, qk[:half], 1, 1)
        weights = jnp.where(causal(False, half, BLOCK), silu_half(scores), 0.0).astype(BF16)
        mixed = dot(weights, values[:half], 1, 0)
        scores = dot(side[half:], qk[half:], 1, 1)
        weights = jnp.where(causal(False, half, half), silu_half(scores), 0.0).astype(BF16)
        lower = mixed[half:] + dot(weights, values[half:], 1, 0)
        mixed_ref[:half, VW * which : VW * (which + 1)] = mixed[:half]
        mixed_ref[half:, VW * which : VW * (which + 1)] = lower

        side_ref[:, 2 * KW * which : 2 * KW * (which + 1)] = side

    @pl.when(jnp.logical_and(step == 1, joined))
    def _():
        for which in range(H):
            first = HW * which
            side = side_ref[:, 2 * KW * which : 2 * KW * (which + 1)]
            scores = dot(side, seen_ref[:, first : first + 2 * KW], 1, 1)
            mixed_ref[:, VW * which : VW * (which + 1)] += dot(
                silu_half(scores).astype(BF16), seen_ref[:, first + 2 * KW : first + HW], 1, 0
            )

    @pl.when(step == 0)
    def _():
        seen_ref[...] = act

    out, gated, grad_gate, grad_mixed = head_out(
        x_ref[...],
        cot_ref[...],
        pout_ref[...],
        gate_u,
        slope_gate,
        mixed_ref[...] * share,
    )
    out_ref[...] = out
    grad_gate_ref[...] = grad_gate
    g_ref[...] = (grad_mixed.astype(BF16).astype(F32) * share).astype(BF16)
    gates = gated.shape[1]

    @pl.when(step == 0)
    def _():
        sum_ref[:, :gates] = dot(cot_ref[...], gated, 0, 0)
        sum_ref[:, gates:] = dot(turned_ref[...], grad_gate_ref[...], 1, 0)

    @pl.when(step == 1)
    def _():
        part = mine_ref.shape[0] // 2
        core = lax.rem(lax.axis_index("dp"), 2)
        for target, side in ((mine_ref, core), (other_ref, 1 - core)):
            for block, features in split_rows(part, side * part):
                here = slice(block * part, (block + 1) * part)
                total = sum_ref[features, :gates] + dot(cot_ref[:, features], gated, 0, 0)
                target[here, :gates] = total.astype(BF16)
                total = dot(turned_ref[features, :], grad_gate_ref[...], 1, 0)
                target[here, gates:] = (sum_ref[features, gates:] + total).astype(BF16)


def back_block(query_side, query_qk, key_qk, values, g_rows, mask):
    act, slope = silu_both(dot(key_qk, query_side, 1, 1))
    slopes = dot(values, g_rows, 1, 1) * slope
    if mask is not None:
        act = jnp.where(mask, act, 0.0)
        slopes = jnp.where(mask, slopes, 0.0)
    slopes = slopes.astype(BF16)
    grad_q = dot(slopes, key_qk, 0, 0)
    grad_k = dot(slopes, query_qk, 1, 0)
    grad_v = dot(act.astype(BF16), g_rows, 1, 0)
    return grad_q, grad_k, grad_v


def short_back_kernel(
    user_ref, qkv_ref, g_ref, slope_ref, turned_ref, grad_ref, mine_ref, other_ref, acc_ref, side_ref
):
    joined = user_ref[0, 0] == user_ref[0, 1]
    half = BLOCK // 2
    heads = range(qkv_ref.shape[1] // HW)
    for which in heads:
        first = HW * which
        qk = qkv_ref[:, first : first + 2 * KW]
        side = score_side(qk)
        values = qkv_ref[:, first + 2 * KW : first + HW]
        g_rows = g_ref[:, VW * which : VW * (which + 1)]
        lanes = low_lanes((half, 2 * KW))
        for block in range(qkv_ref.shape[0] // BLOCK):
            top = slice(block * BLOCK, block * BLOCK + half)
            end = slice(block * BLOCK + half, (block + 1) * BLOCK)
            both = slice(block * BLOCK, (block + 1) * BLOCK)
            dq_one, dk_one, dv_one = back_block(
                side[both], qk[both], qk[top], values[top], g_rows[both], causal(True, half, BLOCK)
            )
            dq_two, dk_two, dv_two = back_block(
                side[end], qk[end], qk[end], values[end], g_rows[end], causal(True, half, half)
            )
            acc_ref[top, first : first + 2 * KW] = jnp.where(lanes, dk_one, dq_one[:half])
            acc_ref[end, first : first + 2 * KW] = jnp.where(lanes, dk_two, dq_one[half:] + dq_two)
            acc_ref[top, first + 2 * KW : first + HW] = dv_one
            acc_ref[end, first + 2 * KW : first + HW] = dv_two
        side_ref[:, 2 * KW * which : 2 * KW * (which + 1)] = side[BLOCK:]

    @pl.when(joined)
    def _():
        one, two = slice(0, BLOCK), slice(BLOCK, 2 * BLOCK)
        for which in heads:
            first = HW * which
            pair = slice(first, first + 2 * KW)
            grad_q, grad_k, grad_v = back_block(
                side_ref[:, 2 * KW * which : 2 * KW * (which + 1)],
                qkv_ref[two, pair],
                qkv_ref[one, pair],
                qkv_ref[one, first + 2 * KW : first + HW],
                g_ref[two, VW * which : VW * (which + 1)],
                None,
            )
            lanes = low_lanes((BLOCK, 2 * KW))
            acc_ref[one, pair] += jnp.where(lanes, grad_k, 0.0)
            acc_ref[two, pair] += jnp.where(lanes, 0.0, grad_q)
            acc_ref[one, first + 2 * KW : first + HW] += grad_v

    for which in heads:
        first = HW * which
        pair, rest = slice(first, first + 2 * KW), slice(first + 2 * KW, first + HW)
        grads = turned(acc_ref[:, pair]) * HALF_SCALE
        grad_ref[:, pair] = (grads * slope_ref[:, pair].astype(F32)).astype(BF16)
        grad_ref[:, rest] = (acc_ref[:, rest] * slope_ref[:, rest].astype(F32)).astype(BF16)
    grad_pre = grad_ref[...]
    part = mine_ref.shape[0] // 2
    core = lax.rem(lax.axis_index("dp"), 2)
    for target, side in ((mine_ref, core), (other_ref, 1 - core)):
        for block, features in split_rows(part, side * part):
            total = dot(turned_ref[features, :], grad_pre, 1, 0)
            target[block * part : (block + 1) * part] = total.astype(BF16)


def rows_at(index):
    return pl.ds(pl.multiple_of(index * BLOCK, BLOCK), BLOCK)


def long_attend_kernel(blocks_smem, all_ref, *refs):
    mixed_refs, acc_ref = refs[:H], refs[H]
    mine, chunk, group = run_place()
    valid = blocks_smem[group]
    acc_ref[...] = jnp.zeros_like(acc_ref)

    @pl.when(chunk < valid)
    def _():
        side = score_side(all_ref[rows_at(chunk), : 2 * KW])

        @pl.loop(0, chunk)
        def _(index):
            scores = dot(side, all_ref[rows_at(index), : 2 * KW], 1, 1)
            acc_ref[...] += dot(
                silu_half(scores).astype(BF16), all_ref[rows_at(index), 2 * KW :], 1, 0
            )

        weights = silu_half(dot(side, all_ref[rows_at(chunk), : 2 * KW], 1, 1))
        weights = jnp.where(causal(False, BLOCK, BLOCK), weights, 0.0).astype(BF16)
        acc_ref[...] += dot(weights, all_ref[rows_at(chunk), 2 * KW :], 1, 0)

    coeff = 1.0 / (valid * BLOCK).astype(F32)
    rows = mixed_refs[0].shape[0]
    for bits in range(H):
        start = pl.multiple_of((mine ^ bits) * rows, rows)
        mixed_refs[bits][...] = (acc_ref[pl.ds(start, rows), :] * coeff).astype(BF16)


def long_back_kernel(blocks_smem, all_ref, g_ref, *refs):
    grad_refs, (dq_ref, dk_ref, dv_ref) = refs[:H], refs[H:]
    mine, chunk, group = run_place()
    valid = blocks_smem[group]
    dq_ref[...] = jnp.zeros_like(dq_ref)
    dk_ref[...] = jnp.zeros_like(dk_ref)
    dv_ref[...] = jnp.zeros_like(dv_ref)

    @pl.when(chunk < valid)
    def _():
        own = rows_at(chunk)
        qk = all_ref[own, : 2 * KW]
        side = score_side(qk)
        values = all_ref[own, 2 * KW :]
        g_own = g_ref[own, :]
        grad_q, grad_k, grad_v = back_block(
            side, qk, qk, values, g_own, causal(True, BLOCK, BLOCK)
        )
        dq_ref[...] = grad_q
        dk_ref[...] = grad_k
        dv_ref[...] = grad_v

        @pl.loop(0, chunk)
        def _(index):
            keys = all_ref[rows_at(index), : 2 * KW]
            act, slope = silu_both(dot(side, keys, 1, 1))
            slopes = dot(g_own, all_ref[rows_at(index), 2 * KW :], 1, 1) * slope
            dq_ref[...] += dot(slopes.astype(BF16), keys, 1, 0)

        @pl.loop(chunk + 1, valid)
        def _(index):
            g_rows = g_ref[rows_at(index), :]
            queries = all_ref[rows_at(index), : 2 * KW]
            act, slope = silu_both(dot(qk, score_side(queries), 1, 1))
            slopes = (dot(values, g_rows, 1, 1) * slope).astype(BF16)
            dk_ref[...] += dot(slopes, queries, 1, 0)
            dv_ref[...] += dot(act.astype(BF16), g_rows, 1, 0)

    coeff = 1.0 / (valid * BLOCK).astype(F32)
    rows = grad_refs[0].shape[0]
    lanes = low_lanes((rows, 2 * KW))
    for bits in range(H):
        part = pl.ds(pl.multiple_of((mine ^ bits) * rows, rows), rows)
        pair = turned(jnp.where(lanes, dk_ref[part, :], dq_ref[part, :])) * HALF_SCALE
        grad_refs[bits][:, : 2 * KW] = (pair * coeff).astype(BF16)
        grad_refs[bits][:, 2 * KW :] = (dv_ref[part, :] * coeff).astype(BF16)


def long_head_kernel(
    got_0,
    got_1,
    got_2,
    got_3,
    x_ref,
    cot_ref,
    pout_ref,
    gate_ref,
    slope_ref,
    out_ref,
    send_ref,
    mid_ref,
    mixed_ref,
):
    mine, _, _ = run_place()
    for bits, got in enumerate((got_0, got_1, got_2, got_3)):
        start = pl.multiple_of((mine ^ bits) * VW, VW)
        mixed_ref[:, pl.ds(start, VW)] = got[...].astype(F32)
    out, gated, grad_gate, grad_mixed = head_out(
        x_ref[...],
        cot_ref[...],
        pout_ref[...],
        gate_ref[...],
        slope_ref[...].astype(F32),
        mixed_ref[...],
    )
    out_ref[...] = out
    cols = gated.shape[1]
    mid_ref[:, :cols] = gated
    mid_ref[:, cols:] = grad_gate
    grad_mixed = grad_mixed.astype(BF16)
    for copy in range(send_ref.shape[0]):
        for which in range(H):
            send_ref[copy, which] = grad_mixed[:, VW * which : VW * (which + 1)]


def early_sums_kernel(
    xbf_ref, cot_ref, mid_ref, half_ref, mid_got, mine_ref, got_ref, sum_ref
):
    cols = mid_ref.shape[1] // 2
    part = sum_ref.shape[0] // 2
    core = lax.rem(lax.axis_index("dp"), 2)
    mid = jnp.concatenate([mid_ref[...], mid_got[...]], axis=0)
    for block, features in split_rows(part, core * part):
        here = slice(block * part, (block + 1) * part)
        for place, own in ((0, cot_ref), (1, xbf_ref)):
            start = (2 * place + block) * part
            rows = jnp.concatenate([own[:, features], half_ref[:, start : start + part]], axis=0)
            there = slice(place * cols, (place + 1) * cols)
            total = mine_ref[here, there].astype(F32) + got_ref[here, there].astype(F32)
            sum_ref[here, there] = (total + dot(rows, mid[:, there], 0, 0)).astype(BF16)


def long_slopes_kernel(got_0, got_1, got_2, got_3, slope_ref, grad_ref):
    mine, _, _ = run_place()
    for bits, got in enumerate((got_0, got_1, got_2, got_3)):
        there = pl.ds(pl.multiple_of((mine ^ bits) * HW, HW), HW)
        grads = got[...].astype(F32) * slope_ref[:, there].astype(F32)
        grad_ref[:, there] = grads.astype(BF16)


def late_sums_kernel(mine_ref, got_ref, xbf_ref, half_ref, grad_ref, grad_got, sum_ref):
    part = sum_ref.shape[0]
    core = lax.rem(lax.axis_index("dp"), 2)
    start = (core + 2 * pl.program_id(0)) * part
    features = pl.ds(pl.multiple_of(start, part), part)
    rows = jnp.concatenate([xbf_ref[:, features], half_ref[...]], axis=0)
    grads = jnp.concatenate([grad_ref[...], grad_got[...]], axis=0)
    total = mine_ref[...].astype(F32) + got_ref[...].astype(F32)
    sum_ref[...] = (total + dot(rows, grads, 0, 0)).astype(BF16)


def final_sums_kernel(factor, early_ref, late_ref, in_ref, out_ref):
    gates = out_ref.shape[1]
    out_ref[...] = early_ref[:, :gates] * factor
    in_ref[:, :gates] = early_ref[:, gates:] * factor
    late = late_ref[0].astype(F32)
    for step in range(1, late_ref.shape[0]):
        late += late_ref[step].astype(F32)
    late = late * factor
    low = low_lanes((late.shape[0], 2 * KW))
    for pair in range(H // 2):
        first = 2 * HW * pair
        even, odd = late[:, first : first + 2 * KW], late[:, first + HW : first + HW + 2 * KW]
        first_q = gates + 2 * KW * pair
        first_k = first_q + H * KW
        first_v = gates + 2 * H * KW + 2 * VW * pair
        in_ref[:, first_q : first_q + 2 * KW] = jnp.where(low, even, turned(odd))
        in_ref[:, first_k : first_k + 2 * KW] = jnp.where(low, turned(even), odd)
        in_ref[:, first_v : first_v + VW] = late[:, first + 2 * KW : first + HW]
        in_ref[:, first_v + VW : first_v + 2 * VW] = late[:, first + HW + 2 * KW : first + 2 * HW]


def input_back_kernel(
    grad_gate_ref,
    grad_ref,
    cot_ref,
    xbf_ref,
    inv_ref,
    pin_ref,
    proj_ref,
    long_gate_ref,
    long_grad_ref,
    long_cot_ref,
    long_xbf_ref,
    long_inv_ref,
    back_ref,
    long_back_ref,
):
    step = pl.program_id(0)

    def finish(gate, grad, cot, normed, inv, target):
        grad_norm = dot(gate[...], pin_ref[...], 1, 1) + dot(grad[...], proj_ref[...], 1, 1)
        back = norm_back(grad_norm, normed.astype(F32), inv[...])
        target[...] = (cot[...].astype(F32) + back).astype(BF16)

    @pl.when(step < 2)
    def _():
        finish(grad_gate_ref, grad_ref, cot_ref, xbf_ref[...], inv_ref, back_ref)

    @pl.when(step == 2)
    def _():
        finish(
            long_gate_ref,
            long_grad_ref,
            long_cot_ref,
            long_xbf_ref[...],
            long_inv_ref,
            long_back_ref,
        )


def shaped(shape, dtype=BF16):
    return jax.ShapeDtypeStruct(shape, dtype)


def in_hbm(shape, dtype=BF16):
    return pltpu.HBM(shape, dtype)


def call(kernel, out_shape, flops, moved, name, vmem=24, **kwargs):
    return pl.pallas_call(
        kernel,
        out_shape=out_shape,
        cost_estimate=pl.CostEstimate(flops=flops, bytes_accessed=moved, transcendentals=0),
        compiler_params=pltpu.CompilerParams(vmem_limit_bytes=vmem * MIB),
        name=name,
        **kwargs,
    )


SMEM = pl.BlockSpec(memory_space=pltpu.SMEM)
WHOLE = pl.BlockSpec(memory_space=pltpu.VMEM)


def rows_spec(rows, cols):
    return pl.BlockSpec((rows, cols), lambda step: (step, 0))


def cols_spec(rows, cols):
    return pl.BlockSpec((rows, cols), lambda step: (0, step))


def fixed_spec(rows, cols):
    return pl.BlockSpec((rows, cols), lambda step: (0, 0))


def swap_heads(pieces):
    size = lax.axis_size("sp")
    return [pieces[0]] + [
        lax.ppermute(pieces[bits], "sp", [(src, src ^ bits) for src in range(size)])
        for bits in range(1, H)
    ]


def spread_heads(sent):
    chunks, heads, rows, cols = sent.shape
    got = lax.all_to_all(sent.reshape(chunks * heads, rows, cols), "sp", 0, 0, tiled=True)
    return got.reshape(chunks * heads * rows, cols)


def swap_cores(half):
    size = lax.axis_size("dp")
    return lax.ppermute(half, "dp", [(src, src ^ 1) for src in range(size)])


def scatter_pairs(partial):
    runs, size = lax.axis_size("dp"), lax.axis_size("sp")
    groups = [
        [run * size + place for run in range(core, runs, 2) for place in range(size)]
        for core in range(2)
    ]
    count = len(groups[0])
    sent = partial.reshape(count, partial.shape[0] // count, partial.shape[1])
    return lax.all_to_all(sent, ("dp", "sp"), 0, 0, tiled=True, axis_index_groups=groups)


def body(x_long, x_short, long_blocks, short_user, proj_in, proj_out, cot_long, cot_short):
    sp_size = lax.axis_size("sp")
    long_rows, width = x_long.shape
    short_rows = x_short.shape[0]
    gates = proj_out.shape[0]
    cols = proj_in.shape[1]
    rest = cols - gates
    half = width // 2
    chunks = sp_size // H

    proj, sent, inv_long, xbf_long, slope_rest = call(
        long_project_kernel,
        (
            in_hbm((width, rest)),
            in_hbm((chunks, H, long_rows, HW)),
            in_hbm((long_rows, 1), F32),
            in_hbm((long_rows, width)),
            in_hbm((long_rows, rest)),
        ),
        2 * long_rows * width * rest,
        8 * 2**20,
        "long_project",
        vmem=60,
        grid=(2,),
        in_specs=[
            fixed_spec(long_rows, width),
            pl.BlockSpec((width, 2 * KW), lambda step: (0, step + gates // (2 * KW))),
            pl.BlockSpec((width, 2 * KW), lambda step: (0, step + (gates + H * KW) // (2 * KW))),
            pl.BlockSpec((width, 2 * VW), lambda step: (0, step + (gates + 2 * H * KW) // (2 * VW))),
        ],
        out_specs=[
            cols_spec(width, rest // 2),
            pl.BlockSpec((chunks, 2, long_rows, HW), lambda step: (0, step, 0, 0)),
            fixed_spec(long_rows, 1),
            fixed_spec(long_rows, width),
            cols_spec(long_rows, rest // 2),
        ],
    )(x_long, proj_in, proj_in, proj_in)
    whole = spread_heads(sent)
    short_out = call(
        short_forward_kernel,
        (
            in_hbm((short_rows, width)),
            in_hbm((short_rows, rest)),
            in_hbm((short_rows, gates)),
            in_hbm((short_rows, gates)),
            in_hbm((short_rows, rest)),
            in_hbm((short_rows, width)),
            in_hbm((width, short_rows)),
            in_hbm((short_rows, 1), F32),
            in_hbm((half, 2 * gates)),
            in_hbm((half, 2 * gates)),
            in_hbm((long_rows, gates)),
            in_hbm((long_rows, gates)),
            in_hbm((long_rows, width)),
        ),
        20 * 10**9,
        24 * 2**20,
        "short_forward",
        vmem=56,
        grid=(short_rows // BLOCK,),
        in_specs=[
            SMEM,
            rows_spec(BLOCK, width),
            rows_spec(BLOCK, width),
            fixed_spec(width, gates),
            fixed_spec(width, rest),
            fixed_spec(gates, width),
            fixed_spec(long_rows, width),
            fixed_spec(long_rows, width),
        ],
        out_specs=[
            rows_spec(BLOCK, width),
            rows_spec(BLOCK, rest),
            rows_spec(BLOCK, gates),
            rows_spec(BLOCK, gates),
            rows_spec(BLOCK, rest),
            rows_spec(BLOCK, width),
            cols_spec(width, BLOCK),
            rows_spec(BLOCK, 1),
            fixed_spec(half, 2 * gates),
            fixed_spec(half, 2 * gates),
            fixed_spec(long_rows, gates),
            fixed_spec(long_rows, gates),
            fixed_spec(long_rows, width),
        ],
        scratch_shapes=[
            pltpu.VMEM((width, 2 * gates), F32),
            pltpu.VMEM((BLOCK, rest), BF16),
            pltpu.VMEM((BLOCK, gates), F32),
            pltpu.VMEM((BLOCK, 2 * KW * H), BF16),
        ],
    )(short_user, x_short, cot_short, proj_in, proj, proj_out, xbf_long, cot_long)
    out_short, qkv_short, g_short, gate_short, slope_short, xbf_short = short_out[:6]
    turned_short, inv_short, early_mine, early_other = short_out[6:10]
    gate_long, slope_long, half_other = short_out[10:]
    early_got = swap_cores(early_other)


    whole, early_got, out_short = lax.optimization_barrier((whole, early_got, out_short))
    mixed = call(
        long_attend_kernel,
        (shaped((long_rows, VW)),) * H,
        2 * 10**9,
        2 * 2**20,
        "long_attend",
        in_specs=[SMEM, WHOLE],
        scratch_shapes=[pltpu.VMEM((BLOCK, VW), F32)],
    )(long_blocks, whole)
    out_long, sent, mid = call(
        long_head_kernel,
        (
            shaped((long_rows, width)),
            in_hbm((chunks, H, long_rows, VW)),
            in_hbm((long_rows, 2 * gates)),
        ),
        4 * long_rows * width * gates,
        3 * 2**20,
        "long_head",
        in_specs=[WHOLE] * 9,
        scratch_shapes=[pltpu.VMEM((long_rows, gates), F32)],
    )(*swap_heads(mixed), x_long, cot_long, proj_out, gate_long, slope_long)
    sent, qkv_short, mid, half_other = lax.optimization_barrier((sent, qkv_short, mid, half_other))
    all_g = spread_heads(sent)
    half_got = swap_cores(half_other)
    mid_got = swap_cores(mid)
    grad_short, short_mine, short_other = call(
        short_back_kernel,
        (in_hbm((short_rows, rest)), in_hbm((half, rest)), in_hbm((half, rest))),
        16 * 10**9,
        13 * 2**20,
        "short_back",
        vmem=56,
        grid=(2,),
        in_specs=[
            SMEM,
            cols_spec(short_rows, rest // 2),
            cols_spec(short_rows, gates // 2),
            cols_spec(short_rows, rest // 2),
            fixed_spec(width, short_rows),
        ],
        out_specs=[
            cols_spec(short_rows, rest // 2),
            cols_spec(half, rest // 2),
            cols_spec(half, rest // 2),
        ],
        scratch_shapes=[
            pltpu.VMEM((short_rows, rest // 2), F32),
            pltpu.VMEM((BLOCK, rest // 4), BF16),
        ],
    )(short_user, qkv_short, g_short, slope_short, turned_short)
    mid_got, half_got, grad_short = lax.optimization_barrier((mid_got, half_got, grad_short))
    short_got = swap_cores(short_other)
    early = call(
        early_sums_kernel,
        in_hbm((half, 2 * gates)),
        8 * long_rows * half * gates,
        5 * 2**20,
        "early_sums",
    )(xbf_long, cot_long, mid, half_got, mid_got, early_mine, early_got)
    all_g, early = lax.optimization_barrier((all_g, early))
    early = scatter_pairs(early)

    grads = call(
        long_back_kernel,
        (shaped((long_rows, HW)),) * H,
        6 * 10**9,
        4 * 2**20,
        "long_back",
        vmem=62,
        in_specs=[SMEM, WHOLE, WHOLE],
        scratch_shapes=[
            pltpu.VMEM((BLOCK, 2 * KW), F32),
            pltpu.VMEM((BLOCK, 2 * KW), F32),
            pltpu.VMEM((BLOCK, VW), F32),
        ],
    )(long_blocks, whole, all_g)
    grad_long = call(
        long_slopes_kernel,
        shaped((long_rows, rest)),
        long_rows * rest,
        2**20,
        "long_slopes",
    )(*swap_heads(grads), slope_rest)
    late = call(
        late_sums_kernel,
        in_hbm((half, rest)),
        4 * long_rows * half * rest,
        5 * 2**20,
        "late_sums",
        grid=(2,),
        in_specs=[
            rows_spec(half // 2, rest),
            rows_spec(half // 2, rest),
            fixed_spec(long_rows, width),
            pl.BlockSpec((long_rows, half // 2), lambda step: (0, step + 2)),
            fixed_spec(long_rows, rest),
            fixed_spec(long_rows, rest),
        ],
        out_specs=rows_spec(half // 2, rest),
    )(short_mine, short_got, xbf_long, half_got, grad_long, swap_cores(grad_long))
    late, gate_short = lax.optimization_barrier((late, gate_short))
    late = scatter_pairs(late)

    def short_rows_spec(cols):
        return pl.BlockSpec((BLOCK, cols), lambda step: (jnp.minimum(step, 1), 0))

    back_short, back_long = call(
        input_back_kernel,
        (in_hbm((short_rows, width)), in_hbm((long_rows, width))),
        2 * (short_rows + long_rows) * width * cols,
        14 * 2**20,
        "input_back",
        vmem=59,
        grid=(short_rows // BLOCK + 1,),
        in_specs=[
            short_rows_spec(gates),
            short_rows_spec(rest),
            short_rows_spec(width),
            short_rows_spec(width),
            short_rows_spec(1),
            fixed_spec(width, gates),
            fixed_spec(width, rest),
        ]
        + [
            pl.BlockSpec((long_rows, gates), lambda step: (0, 1)),
            fixed_spec(long_rows, rest),
            fixed_spec(long_rows, width),
            fixed_spec(long_rows, width),
            fixed_spec(long_rows, 1),
        ],
        out_specs=[short_rows_spec(width), fixed_spec(long_rows, width)],
    )(
        gate_short,
        grad_short,
        cot_short,
        xbf_short,
        inv_short,
        proj_in,
        proj,
        mid,
        grad_long,
        cot_long,
        xbf_long,
        inv_long,
    )
    total_rows = lax.axis_size("dp") * sp_size * (long_rows + short_rows)
    early = jnp.sum(early.astype(F32), axis=0)
    sum_in, sum_out = call(
        functools.partial(final_sums_kernel, float(total_rows) ** (-0.5)),
        (shaped((early.shape[0], cols), F32), shaped((early.shape[0], gates), F32)),
        128 * 2**10,
        2**20,
        "final_sums",
    )(early, late)
    return (out_long, out_short, back_long, back_short, sum_in, sum_out)


def solution(mesh):
    rows = P(("dp", "sp"), None)
    return jax.shard_map(
        body,
        mesh=mesh,
        in_specs=(rows, rows, P(), rows, P(), P(), rows, rows),
        out_specs=(rows,) * 6,
        check_vma=False,
    )
```
